32 devices in a mesh: groups: 2 (over y), lat: 4 (over z), lon: 2 (over x), rep: 2 (over core).
Axes of the slice: x: 2, y: 2, z: 4, core: 2. Of those that a mesh axis runs over, the one named last changes fastest.
Arguments:
- grid_in: bfloat16 [32768, 227], P(('groups', 'lat', 'lon')), parts along dimension 0, may hold values from -6 to 6
- w_embed: bfloat16 [227, 512], P(None, 'rep'), may hold values from -0.375 to 0.375
- interp_tiles: bfloat16 [256, 128, 128], P(('groups', 'lat', 'lon')), parts along dimension 0, may hold values from -0.5 to 0.5
- route_device: int32 [256, 1], P(('groups', 'lat', 'lon')), parts along dimension 0, may hold values from 0 to 7, as said below
- route_slot: int32 [256], P(('groups', 'lat', 'lon')), parts along dimension 0, may hold values from 0 to 3
- mesh_embed: bfloat16 [8192, 512], P(('groups', 'lat', 'lon'), 'rep'), parts along dimension 0, may hold values from -36 to 36
- w_up: bfloat16 [512, 512], P(None, 'rep'), may hold values from -0.25 to 0.25
- w_down: bfloat16 [512, 512], P('rep'), may hold values from -0.25 to 0.25
- w_out: bfloat16 [512, 227], P('rep'), may hold values from -0.25 to 0.25
- cotangent: bfloat16 [32768, 227], P(('groups', 'lat', 'lon')), parts along dimension 0, may hold values from -6 to 6
Outputs:
- grid_out: bfloat16 [32768, 227], P(('groups', 'lat', 'lon', 'rep')), parts along dimension 0
- grad_out: float32 [1024, 227], P(('groups', 'rep')), parts along dimension 0
- grad_up: float32 [1024, 512], P('groups', 'rep'), parts along dimension 0
- grad_down: float32 [1024, 512], P(('groups', 'rep')), parts along dimension 0
- grad_mesh: float32 [8192, 512], P(('groups', 'lat', 'lon'), 'rep'), parts along dimension 0
The draws below stay inside these ranges and needn't reach their ends.
There are 2 independent parts, one for each index of `groups`. The reference program is written for one: setup_inputs(seed, part) draws one part's arguments, and reference() takes and returns one part's arrays. A program takes and returns all parts, laid end to end along the dimension named above; an argument that names none is the same for every part. Nothing has to cross between parts.
Inputs may be any that keep to these rules, and one draw needn't show every extreme that they name: `route_device`: grid blocks of a band and sector name only patches of the same band or an adjacent band, in the same sector or the next sector eastward (cyclically). Among the 16 blocks of one band and sector at most 4 name the same patch, and their own patch is named by exactly 4 of them.
All inputs are finite; a program needn't handle non-finite values.
Results may differ from the reference program's by a relative error of at most 0.0088.
Values may be sent and summed in bfloat16 or wider, within the bound.
No kernel may reach another device: no remote copies, remote signals or barrier semaphores. Data moves between devices by JAX's collectives and lax.ppermute only.
A program may use at most 64 MiB of HBM per device.

```python
import math
import jax
import jax.numpy as jnp
from jax import lax

C = 227
L = 512
F = 512
TILE = 128
MB_DEV = 4
GB = 16
NG = 16384
NG_BLK = 128
NM = 4096
N_LAT = 4
N_LON = 2


def draw_mesh_embed(key, part):
    key = jax.random.fold_in(key, 11)
    key_rows, key_columns, key_values = jax.random.split(key, 3)
    row_scale = jnp.exp(jax.random.uniform(key_rows, (NM, 1), jnp.float32, math.log(0.3), math.log(3.0)))
    column_scale = jnp.exp(jax.random.uniform(key_columns, (1, L), jnp.float32, math.log(0.3), math.log(3.0)))
    draw_base = jnp.clip(jax.random.normal(key_values, (NM, L), jnp.float32), -4.0, 4.0)
    return (draw_base * row_scale * column_scale).astype(jnp.bfloat16)


def draw_route_device(key, part):
    key = jax.random.fold_in(key, 5)
    patch_count = N_LAT * N_LON
    per_patch = GB // 4
    entries = 6 * per_patch
    device_keys = jax.random.split(key, patch_count)

    def one_device(device_key, device):
        key_score, key_order = jax.random.split(device_key)
        band = device // N_LON
        sector = device % N_LON
        candidate = jnp.arange(entries, dtype=jnp.int32) // per_patch
        band_step = candidate // 2 - 1
        sector_step = candidate % 2
        valid = jnp.logical_and(band + band_step >= 0, band + band_step < N_LAT)
        own = jnp.logical_and(band_step == 0, sector_step == 0)
        score = jax.random.permutation(key_score, entries).astype(jnp.int32)
        score = jnp.where(own, score - entries, jnp.where(valid, score, score + entries))
        chosen = jnp.argsort(score)[:GB]
        picked = candidate[chosen]
        picked = picked[jax.random.permutation(key_order, GB)]
        return ((band + picked // 2 - 1) * N_LON + (sector + picked % 2) % N_LON).astype(jnp.int32)
    routed = jax.vmap(one_device)(device_keys, jnp.arange(patch_count, dtype=jnp.int32))
    return routed.reshape(NG_BLK, 1).astype(jnp.int32)


def plant(drawn, stream_key, smallest, largest):
    longest = drawn.shape.index(max(drawn.shape))
    spots = []
    for shift in (0, 1):
        where = [jax.random.randint(jax.random.fold_in(stream_key, axis), (), 0, length) for axis, length in enumerate(drawn.shape)]
        where[longest] = (where[longest] + shift) % drawn.shape[longest]
        spots.append(tuple(where))
    return drawn.at[spots[0]].set(smallest).at[spots[1]].set(largest)


def block_scale(stream_key, extent, shards, smallest, largest):
    factor_of, own = 1.0, jax.random.fold_in(stream_key, 6)
    for axis_at, shards_of in shards:
        draws = jnp.exp(jax.random.uniform(jax.random.fold_in(own, axis_at), (shards_of,), jnp.float32, smallest / len(shards), largest / len(shards)))
        factor_of = factor_of * jnp.repeat(draws, extent[axis_at] // shards_of).reshape([-1 if axis == axis_at else 1 for axis in range(len(extent))])
    return factor_of


def centred(rng, shape, deviation, bound, shards=(), held_as=jnp.bfloat16):
    drawn = jax.random.normal(rng, shape, jnp.float32) * deviation
    if len(shards) > 0:
        drawn = block_scale(rng, shape, shards, -0.22, 0.18) * drawn
    return jnp.clip(drawn, min=-bound, max=bound).astype(held_as)


def setup_inputs(seed: int = 0, part: int = 0) -> dict:
    splits = jax.random.split(jax.random.key(seed), 11)
    own_keys = jax.random.split(jax.random.fold_in(splits[10], part), 11)
    grid_in = centred(own_keys[0], (NG, C), 1.0, 6.0, ((0, 8),))
    w_embed = centred(splits[1], (C, L), C ** -0.5, 0.375, ((1, 2),))
    interp_tiles = centred(own_keys[2], (NG_BLK, TILE, TILE), TILE ** -0.5, 0.5, ((0, 8),))
    route_device = draw_route_device(jax.random.fold_in(jax.random.fold_in(splits[10], part), 71), part)
    route_slot = plant(jax.random.randint(own_keys[4], (NG_BLK,), 0, MB_DEV), jax.random.fold_in(own_keys[4], 1), 0, MB_DEV - 1).astype(jnp.int32)
    mesh_embed = draw_mesh_embed(jax.random.fold_in(jax.random.fold_in(splits[10], part), 71), part)
    w_up = centred(splits[6], (L, F), L ** -0.5, 0.25, ((1, 2),))
    w_down = centred(splits[7], (F, L), F ** -0.5, 0.25, ((0, 2),))
    w_out = centred(splits[8], (L, C), L ** -0.5, 0.25, ((0, 2),))
    cotangent = centred(own_keys[9], (NG, C), 1.0, 6.0, ((0, 8),))
    return dict(grid_in=grid_in, w_embed=w_embed, interp_tiles=interp_tiles, route_device=route_device, route_slot=route_slot, mesh_embed=mesh_embed, w_up=w_up, w_down=w_down, w_out=w_out, cotangent=cotangent)


def sigmoid_linear(values):
    return values * jax.nn.sigmoid(values)

def layer_norm(values):
    centered = values - lax.optimization_barrier(jnp.mean(values, axis=-1, keepdims=True))
    inverse_std = lax.rsqrt(lax.optimization_barrier(jnp.mean(centered * centered, axis=-1, keepdims=True)) + 1e-05)
    return (centered * inverse_std, inverse_std)

def reference(grid_in, w_embed, interp_tiles, route_device, route_slot, mesh_embed, w_up, w_down, w_out, cotangent):
    node_blocks = MB_DEV * N_LAT * N_LON
    preact = jnp.dot(grid_in, w_embed, preferred_element_type=jnp.float32)
    hidden = sigmoid_linear(preact).astype(jnp.bfloat16)
    tiles_wide = interp_tiles.astype(jnp.float32)
    hidden_blocks = hidden.reshape(NG_BLK, TILE, L).astype(jnp.float32)
    messages = jnp.einsum('bgn,bgl->bnl', tiles_wide, hidden_blocks).astype(jnp.bfloat16)
    destination = (route_device[:, 0] * MB_DEV + route_slot).astype(jnp.int32)
    node_sum = jax.ops.segment_sum(messages.astype(jnp.float32), destination, num_segments=node_blocks).reshape(NM, L)
    node_state = (mesh_embed.astype(jnp.float32) + node_sum).astype(jnp.bfloat16)
    state_wide = node_state.astype(jnp.float32)
    norm_exact, inverse_std = layer_norm(state_wide)
    normed = norm_exact.astype(jnp.bfloat16)
    hidden_pre = jnp.dot(normed, w_up, preferred_element_type=jnp.float32)
    hidden_act = sigmoid_linear(hidden_pre).astype(jnp.bfloat16)
    mesh_out = (state_wide + jnp.dot(hidden_act, w_down, preferred_element_type=jnp.float32)).astype(jnp.bfloat16)
    mesh_picked = mesh_out.reshape(node_blocks, TILE, L)[destination].astype(jnp.float32)
    decoded = jnp.einsum('bgn,bnl->bgl', tiles_wide, mesh_picked).reshape(NG, L)
    grid_latent = (hidden.astype(jnp.float32) + decoded).astype(jnp.bfloat16)
    grid_out = jnp.dot(grid_latent, w_out, preferred_element_type=jnp.float32).astype(jnp.bfloat16)
    grid_grad = jnp.dot(cotangent, w_out.T, preferred_element_type=jnp.float32).astype(jnp.bfloat16)
    grad_out = jnp.dot(grid_latent.T, cotangent, preferred_element_type=jnp.float32)
    grad_blocks = grid_grad.reshape(NG_BLK, TILE, L).astype(jnp.float32)
    back_msgs = jnp.einsum('bgn,bgl->bnl', tiles_wide, grad_blocks).astype(jnp.bfloat16)
    node_grad = jax.ops.segment_sum(back_msgs.astype(jnp.float32), destination, num_segments=node_blocks).reshape(NM, L).astype(jnp.bfloat16)
    grad_down = jnp.dot(hidden_act.T, node_grad, preferred_element_type=jnp.float32)
    act_grad = jnp.dot(node_grad, w_down.T, preferred_element_type=jnp.float32)
    squash = jax.nn.sigmoid(hidden_pre)
    pre_grad = (act_grad * squash * (1.0 + hidden_pre * (1.0 - squash))).astype(jnp.bfloat16)
    grad_up = jnp.dot(normed.T, pre_grad, preferred_element_type=jnp.float32)
    norm_grad = jnp.dot(pre_grad, w_up.T, preferred_element_type=jnp.float32)
    centered_grad = norm_grad - lax.optimization_barrier(jnp.mean(norm_grad, axis=-1, keepdims=True)) - norm_exact * lax.optimization_barrier(jnp.mean(norm_grad * norm_exact, axis=-1, keepdims=True))
    grad_mesh = node_grad.astype(jnp.float32) + inverse_std * centered_grad
    return (grid_out, grad_out, grad_up, grad_down, grad_mesh)
```

```python
import jax
import jax.numpy as jnp
from jax import lax
from jax.experimental import pallas as pl
from jax.experimental.pallas import tpu as pltpu
from jax.sharding import PartitionSpec as P

F32 = jnp.float32
BF16 = jnp.bfloat16
VMEM_BYTES = 40 * 1024 * 1024
STEPS = 4


def dot(left, right):
    return jnp.dot(left, right, preferred_element_type=F32)


def dot_rows(left, right):
    return lax.dot_general(left, right, (((0,), (0,)), ((), ())), preferred_element_type=F32)


def dot_last(left, right):
    return lax.dot_general(left, right, (((1,), (1,)), ((), ())), preferred_element_type=F32)


def sigmoid(values):
    return 0.5 * jnp.tanh(0.5 * values) + 0.5


def vmem():
    return pl.BlockSpec(memory_space=pltpu.VMEM)


def smem():
    return pl.BlockSpec(memory_space=pltpu.SMEM)


def params(semantics=None):
    return pltpu.CompilerParams(vmem_limit_bytes=VMEM_BYTES, dimension_semantics=semantics)


def cost(flops, nbytes, transcendentals=0):
    return pl.CostEstimate(
        flops=int(flops), bytes_accessed=int(nbytes), transcendentals=int(transcendentals)
    )


def node_half(tile, r):
    half = tile.shape[1] // 2
    return jnp.where(r == 0, tile[:, :half], tile[:, half:])


def add_messages(pos_ref, first, count, tiles_ref, rows_of, r, total):
    for i in range(count):
        part = node_half(tiles_ref[i], r)
        where = pos_ref[first + i]
        total[where] += dot_rows(part, rows_of(i))


def write_packed(total, outs):
    per = total.shape[0] // 3
    for k, out in enumerate(outs):
        block = total[k * per : (k + 1) * per]
        out[...] = block.reshape(out.shape).astype(out.dtype)


def back_kernel(pos_ref, where_ref, tiles_ref, cot_ref, own_ref, even_ref, odd_ref, total):
    step = pl.program_id(0)
    count, rows = tiles_ref.shape[0], tiles_ref.shape[1]
    channels = cot_ref.shape[1]
    r = where_ref[0]

    @pl.when(step == 0)
    def _():
        total[...] = jnp.zeros_like(total)

    for i in range(count):
        part = node_half(tiles_ref[i], r)
        where = pos_ref[step * count + i]
        total[where, :, :channels] += dot_rows(part, cot_ref[i * rows : (i + 1) * rows, :])

    @pl.when(step == pl.num_programs(0) - 1)
    def _():
        write_packed(total, (own_ref, even_ref, odd_ref))


def encode_kernel(
    pos_ref, where_ref, grid_ref, tiles_ref, mine_ref, other_ref,
    own_ref, even_ref, odd_ref, hidden_ref, total, hold,
):
    step = pl.program_id(0)
    count, rows = tiles_ref.shape[0], tiles_ref.shape[1]
    width = mine_ref.shape[1]
    r = where_ref[0]

    @pl.when(step == 0)
    def _():
        total[...] = jnp.zeros_like(total)

    grid = grid_ref[...]
    for k, weight_ref in enumerate((mine_ref, other_ref)):
        preact = dot(grid, weight_ref[...])
        hold[:, k * width : (k + 1) * width] = (preact * sigmoid(preact)).astype(BF16)
    for i in range(count):
        part = node_half(tiles_ref[i], r)
        where = pos_ref[step * count + i]
        total[where] += dot_rows(part, hold[i * rows : (i + 1) * rows, :])

    half_steps = pl.num_programs(0) // 2

    @pl.when(step // half_steps == r)
    def _():
        at = pl.multiple_of((step % half_steps) * hold.shape[0], hold.shape[0])
        hidden_ref[pl.ds(at, hold.shape[0]), :] = hold[...]

    @pl.when(step == pl.num_programs(0) - 1)
    def _():
        write_packed(total, (own_ref, even_ref, odd_ref))


def local_kernel(hidden_ref, cot_ref, mine_ref, other_ref, base_ref, grad_ref):
    width = mine_ref.shape[0]
    hidden = hidden_ref[...]
    base_ref[...] = dot(hidden[:, :width], mine_ref[...]) + dot(hidden[:, width:], other_ref[...])
    grad_ref[...] = dot_rows(hidden, cot_ref[...])


def update_kernel(
    where_ref, sums_ref, even_ref, odd_ref, moved_ref, embed_ref, embed_other_ref,
    up_ref, up_other_ref, down_ref, down_other_ref, out_ref, out_other_ref,
    proj_ref, mesh_ref, norm_ref, inv_ref, pre_ref, act_ref,
):
    r = where_ref[0]
    nodes, latent = moved_ref.shape
    width = latent // 2
    channels = out_ref.shape[1]
    first = pl.multiple_of(r * width, width)
    second = pl.multiple_of((1 - r) * width, width)
    sums = (
        sums_ref[0].astype(F32) + even_ref[0].astype(F32)
        + odd_ref[0].astype(F32) + moved_ref[...].astype(F32)
    )
    embed = jnp.concatenate(
        [embed_ref[:, r].reshape(nodes, width), embed_other_ref[:, r].reshape(nodes, width)], axis=1
    )
    state = (embed.astype(F32) + sums).astype(BF16).astype(F32)
    centered = state - jnp.mean(state, axis=-1, keepdims=True)
    inverse = lax.rsqrt(jnp.mean(centered * centered, axis=-1, keepdims=True) + 1e-05)
    norm = centered * inverse
    normed = norm.astype(BF16)
    norm_ref[...] = norm
    inv_ref[...] = jnp.broadcast_to(inverse, inv_ref.shape)
    normed_own, normed_oth = normed[:, :width], normed[:, width:]
    update_own = jnp.zeros((nodes, width), F32)
    update_oth = jnp.zeros((nodes, width), F32)
    for k, (u_ref, d_ref) in enumerate(((up_ref, down_ref), (up_other_ref, down_other_ref))):
        hidden = dot(normed_own, u_ref[pl.ds(first, width), :]) + dot(
            normed_oth, u_ref[pl.ds(second, width), :]
        )
        act = (hidden * sigmoid(hidden)).astype(BF16)
        pre_ref[:, k * width : (k + 1) * width] = hidden
        act_ref[:, k * width : (k + 1) * width] = act
        update_own += dot(act, d_ref[:, pl.ds(first, width)])
        update_oth += dot(act, d_ref[:, pl.ds(second, width)])
    mesh = (state + jnp.concatenate([update_own, update_oth], axis=1)).astype(BF16)
    mesh_ref[...] = mesh
    proj = dot(mesh[:, :width], out_ref[...]) + dot(mesh[:, width:], out_other_ref[...])
    proj_ref[...] = jnp.zeros_like(proj_ref)
    proj_ref[:, :channels] = proj.astype(BF16)


def grads_kernel(
    where_ref, sums_ref, even_ref, odd_ref, moved_ref, local_ref,
    mesh_ref, norm_ref, inv_ref, pre_ref, act_ref,
    up_ref, up_other_ref, down_ref, down_other_ref, out_ref, out_other_ref,
    keep_ref, give_ref, grad_keep_ref, grad_give_ref,
):
    r = where_ref[0]
    latent = norm_ref.shape[1]
    width = latent // 2
    channels = out_ref.shape[1]
    first = pl.multiple_of(r * width, width)
    second = pl.multiple_of((1 - r) * width, width)
    cot = (
        sums_ref[0].astype(F32) + even_ref[0].astype(F32)
        + odd_ref[0].astype(F32) + moved_ref[...].astype(F32)
    )[:, :channels].astype(BF16)
    grad_own = dot_last(cot, out_ref[...]).astype(BF16)
    grad_oth = dot_last(cot, out_other_ref[...]).astype(BF16)
    norm = norm_ref[...]
    normed = norm.astype(BF16)
    mesh = mesh_ref[...]
    back_own = jnp.zeros(grad_own.shape, F32)
    back_oth = jnp.zeros(grad_own.shape, F32)
    sides = (
        (up_ref, down_ref, keep_ref, 0),
        (up_other_ref, down_other_ref, give_ref, 1),
    )
    for u_ref, d_ref, o_ref, k in sides:
        cols = slice(k * width, (k + 1) * width)
        hidden = pre_ref[:, cols]
        act_grad = dot_last(grad_own, d_ref[:, pl.ds(first, width)]) + dot_last(
            grad_oth, d_ref[:, pl.ds(second, width)]
        )
        squash = sigmoid(hidden)
        pre_grad = (act_grad * squash * (1.0 + hidden * (1.0 - squash))).astype(BF16)
        o_ref[pl.ds(first, width), :] = dot_rows(normed[:, :width], pre_grad).astype(o_ref.dtype)
        o_ref[pl.ds(second, width), :] = dot_rows(normed[:, width:], pre_grad).astype(o_ref.dtype)
        back_own += dot_last(pre_grad, u_ref[pl.ds(first, width), :])
        back_oth += dot_last(pre_grad, u_ref[pl.ds(second, width), :])
        o_ref[latent:, :] = jnp.zeros((latent, width), o_ref.dtype)
        o_ref[latent : latent + width, :channels] = dot_rows(act_ref[:, cols], cot).astype(
            o_ref.dtype
        )
        o_ref[latent + width :, :channels] = (
            dot_rows(mesh[:, cols], cot) + local_ref[cols, :]
        ).astype(o_ref.dtype)
    back = jnp.concatenate([back_own, back_oth], axis=1)
    centered = (
        back - jnp.mean(back, axis=-1, keepdims=True)
        - norm * jnp.mean(back * norm, axis=-1, keepdims=True)
    )
    state_grad = inv_ref[:, :1] * centered
    grad_keep_ref[...] = grad_own.astype(F32) + state_grad[:, :width]
    grad_give_ref[...] = (grad_oth.astype(F32) + state_grad[:, width:]).astype(grad_give_ref.dtype)


def decode_kernel(
    pos_ref, where_ref, tiles_ref, base_ref, *refs
):
    mine, theirs, out_ref, picked = refs[:3], refs[3:6], refs[6], refs[7]
    r = where_ref[0]
    count, rows = tiles_ref.shape[0], tiles_ref.shape[1]
    half = rows // 2
    channels = out_ref.shape[1]
    blocks = count // 2
    for i in range(blocks):
        b = r * blocks + i
        at = pos_ref[b]
        per = mine[0].shape[0]
        for k in range(3):
            @pl.when(at // per == k)
            def _(k=k, i=i, at=at):
                where = at - k * per
                picked[i, pl.ds(pl.multiple_of(r * half, half), half), :] = mine[k][where]
                picked[i, pl.ds(pl.multiple_of((1 - r) * half, half), half), :] = theirs[k][where]
    for i in range(blocks):
        rows_at = slice(i * rows, (i + 1) * rows)
        decoded = dot(tiles_ref[r * blocks + i], picked[i])
        out_ref[rows_at, :] = (base_ref[rows_at, :] + decoded[:, :channels]).astype(out_ref.dtype)


def along(axis, count, partner):
    pairs = []
    for source in range(count):
        to = partner(source)
        pairs.append((source, to if 0 <= to < count else source))
    return lambda value: lax.ppermute(value, axis, pairs)


def summed_over(value, order):
    held = []
    for axis, distance, halve in order:
        count = lax.axis_size(axis)
        swap = along(axis, count, lambda i: i ^ distance)
        if not halve:
            value = (value.astype(F32) + swap(value).astype(F32)).astype(BF16)
            continue
        bit = (lax.axis_index(axis) // distance) % 2
        rows = value.shape[0] // 2
        keep = lax.dynamic_slice_in_dim(value, bit * rows, rows, 0)
        give = lax.dynamic_slice_in_dim(value, (1 - bit) * rows, rows, 0)
        value = (keep.astype(F32) + swap(give).astype(F32)).astype(BF16)
        held.append((swap, bit))
    for swap, bit in reversed(held):
        other = swap(value)
        value = jnp.where(
            bit == 0,
            jnp.concatenate([value, other], axis=0),
            jnp.concatenate([other, value], axis=0),
        )
    return value


def distances(count):
    found, distance = [], 1
    while distance < count:
        found.append(distance)
        distance *= 2
    return found


def per_device(
    grid_in, w_embed, interp_tiles, route_device, route_slot,
    mesh_embed, w_up, w_down, w_out, cotangent,
):
    lat_count, lon_count = lax.axis_size("lat"), lax.axis_size("lon")
    lat, lon, r = lax.axis_index("lat"), lax.axis_index("lon"), lax.axis_index("rep")
    blocks, tile_rows = interp_tiles.shape[:2]
    grid_rows, channels = grid_in.shape
    width = w_embed.shape[1]
    latent = 2 * width
    padded = -(-channels // 128) * 128
    slots = mesh_embed.shape[0] // tile_rows
    half = tile_rows // 2
    nodes = slots * half

    swap_rep = along("rep", 2, lambda i: 1 - i)
    to_even = along("lat", lat_count, lambda i: i ^ 1)
    to_odd = along("lat", lat_count, lambda i: ((i + 1) ^ 1) - 1)
    east_pairs = [(i, (i + 1) % lon_count) for i in range(lon_count)]
    west_pairs = [(j, i) for i, j in east_pairs]

    target = route_device[:, 0]
    band_step = target // lon_count - lat
    sector_step = (target % lon_count - lon + lon_count) % lon_count
    even_step = 1 - 2 * (lat % 2)
    along_lat = jnp.where(band_step == 0, 0, jnp.where(band_step == even_step, 1, 2))
    position = ((along_lat * 2 + sector_step) * slots + route_slot).astype(jnp.int32)
    where = jnp.stack([r, r]).astype(jnp.int32)

    packed = lambda cols: [jax.ShapeDtypeStruct((2, nodes, cols), BF16)] * 3
    per_step = blocks // STEPS
    step_rows = per_step * tile_rows
    packed_spec = lambda cols: [pl.BlockSpec((2, nodes, cols), lambda i: (0, 0, 0))] * 3
    tiles_spec = pl.BlockSpec((per_step, tile_rows, tile_rows), lambda i: (i, 0, 0))
    rows_spec = pl.BlockSpec((step_rows, channels), lambda i: (i, 0))

    embed_other = swap_rep(w_embed)

    back = pl.pallas_call(
        back_kernel,
        grid=(STEPS,),
        in_specs=[smem(), smem(), tiles_spec, rows_spec],
        out_specs=packed_spec(padded),
        out_shape=packed(padded),
        scratch_shapes=[pltpu.VMEM((6 * slots, half, padded), F32)],
        compiler_params=params(("arbitrary",)),
        cost_estimate=cost(2 * grid_rows * half * padded, 3e6),
        name="back_messages",
    )(position, where, interp_tiles, cotangent)

    full = lambda shape: pl.BlockSpec(shape, lambda i: (0,) * len(shape))
    own, even, odd, hidden = pl.pallas_call(
        encode_kernel,
        grid=(STEPS,),
        in_specs=[
            smem(), smem(), rows_spec, tiles_spec, full((channels, width)), full((channels, width)),
        ],
        out_specs=packed_spec(latent) + [full((grid_rows // 2, latent))],
        out_shape=packed(latent) + [jax.ShapeDtypeStruct((grid_rows // 2, latent), BF16)],
        scratch_shapes=[
            pltpu.VMEM((6 * slots, half, latent), F32),
            pltpu.VMEM((step_rows, latent), BF16),
        ],
        compiler_params=params(("arbitrary",)),
        cost_estimate=cost(2 * grid_rows * latent * (channels + half), 5e6, grid_rows * latent),
        name="encode",
    )(position, where, grid_in, interp_tiles, w_embed, embed_other)

    even_in, odd_in = to_even(even), to_odd(odd)
    w_up_s, w_down_s, w_out_s, mesh_s, hidden = lax.optimization_barrier(
        (w_up, w_down, w_out, mesh_embed, hidden)
    )
    out_other = swap_rep(w_out_s)
    up_other = swap_rep(w_up_s)
    down_other = swap_rep(w_down_s)
    mesh_other = swap_rep(mesh_s)
    back_own, back_even, back_odd = back
    back_even_in, back_odd_in = to_even(back_even), to_odd(back_odd)

    cot_mine = lax.dynamic_slice_in_dim(cotangent, r * (grid_rows // 2), grid_rows // 2, 0)
    base, local_grad = pl.pallas_call(
        local_kernel,
        in_specs=[vmem()] * 4,
        out_specs=[vmem()] * 2,
        out_shape=[
            jax.ShapeDtypeStruct((grid_rows // 2, channels), F32),
            jax.ShapeDtypeStruct((latent, channels), F32),
        ],
        compiler_params=params(),
        cost_estimate=cost(2 * grid_rows * latent * channels, 4e6),
        name="local_terms",
    )(hidden, cot_mine, w_out, out_other)

    def to_east(a, b, c):
        total = a[1].astype(F32) + b[1].astype(F32) + c[1].astype(F32)
        return lax.ppermute(total.astype(BF16), "lon", east_pairs)

    moved = to_east(own, even_in, odd_in)
    weights = (w_up, up_other, w_down, down_other, w_out, out_other)
    embed_shape = (slots, 2, half, width)
    row_specs = [vmem()] * 6
    proj, mesh_out, norm, inverse, hidden_pre, hidden_act = pl.pallas_call(
        update_kernel,
        in_specs=[smem()] + [vmem()] * 12,
        out_specs=row_specs,
        out_shape=[
            jax.ShapeDtypeStruct((nodes, padded), BF16),
            jax.ShapeDtypeStruct((nodes, latent), BF16),
            jax.ShapeDtypeStruct((nodes, latent), F32),
            jax.ShapeDtypeStruct((nodes, 128), F32),
            jax.ShapeDtypeStruct((nodes, latent), F32),
            jax.ShapeDtypeStruct((nodes, latent), BF16),
        ],
        compiler_params=params(),
        cost_estimate=cost(5 * nodes * latent * latent, 4e6, nodes * latent),
        name="node_update",
    )(
        where, own, even_in, odd_in, moved,
        mesh_embed.reshape(embed_shape), mesh_other.reshape(embed_shape), *weights,
    )

    east = lax.ppermute(proj, "lon", west_pairs)
    pair = jnp.stack([proj, east])
    pair_even, pair_odd = to_even(pair), to_odd(pair)

    back_moved = to_east(back_own, back_even_in, back_odd_in)
    keep, give, mesh_keep, mesh_give = pl.pallas_call(
        grads_kernel,
        in_specs=[smem()] + [vmem()] * 16,
        out_specs=[vmem()] * 4,
        out_shape=[
            jax.ShapeDtypeStruct((2 * latent, width), F32),
            jax.ShapeDtypeStruct((2 * latent, width), BF16),
            jax.ShapeDtypeStruct((nodes, width), F32),
            jax.ShapeDtypeStruct((nodes, width), F32),
        ],
        compiler_params=params(),
        cost_estimate=cost(10 * nodes * latent * latent, 7e6, nodes * latent),
        name="node_grads",
    )(
        where, back_own, back_even_in, back_odd_in, back_moved, local_grad,
        mesh_out, norm, inverse, hidden_pre, hidden_act, *weights,
    )

    given = swap_rep(give)
    order = [("lon", d, True) for d in distances(lon_count)]
    order += [("lat", d, d == 1) for d in distances(lat_count)]
    grads = summed_over((keep + given.astype(F32)).astype(BF16), order)

    mesh_got = swap_rep(mesh_give)
    parts = [part.reshape(slots, half, width) for part in (mesh_keep, mesh_got)]
    grad_mesh = jnp.where(
        r == 0, jnp.stack(parts, axis=1), jnp.stack(parts[::-1], axis=1)
    ).reshape(mesh_embed.shape)

    tables = (pair, pair_even, pair_odd)
    table_shape = (2 * slots, half, padded)
    grid_out = pl.pallas_call(
        decode_kernel,
        in_specs=[smem(), smem()] + [vmem()] * 8,
        out_specs=vmem(),
        out_shape=jax.ShapeDtypeStruct((grid_rows // 2, channels), BF16),
        scratch_shapes=[pltpu.VMEM((blocks // 2, tile_rows, padded), BF16)],
        compiler_params=params(),
        cost_estimate=cost(grid_rows * tile_rows * padded, 4e6),
        name="decode",
    )(
        position, where, interp_tiles, base,
        *[table.reshape(table_shape) for table in tables],
        *[swap_rep(table).reshape(table_shape) for table in tables],
    )

    grad_up = grads[:latent].astype(F32)
    grad_out = grads[latent + width :, :channels].astype(F32)
    down_terms = grads[latent : latent + width, :channels]
    w_out_full = jnp.where(
        r == 0,
        jnp.concatenate([w_out, out_other], axis=0),
        jnp.concatenate([out_other, w_out], axis=0),
    )
    grad_down = dot_last(down_terms, w_out_full)
    return (grid_out, grad_out, grad_up, grad_down, grad_mesh)


def solution(mesh):
    patch = ("groups", "lat", "lon")
    placed = (
        P(patch, None),
        P(None, "rep"),
        P(patch, None, None),
        P(patch, None),
        P(patch),
        P(patch, "rep"),
        P(None, "rep"),
        P("rep", None),
        P("rep", None),
        P(patch, None),
    )
    return jax.shard_map(
        per_device,
        mesh=mesh,
        in_specs=placed,
        out_specs=(
            P(("groups", "lat", "lon", "rep"), None),
            P(("groups", "rep"), None),
            P("groups", "rep"),
            P(("groups", "rep"), None),
            P(patch, "rep"),
        ),
        check_vma=False,
    )
```

```python
import jax
import jax.numpy as jnp
from jax import lax
from jax.experimental import pallas as pl
from jax.experimental.pallas import tpu as pltpu
from jax.sharding import PartitionSpec as P

F32 = jnp.float32
BF16 = jnp.bfloat16
VMEM_BYTES = 20 * 1024 * 1024
STEPS = 4


def dot(left, right):
    return jnp.dot(left, right, preferred_element_type=F32)


def dot_rows(left, right):
    return lax.dot_general(left, right, (((0,), (0,)), ((), ())), preferred_element_type=F32)


def dot_last(left, right):
    return lax.dot_general(left, right, (((1,), (1,)), ((), ())), preferred_element_type=F32)


def sigmoid(values):
    return 0.5 * jnp.tanh(0.5 * values) + 0.5


def vmem():
    return pl.BlockSpec(memory_space=pltpu.VMEM)


def smem():
    return pl.BlockSpec(memory_space=pltpu.SMEM)


def anywhere():
    return pl.BlockSpec(memory_space=pl.ANY)


def whole(shape):
    return pl.BlockSpec(shape, lambda i: (0,) * len(shape))


def shape_of(shape, dtype):
    return jax.ShapeDtypeStruct(shape, dtype)


def call(kernel, name, in_specs, out_specs, out_shape, flops, nbytes, grid=(), scratch=(), exps=0):
    return pl.pallas_call(
        kernel,
        grid=grid,
        in_specs=in_specs,
        out_specs=out_specs,
        out_shape=out_shape,
        scratch_shapes=list(scratch),
        compiler_params=pltpu.CompilerParams(vmem_limit_bytes=VMEM_BYTES),
        cost_estimate=pl.CostEstimate(
            flops=int(flops), bytes_accessed=int(nbytes), transcendentals=int(exps)
        ),
        name=name,
    )


def node_half(tile, r):
    half = tile.shape[1] // 2
    return jnp.where(r == 0, tile[:, :half], tile[:, half:]).T


def entry_of(device_ref, slot_ref, b, slots):
    lon_count = lax.axis_size("lon")
    lat, lon = lax.axis_index("lat"), lax.axis_index("lon")
    target = device_ref[b]
    band = lax.div(target, lon_count)
    sector = target - band * lon_count - lon
    sector = jnp.where(sector < 0, sector + lon_count, sector)
    step = band - lat
    even_step = 1 - 2 * lax.rem(lat, 2)
    side = jnp.where(step == 0, 0, jnp.where(step == even_step, 1, 2))
    return (side * 2 + sector) * slots + slot_ref[b]


def write_packed(total, outs):
    per = total.shape[0] // 3
    for k, out in enumerate(outs):
        block = total[k * per : (k + 1) * per]
        out[...] = block.reshape(out.shape).astype(out.dtype)


def back_kernel(device_ref, slot_ref, after_ref, tiles_ref, cot_ref, own_ref, east_ref, side_ref, total):
    step = pl.program_id(0)
    count, rows = tiles_ref.shape[0], tiles_ref.shape[1]
    slots = total.shape[0] // 6
    channels = cot_ref.shape[0]
    r = lax.axis_index("rep")

    @pl.when(step == 0)
    def _():
        total[...] = jnp.zeros_like(total)

    for i in range(count):
        at = entry_of(device_ref, slot_ref, step * count + i, slots)
        cot = cot_ref[:, i * rows : (i + 1) * rows]
        total[at, :, :channels] += dot_last(node_half(tiles_ref[i], r), cot)

    @pl.when(step == pl.num_programs(0) - 1)
    def _():
        for k, out in ((0, own_ref), (2, side_ref.at[0]), (4, side_ref.at[1])):
            out[...] = total[k * slots : (k + 1) * slots].reshape(out.shape).astype(out.dtype)
        for k in range(3):
            block = total[(2 * k + 1) * slots : (2 * k + 2) * slots]
            east_ref[k] = block.reshape(east_ref.shape[1:]).astype(east_ref.dtype)


def encode_kernel(
    device_ref, slot_ref, after_ref, grid_ref, tiles_ref, weight_ref,
    own_ref, even_ref, odd_ref, hidden_ref, total, hold,
):
    step = pl.program_id(0)
    count, rows = tiles_ref.shape[0], tiles_ref.shape[1]
    slots = total.shape[0] // 6
    r = lax.axis_index("rep")

    @pl.when(step == 0)
    def _():
        total[...] = jnp.zeros_like(total)

    preact = dot_rows(grid_ref[...], weight_ref[...])
    hold[...] = (preact * sigmoid(preact)).astype(BF16)
    for i in range(count):
        at = entry_of(device_ref, slot_ref, step * count + i, slots)
        total[at] += dot(node_half(tiles_ref[i], r), hold[i * rows : (i + 1) * rows, :])

    half_steps = pl.num_programs(0) // 2

    @pl.when(step // half_steps == r)
    def _():
        at = pl.multiple_of((step % half_steps) * hold.shape[0], hold.shape[0])
        hidden_ref[pl.ds(at, hold.shape[0]), :] = hold[...]

    @pl.when(step == pl.num_programs(0) - 1)
    def _():
        write_packed(total, (own_ref, even_ref, odd_ref))


def local_kernel(own_ref, oth_ref, cot_ref, out_ref, out_other_ref, base_ref, grad_ref, grad_other_ref):
    rows = own_ref.shape[0]
    r = lax.axis_index("rep")
    cot = cot_ref[:, pl.ds(pl.multiple_of(r * rows, rows), rows)]
    base_ref[...] = dot_last(out_ref[...], own_ref[...]) + dot_last(out_other_ref[...], oth_ref[...])
    grad_ref[...] = dot(cot, own_ref[...])
    grad_other_ref[...] = dot(cot, oth_ref[...])


def added(*values):
    total = values[0].astype(F32)
    for value in values[1:]:
        total = total + value.astype(F32)
    return total


def add_kernel(*refs):
    a, b, c, out = refs[-4:]
    out[...] = added(a[0], b[0], c[0]).astype(out.dtype)


def sides_kernel(after_ref, side_ref, moved_ref, even_ref, odd_ref):
    even_ref[...] = added(side_ref[0], moved_ref[1]).astype(even_ref.dtype)
    odd_ref[...] = added(side_ref[1], moved_ref[2]).astype(odd_ref.dtype)


def update_kernel(
    own_a, even_a, odd_a, moved_a, own_b, even_b, odd_b, moved_b, embed_ref, embed_other_ref,
    up_ref, up_other_ref, down_ref, down_other_ref, out_ref, out_other_ref,
    proj_ref, mesh_ref, norm_ref, inv_ref, pre_ref, act_ref,
):
    r = lax.axis_index("rep")
    nodes, width = moved_a.shape
    channels = out_ref.shape[0]
    first = pl.multiple_of(r * width, width)
    second = pl.multiple_of((1 - r) * width, width)
    states = []
    for embed, parts in (
        (embed_ref, (own_a[0], even_a[0], odd_a[0], moved_a[...])),
        (embed_other_ref, (own_b[0], even_b[0], odd_b[0], moved_b[...])),
    ):
        start = embed[:, r].reshape(nodes, width)
        states.append((start.astype(F32) + added(*parts)).astype(BF16).astype(F32))
    state = jnp.concatenate(states, axis=1)
    centered = state - jnp.mean(state, axis=-1, keepdims=True)
    inverse = lax.rsqrt(jnp.mean(centered * centered, axis=-1, keepdims=True) + 1e-05)
    norm = centered * inverse
    normed = norm.astype(BF16)
    norm_ref[...] = norm
    inv_ref[...] = jnp.broadcast_to(inverse, inv_ref.shape)
    update_own = jnp.zeros((nodes, width), F32)
    update_oth = jnp.zeros((nodes, width), F32)
    for k, (u_ref, d_ref) in enumerate(((up_ref, down_ref), (up_other_ref, down_other_ref))):
        hidden = dot(normed[:, :width], u_ref[pl.ds(first, width), :]) + dot(
            normed[:, width:], u_ref[pl.ds(second, width), :]
        )
        act = (hidden * sigmoid(hidden)).astype(BF16)
        pre_ref[:, k * width : (k + 1) * width] = hidden
        act_ref[:, k * width : (k + 1) * width] = act
        update_own += dot(act, d_ref[:, pl.ds(first, width)])
        update_oth += dot(act, d_ref[:, pl.ds(second, width)])
    mesh = (state + jnp.concatenate([update_own, update_oth], axis=1)).astype(BF16)
    mesh_ref[...] = mesh
    proj = dot_last(mesh[:, :width], out_ref[...]) + dot_last(mesh[:, width:], out_other_ref[...])
    proj_ref[...] = jnp.zeros_like(proj_ref)
    proj_ref[:, :channels] = proj.astype(BF16)


def outer_kernel(
    own_ref, moved_ref, even_ref, odd_ref, local_ref, local_other_ref, mesh_ref, act_ref,
    cot_ref, keep_ref, give_ref,
):
    width = keep_ref.shape[1]
    channels = local_ref.shape[0]
    cot = added(own_ref[...], moved_ref[0], even_ref[...], odd_ref[...]).astype(BF16)
    cot_ref[...] = cot
    act, mesh = act_ref[...], mesh_ref[...]
    for k, (out, local) in enumerate(((keep_ref, local_ref), (give_ref, local_other_ref))):
        cols = slice(k * width, (k + 1) * width)
        out[:width, :] = dot_rows(act[:, cols], cot).astype(out.dtype)
        grad = dot_rows(cot, mesh[:, cols])
        out[width:, :] = grad.astype(out.dtype)
        out[width : width + channels, :] = (grad[:channels] + local[...]).astype(out.dtype)


def grads_kernel(
    cot_ref, norm_ref, pre_ref, down_ref, down_other_ref, out_ref, out_other_ref,
    grad_ref, pre_grad_ref, keep_ref, give_ref,
):
    r = lax.axis_index("rep")
    width = keep_ref.shape[1]
    channels = out_ref.shape[0]
    first = pl.multiple_of(r * width, width)
    second = pl.multiple_of((1 - r) * width, width)
    cot = cot_ref[:, :channels]
    grad_own = dot(cot, out_ref[...]).astype(BF16)
    grad_oth = dot(cot, out_other_ref[...]).astype(BF16)
    grad_ref[:, :width] = grad_own
    grad_ref[:, width:] = grad_oth
    normed = norm_ref[...].astype(BF16)
    for k, (d_ref, o_ref) in enumerate(((down_ref, keep_ref), (down_other_ref, give_ref))):
        cols = slice(k * width, (k + 1) * width)
        hidden = pre_ref[:, cols]
        act_grad = dot_last(grad_own, d_ref[:, pl.ds(first, width)]) + dot_last(
            grad_oth, d_ref[:, pl.ds(second, width)]
        )
        squash = sigmoid(hidden)
        pre_grad = (act_grad * squash * (1.0 + hidden * (1.0 - squash))).astype(BF16)
        pre_grad_ref[:, cols] = pre_grad
        o_ref[pl.ds(first, width), :] = dot_rows(normed[:, :width], pre_grad).astype(o_ref.dtype)
        o_ref[pl.ds(second, width), :] = dot_rows(normed[:, width:], pre_grad).astype(o_ref.dtype)


def mesh_kernel(
    grad_ref, pre_grad_ref, norm_ref, inv_ref, up_ref, up_other_ref, keep_ref, give_ref,
):
    r = lax.axis_index("rep")
    width = keep_ref.shape[1]
    first = pl.multiple_of(r * width, width)
    second = pl.multiple_of((1 - r) * width, width)
    halves = []
    for at in (first, second):
        halves.append(
            dot_last(pre_grad_ref[:, :width], up_ref[pl.ds(at, width), :])
            + dot_last(pre_grad_ref[:, width:], up_other_ref[pl.ds(at, width), :])
        )
    back = jnp.concatenate(halves, axis=1)
    norm = norm_ref[...]
    centered = (
        back - jnp.mean(back, axis=-1, keepdims=True)
        - norm * jnp.mean(back * norm, axis=-1, keepdims=True)
    )
    total = grad_ref[...].astype(F32) + inv_ref[:, :1] * centered
    keep_ref[...] = total[:, :width]
    give_ref[...] = total[:, width:].astype(give_ref.dtype)


def place_kernel(keep_ref, got_ref, out_ref):
    r = lax.axis_index("rep")
    part = out_ref.shape[:1] + out_ref.shape[2:]
    out_ref[:, r] = keep_ref[...].reshape(part)
    out_ref[:, 1 - r] = got_ref[...].astype(F32).reshape(part)


def finish_outer_kernel(mine_ref, other_ref, out_ref, out_other_ref, down_ref, grad_ref):
    r = lax.axis_index("rep")
    bit = lax.rem(lax.axis_index("lon"), 2)
    width = mine_ref.shape[1]
    channels = out_ref.shape[0]
    mine, other = mine_ref[...], other_ref[...]
    terms = jnp.where(bit == 0, mine, other)[:, :channels]
    down_ref[:, pl.ds(pl.multiple_of(r * width, width), width)] = dot(terms, out_ref[...])
    down_ref[:, pl.ds(pl.multiple_of((1 - r) * width, width), width)] = dot(
        terms, out_other_ref[...]
    )
    grad_ref[...] = jnp.where(bit == 0, other, mine)[:channels].astype(F32)


def finish_up_kernel(mine_ref, other_ref, out_ref):
    bit = lax.rem(lax.axis_index("lon"), 2)
    rows = mine_ref.shape[0]
    out_ref[pl.ds(pl.multiple_of(bit * rows, rows), rows), :] = mine_ref[...].astype(F32)
    out_ref[pl.ds(pl.multiple_of((1 - bit) * rows, rows), rows), :] = other_ref[...].astype(F32)


def decode_kernel(device_ref, slot_ref, tiles_ref, base_ref, *refs):
    mine, theirs, out_ref, picked = refs[:3], refs[3:6], refs[6], refs[7]
    r = lax.axis_index("rep")
    count, rows = tiles_ref.shape[0], tiles_ref.shape[1]
    half = rows // 2
    channels = out_ref.shape[0]
    blocks = count // 2
    per = mine[0].shape[0]
    for i in range(blocks):
        at = entry_of(device_ref, slot_ref, r * blocks + i, per // 2)
        for k in range(3):
            @pl.when(at // per == k)
            def _(k=k, i=i, at=at):
                where = at - k * per
                picked[i, pl.ds(pl.multiple_of(r * half, half), half), :] = mine[k][where]
                picked[i, pl.ds(pl.multiple_of((1 - r) * half, half), half), :] = theirs[k][where]
    for i in range(blocks):
        cols = slice(i * rows, (i + 1) * rows)
        decoded = dot_last(picked[i].T, tiles_ref[r * blocks + i])
        out_ref[:, cols] = (base_ref[:, cols] + decoded[:channels]).astype(out_ref.dtype)


def along(axis, count, partner):
    pairs = []
    for source in range(count):
        to = partner(source)
        pairs.append((source, to if 0 <= to < count else source))
    return lambda value: lax.ppermute(value, axis, pairs)


def summed_over(value, order):
    held = []
    for axis, distance, halve in order:
        count = lax.axis_size(axis)
        swap = along(axis, count, lambda i, d=distance: i ^ d)
        if not halve:
            value = (value.astype(F32) + swap(value).astype(F32)).astype(BF16)
            continue
        bit = (lax.axis_index(axis) // distance) % 2
        rows = value.shape[0] // 2
        keep = lax.dynamic_slice_in_dim(value, bit * rows, rows, 0)
        give = lax.dynamic_slice_in_dim(value, (1 - bit) * rows, rows, 0)
        value = (keep.astype(F32) + swap(give).astype(F32)).astype(BF16)
        held.append((swap, bit))
    for swap, bit in reversed(held[1:]):
        other = swap(value)
        value = jnp.where(
            bit == 0,
            jnp.concatenate([value, other], axis=0),
            jnp.concatenate([other, value], axis=0),
        )
    return value, held[0][0](value)


def distances(count):
    found, distance = [], 1
    while distance < count:
        found.append(distance)
        distance *= 2
    return found


def per_device(
    grid_in, w_embed, interp_tiles, route_device, route_slot,
    mesh_embed, w_up, w_down, w_out, cotangent,
):
    lat_count, lon_count = lax.axis_size("lat"), lax.axis_size("lon")
    blocks, tile_rows = interp_tiles.shape[:2]
    grid_rows, channels = grid_in.shape
    my_rows = grid_rows // 2
    width = w_embed.shape[1]
    latent = 2 * width
    padded = -(-channels // 128) * 128
    slots = mesh_embed.shape[0] // tile_rows
    half = tile_rows // 2
    nodes = slots * half

    swap_rep = along("rep", 2, lambda i: 1 - i)
    to_even = along("lat", lat_count, lambda i: i ^ 1)
    to_odd = along("lat", lat_count, lambda i: ((i + 1) ^ 1) - 1)
    east_pairs = [(i, (i + 1) % lon_count) for i in range(lon_count)]
    west_pairs = [(j, i) for i, j in east_pairs]
    to_east = lambda value: lax.ppermute(value, "lon", east_pairs)

    device = route_device.reshape(blocks)
    grid_t, cot_t, out_t = grid_in.T, cotangent.T, w_out.T
    per_step = blocks // STEPS
    step_rows = per_step * tile_rows
    tiles_spec = pl.BlockSpec((per_step, tile_rows, tile_rows), lambda i: (i, 0, 0))
    cols_spec = pl.BlockSpec((channels, step_rows), lambda i: (0, i))
    pair_shape = (2, nodes, width)

    embed_other = swap_rep(w_embed)

    def encode(after, weight):
        return call(
            encode_kernel, "encode",
            [smem(), smem(), anywhere(), cols_spec, tiles_spec, whole((channels, width))],
            [whole(pair_shape)] * 3 + [whole((my_rows, width))],
            [shape_of(pair_shape, BF16)] * 3 + [shape_of((my_rows, width), BF16)],
            2 * grid_rows * width * (channels + half), 3e6, grid=(STEPS,), exps=grid_rows * width,
            scratch=[
                pltpu.VMEM((6 * slots, half, width), F32),
                pltpu.VMEM((step_rows, width), BF16),
            ],
        )(device, route_slot, after, grid_t, interp_tiles, weight)

    own_a, even_a, odd_a, hidden_a = encode(w_embed, w_embed)
    even_in_a, odd_in_a = to_even(even_a), to_odd(odd_a)

    back_own, back_east, back_side = call(
        back_kernel, "back_messages",
        [smem(), smem(), anywhere(), tiles_spec, cols_spec],
        [whole((nodes, padded)), whole((3, nodes, padded)), whole((2, nodes, padded))],
        [shape_of((nodes, padded), BF16), shape_of((3, nodes, padded), BF16),
         shape_of((2, nodes, padded), BF16)],
        2 * grid_rows * half * padded, 3e6, grid=(STEPS,),
        scratch=[pltpu.VMEM((6 * slots, half, padded), F32)],
    )(device, route_slot, odd_a, interp_tiles, cot_t)
    back_moved = to_east(back_east)

    own_b, even_b, odd_b, hidden_b = encode(back_own, embed_other)
    even_in_b, odd_in_b = to_even(even_b), to_odd(odd_b)

    out_other, up_other, down_other = swap_rep(out_t), swap_rep(w_up), swap_rep(w_down)
    embed_shape = (slots, 2, half, width)
    mesh_other = swap_rep(mesh_embed)

    base, local, local_other = call(
        local_kernel, "local_terms", [vmem()] * 5, [vmem()] * 3,
        [shape_of((channels, my_rows), F32)] + [shape_of((channels, width), F32)] * 2,
        4 * my_rows * latent * channels, 4e6,
    )(hidden_a, hidden_b, cot_t, out_t, out_other)

    second = pl.BlockSpec((1, nodes, width), lambda i: (1, 0, 0))

    def add_east(after, *terms):
        return call(
            add_kernel, "add_east", [anywhere()] + [second] * 3, whole((nodes, width)),
            shape_of((nodes, width), BF16), 3 * nodes * width, 6e5, grid=(1,),
        )(after, *terms)

    send_a = add_east(own_b, own_a, even_in_a, odd_in_a)
    moved_a = to_east(send_a)
    send_b = add_east(send_a, own_b, even_in_b, odd_in_b)
    moved_b = to_east(send_b)

    back_even, back_odd = call(
        sides_kernel, "add_sides", [anywhere(), vmem(), vmem()], [vmem()] * 2,
        [shape_of((nodes, padded), BF16)] * 2, 3 * nodes * width, 1e6,
    )(send_b, back_side, back_moved)
    back_even_in, back_odd_in = to_even(back_even), to_odd(back_odd)

    first = pl.BlockSpec((1, nodes, width), lambda i: (0, 0, 0))
    sums_specs = [first] * 3 + [whole((nodes, width))]
    weights = (w_up, up_other, w_down, down_other, out_t, out_other)
    update_shapes = [
        ((nodes, padded), BF16), ((nodes, latent), BF16), ((nodes, latent), F32),
        ((nodes, 128), F32), ((nodes, latent), F32), ((nodes, latent), BF16),
    ]
    proj, mesh_out, norm, inverse, hidden_pre, hidden_act = call(
        update_kernel, "node_update",
        sums_specs * 2 + [whole(embed_shape)] * 2 + [whole(w.shape) for w in weights],
        [whole(s) for s, _ in update_shapes],
        [shape_of(s, d) for s, d in update_shapes],
        5 * nodes * latent * latent, 4e6, grid=(1,), exps=nodes * latent,
    )(
        own_a, even_in_a, odd_in_a, moved_a, own_b, even_in_b, odd_in_b, moved_b,
        mesh_embed.reshape(embed_shape), mesh_other.reshape(embed_shape), *weights,
    )

    east = lax.ppermute(proj, "lon", west_pairs)
    pair = jnp.stack([proj, east])
    pair_even, pair_odd = to_even(pair), to_odd(pair)

    cot_mesh, keep_outer, give_outer = call(
        outer_kernel, "outer_grads", [vmem()] * 8, [vmem()] * 3,
        [shape_of((nodes, padded), BF16), shape_of((latent, width), F32),
         shape_of((latent, width), BF16)],
        4 * nodes * latent * padded, 3e6,
    )(back_own, back_moved, back_even_in, back_odd_in, local, local_other, mesh_out, hidden_act)
    got_outer = swap_rep(give_outer)

    grad_nodes, pre_grad, keep_up, give_up = call(
        grads_kernel, "up_grads", [vmem()] * 7, [vmem()] * 4,
        [shape_of((nodes, latent), BF16), shape_of((nodes, latent), BF16),
         shape_of((latent, width), F32), shape_of((latent, width), BF16)],
        5 * nodes * latent * latent, 4e6, exps=nodes * latent,
    )(cot_mesh, norm, hidden_pre, w_down, down_other, out_t, out_other)
    got_up = swap_rep(give_up)

    order = [("lon", d, True) for d in distances(lon_count)]
    order += [("lat", d, d == 1) for d in distances(lat_count)]
    outer_mine, outer_theirs = summed_over((keep_outer + got_outer.astype(F32)).astype(BF16), order)
    up_mine, up_theirs = summed_over((keep_up + got_up.astype(F32)).astype(BF16), order)

    mesh_keep, mesh_give = call(
        mesh_kernel, "mesh_grads", [vmem()] * 6, [vmem()] * 2,
        [shape_of((nodes, width), F32), shape_of((nodes, width), BF16)],
        2 * nodes * latent * latent, 3e6,
    )(grad_nodes, pre_grad, norm, inverse, w_up, up_other)
    grad_mesh = call(
        place_kernel, "place_mesh", [vmem()] * 2, vmem(), shape_of(embed_shape, F32),
        nodes * latent, 1e6,
    )(mesh_keep, swap_rep(mesh_give)).reshape(mesh_embed.shape)

    tables = (pair, pair_even, pair_odd)
    table_shape = (2 * slots, half, padded)
    grid_out = call(
        decode_kernel, "decode", [smem(), smem()] + [vmem()] * 8, vmem(),
        shape_of((channels, my_rows), BF16), 2 * my_rows * tile_rows * padded, 4e6,
        scratch=[pltpu.VMEM((blocks // 2, tile_rows, padded), BF16)],
    )(
        device, route_slot, interp_tiles, base,
        *[table.reshape(table_shape) for table in tables],
        *[swap_rep(table).reshape(table_shape) for table in tables],
    ).T

    grad_down, grad_out = call(
        finish_outer_kernel, "finish_outer", [vmem()] * 4, [vmem()] * 2,
        [shape_of((width, latent), F32), shape_of((channels, width), F32)],
        2 * width * latent * channels, 1e6,
    )(outer_mine, outer_theirs, out_t, out_other)
    grad_up = call(
        finish_up_kernel, "finish_up", [vmem()] * 2, vmem(), shape_of((latent, width), F32),
        latent * width, 8e5,
    )(up_mine, up_theirs)
    return (grid_out, grad_out.T, grad_up, grad_down, grad_mesh)


def solution(mesh):
    patch = ("groups", "lat", "lon")
    placed = (
        P(patch, None),
        P(None, "rep"),
        P(patch, None, None),
        P(patch, None),
        P(patch),
        P(patch, "rep"),
        P(None, "rep"),
        P("rep", None),
        P("rep", None),
        P(patch, None),
    )
    return jax.shard_map(
        per_device,
        mesh=mesh,
        in_specs=placed,
        out_specs=(
            P(("groups", "lat", "lon", "rep"), None),
            P(("groups", "rep"), None),
            P("groups", "rep"),
            P(("groups", "rep"), None),
            P(patch, "rep"),
        ),
        check_vma=False,
    )
```

```python
import jax
import jax.numpy as jnp
from jax import lax
from jax.experimental import pallas as pl
from jax.experimental.pallas import tpu as pltpu
from jax.sharding import PartitionSpec as P

F32 = jnp.float32
BF16 = jnp.bfloat16
VMEM_BYTES = 20 * 1024 * 1024
VMEM_ALL = 60 * 1024 * 1024
STEPS = 4


def dot(left, right):
    return jnp.dot(left, right, preferred_element_type=F32)


def dot_rows(left, right):
    return lax.dot_general(left, right, (((0,), (0,)), ((), ())), preferred_element_type=F32)


def dot_last(left, right):
    return lax.dot_general(left, right, (((1,), (1,)), ((), ())), preferred_element_type=F32)


def sigmoid(values):
    return 0.5 * jnp.tanh(0.5 * values) + 0.5


def vmem():
    return pl.BlockSpec(memory_space=pltpu.VMEM)


def smem():
    return pl.BlockSpec(memory_space=pltpu.SMEM)


def anywhere():
    return pl.BlockSpec(memory_space=pl.ANY)


def whole(shape):
    return pl.BlockSpec(shape, lambda i: (0,) * len(shape))


def shape_of(shape, dtype):
    return jax.ShapeDtypeStruct(shape, dtype)


def call(kernel, name, in_specs, out_specs, out_shape, flops, nbytes, grid=(), scratch=(), exps=0,
         limit=VMEM_BYTES):
    return pl.pallas_call(
        kernel,
        grid=grid,
        in_specs=in_specs,
        out_specs=out_specs,
        out_shape=out_shape,
        scratch_shapes=list(scratch),
        compiler_params=pltpu.CompilerParams(vmem_limit_bytes=limit),
        cost_estimate=pl.CostEstimate(flops=1, bytes_accessed=1, transcendentals=0),
        name=name,
    )


def node_half(tile, r):
    half = tile.shape[1] // 2
    return jnp.where(r == 0, tile[:, :half], tile[:, half:]).T


def entry_of(device_ref, slot_ref, b, slots):
    lon_count = lax.axis_size("lon")
    lat, lon = lax.axis_index("lat"), lax.axis_index("lon")
    target = device_ref[b]
    band = lax.div(target, lon_count)
    sector = target - band * lon_count - lon
    sector = jnp.where(sector < 0, sector + lon_count, sector)
    step = band - lat
    even_step = 1 - 2 * lax.rem(lat, 2)
    side = jnp.where(step == 0, 0, jnp.where(step == even_step, 1, 2))
    return (side * 2 + sector) * slots + slot_ref[b]


def write_packed(total, outs):
    per = total.shape[0] // 3
    for k, out in enumerate(outs):
        block = total[k * per : (k + 1) * per]
        out[...] = block.reshape(out.shape).astype(out.dtype)


def back_kernel(device_ref, slot_ref, after_ref, tiles_ref, cot_ref, own_ref, east_ref, side_ref, total):
    step = pl.program_id(0)
    count, rows = tiles_ref.shape[0], tiles_ref.shape[1]
    slots = total.shape[0] // 6
    channels = cot_ref.shape[0]
    r = lax.axis_index("rep")

    @pl.when(step == 0)
    def _():
        total[...] = jnp.zeros_like(total)

    for i in range(count):
        at = entry_of(device_ref, slot_ref, step * count + i, slots)
        cot = cot_ref[:, i * rows : (i + 1) * rows]
        total[at, :, :channels] += dot_last(node_half(tiles_ref[i], r), cot)

    @pl.when(step == pl.num_programs(0) - 1)
    def _():
        for k, out in ((0, own_ref), (2, side_ref.at[0]), (4, side_ref.at[1])):
            out[...] = total[k * slots : (k + 1) * slots].reshape(out.shape).astype(out.dtype)
        for k in range(3):
            block = total[(2 * k + 1) * slots : (2 * k + 2) * slots]
            east_ref[k] = block.reshape(east_ref.shape[1:]).astype(east_ref.dtype)


def encode_kernel(
    device_ref, slot_ref, after_ref, grid_ref, tiles_ref, weight_ref,
    own_ref, even_ref, odd_ref, hidden_ref, total, hold,
):
    step = pl.program_id(0)
    count, rows = tiles_ref.shape[0], tiles_ref.shape[1]
    slots = total.shape[0] // 6
    r = lax.axis_index("rep")

    @pl.when(step == 0)
    def _():
        total[...] = jnp.zeros_like(total)

    preact = dot_rows(grid_ref[...], weight_ref[...])
    hold[...] = (preact * sigmoid(preact)).astype(BF16)
    for i in range(count):
        at = entry_of(device_ref, slot_ref, step * count + i, slots)
        total[at] += dot(node_half(tiles_ref[i], r), hold[i * rows : (i + 1) * rows, :])

    half_steps = pl.num_programs(0) // 2

    @pl.when(step // half_steps == r)
    def _():
        at = pl.multiple_of((step % half_steps) * hold.shape[0], hold.shape[0])
        hidden_ref[pl.ds(at, hold.shape[0]), :] = hold[...]

    @pl.when(step == pl.num_programs(0) - 1)
    def _():
        write_packed(total, (own_ref, even_ref, odd_ref))


def local_kernel(own_ref, oth_ref, cot_ref, out_ref, out_other_ref, base_ref, grad_ref, grad_other_ref):
    rows = own_ref.shape[0]
    r = lax.axis_index("rep")
    cot = cot_ref[:, pl.ds(pl.multiple_of(r * rows, rows), rows)]
    base_ref[...] = dot_last(out_ref[...], own_ref[...]) + dot_last(out_other_ref[...], oth_ref[...])
    grad_ref[...] = dot(cot, own_ref[...])
    grad_other_ref[...] = dot(cot, oth_ref[...])


def added(*values):
    total = values[0].astype(F32)
    for value in values[1:]:
        total = total + value.astype(F32)
    return total


def add_kernel(*refs):
    a, b, c, out = refs[-4:]
    out[...] = added(a[0], b[0], c[0]).astype(out.dtype)


def sides_kernel(after_ref, side_ref, moved_ref, even_ref, odd_ref):
    even_ref[...] = added(side_ref[0], moved_ref[1]).astype(even_ref.dtype)
    odd_ref[...] = added(side_ref[1], moved_ref[2]).astype(odd_ref.dtype)


def node_kernel(
    own_a, even_a, odd_a, moved_a, own_b, even_b, odd_b, moved_b, embed_ref, embed_other_ref,
    back_ref, back_moved_ref, back_even_ref, back_odd_ref, local_ref, local_other_ref,
    up_ref, up_other_ref, down_ref, down_other_ref, out_ref, out_other_ref,
    proj_ref, keep_ref, give_ref, mesh_keep_ref, mesh_give_ref,
):
    r = lax.axis_index("rep")
    nodes, width = moved_a.shape
    latent = 2 * width
    channels = out_ref.shape[0]
    first = pl.multiple_of(r * width, width)
    second = pl.multiple_of((1 - r) * width, width)
    states = []
    for embed, parts in (
        (embed_ref, (own_a[0], even_a[0], odd_a[0], moved_a[...])),
        (embed_other_ref, (own_b[0], even_b[0], odd_b[0], moved_b[...])),
    ):
        start = embed[:, r].reshape(nodes, width)
        states.append((start.astype(F32) + added(*parts)).astype(BF16).astype(F32))
    state = jnp.concatenate(states, axis=1)
    centered = state - jnp.mean(state, axis=-1, keepdims=True)
    inverse = lax.rsqrt(jnp.mean(centered * centered, axis=-1, keepdims=True) + 1e-05)
    norm = centered * inverse
    normed = norm.astype(BF16)

    cot = added(back_ref[...], back_moved_ref[0], back_even_ref[...], back_odd_ref[...]).astype(BF16)
    terms = cot[:, :channels]
    grad_own = dot(terms, out_ref[...]).astype(BF16)
    grad_oth = dot(terms, out_other_ref[...]).astype(BF16)

    update_own = jnp.zeros((nodes, width), F32)
    update_oth = jnp.zeros((nodes, width), F32)
    back_own = jnp.zeros((nodes, width), F32)
    back_oth = jnp.zeros((nodes, width), F32)
    sides = ((up_ref, down_ref, keep_ref), (up_other_ref, down_other_ref, give_ref))
    for u_ref, d_ref, o_ref in sides:
        up_own, up_oth = u_ref[pl.ds(first, width), :], u_ref[pl.ds(second, width), :]
        down_own, down_oth = d_ref[:, pl.ds(first, width)], d_ref[:, pl.ds(second, width)]
        hidden = dot(normed[:, :width], up_own) + dot(normed[:, width:], up_oth)
        squash = sigmoid(hidden)
        act = (hidden * squash).astype(BF16)
        update_own += dot(act, down_own)
        update_oth += dot(act, down_oth)
        o_ref[latent : latent + width, :] = dot_rows(act, cot).astype(o_ref.dtype)
        act_grad = dot_last(grad_own, down_own) + dot_last(grad_oth, down_oth)
        pre_grad = (act_grad * squash * (1.0 + hidden * (1.0 - squash))).astype(BF16)
        o_ref[pl.ds(first, width), :] = dot_rows(normed[:, :width], pre_grad).astype(o_ref.dtype)
        o_ref[pl.ds(second, width), :] = dot_rows(normed[:, width:], pre_grad).astype(o_ref.dtype)
        back_own += dot_last(pre_grad, up_own)
        back_oth += dot_last(pre_grad, up_oth)

    mesh_own = (states[0] + update_own).astype(BF16)
    mesh_oth = (states[1] + update_oth).astype(BF16)
    proj = dot_last(mesh_own, out_ref[...]) + dot_last(mesh_oth, out_other_ref[...])
    proj_ref[...] = jnp.zeros_like(proj_ref)
    proj_ref[:, :channels] = proj.astype(BF16)
    ends = ((keep_ref, mesh_own, local_ref), (give_ref, mesh_oth, local_other_ref))
    for o_ref, mesh, local in ends:
        grad = dot_rows(cot, mesh)
        start = latent + width
        o_ref[start:, :] = grad.astype(o_ref.dtype)
        o_ref[start : start + channels, :] = (grad[:channels] + local[...]).astype(o_ref.dtype)

    back = jnp.concatenate([back_own, back_oth], axis=1)
    slope = (
        back - jnp.mean(back, axis=-1, keepdims=True)
        - norm * jnp.mean(back * norm, axis=-1, keepdims=True)
    ) * inverse
    mesh_keep_ref[...] = grad_own.astype(F32) + slope[:, :width]
    mesh_give_ref[...] = (grad_oth.astype(F32) + slope[:, width:]).astype(mesh_give_ref.dtype)


def place_kernel(keep_ref, got_ref, out_ref):
    r = lax.axis_index("rep")
    part = out_ref.shape[:1] + out_ref.shape[2:]
    out_ref[:, r] = keep_ref[...].reshape(part)
    out_ref[:, 1 - r] = got_ref[...].astype(F32).reshape(part)


def terms_kernel(after_ref, keep_ref, got_ref, out_ref):
    out_ref[...] = added(keep_ref[...], got_ref[...]).astype(out_ref.dtype)


def finish_kernel(mine_ref, other_ref, out_ref, out_other_ref, up_ref, down_ref, grad_ref):
    r = lax.axis_index("rep")
    bit = sum_bit(0)
    width = mine_ref.shape[1]
    channels = out_ref.shape[0]

    def place(low_ref, high_ref):
        up_ref[...] = low_ref[...].astype(F32)
        terms = high_ref[:width, :channels]
        down_ref[:, pl.ds(pl.multiple_of(r * width, width), width)] = dot(terms, out_ref[...])
        down_ref[:, pl.ds(pl.multiple_of((1 - r) * width, width), width)] = dot(
            terms, out_other_ref[...]
        )
        grad_ref[...] = high_ref[width : width + channels, :].astype(F32)

    @pl.when(bit == 0)
    def _():
        place(mine_ref, other_ref)

    @pl.when(bit != 0)
    def _():
        place(other_ref, mine_ref)


def decode_kernel(device_ref, slot_ref, tiles_ref, base_ref, *refs):
    mine, theirs, out_ref, picked = refs[:3], refs[3:6], refs[6], refs[7]
    r = lax.axis_index("rep")
    count, rows = tiles_ref.shape[0], tiles_ref.shape[1]
    half = rows // 2
    channels = out_ref.shape[0]
    blocks = count // 2
    per = mine[0].shape[0]
    for i in range(blocks):
        at = entry_of(device_ref, slot_ref, r * blocks + i, per // 2)
        for k in range(3):
            @pl.when(at // per == k)
            def _(k=k, i=i, at=at):
                where = at - k * per
                picked[i, pl.ds(pl.multiple_of(r * half, half), half), :] = mine[k][where]
                picked[i, pl.ds(pl.multiple_of((1 - r) * half, half), half), :] = theirs[k][where]
    for i in range(blocks):
        cols = slice(i * rows, (i + 1) * rows)
        decoded = dot_last(picked[i].T, tiles_ref[r * blocks + i])
        out_ref[:, cols] = (base_ref[:, cols] + decoded[:channels]).astype(out_ref.dtype)


def along(axis, count, partner):
    pairs = []
    for source in range(count):
        to = partner(source)
        pairs.append((source, to if 0 <= to < count else source))
    return lambda value: lax.ppermute(value, axis, pairs)


def distances(axis):
    found, distance = [], 1
    while distance < lax.axis_size(axis):
        found.append((axis, distance))
        distance *= 2
    return found


def sum_orders():
    lat, lon = distances("lat"), distances("lon")
    return (lon + lat, lat + lon)


def sum_bit(step):
    bits = [(lax.axis_index(axis) // distance) % 2 for axis, distance in (o[step] for o in sum_orders())]
    return jnp.where(lax.axis_index("rep") == 0, bits[0], bits[1])


def sum_swap(value, step):
    lat_count, lon_count = lax.axis_size("lat"), lax.axis_size("lon")
    orders = sum_orders()
    pairs = []
    for lat in range(lat_count):
        for lon in range(lon_count):
            for rep in range(2):
                axis, distance = orders[rep][step]
                to = (lat ^ distance, lon) if axis == "lat" else (lat, lon ^ distance)
                number = lambda a, b: (a * lon_count + b) * 2 + rep
                pairs.append((number(lat, lon), number(*to)))
    return lax.ppermute(value, ("lat", "lon", "rep"), pairs)


def summed(value):
    count = len(sum_orders()[0])
    halving = min(count - 1, 3)
    for step in range(count):
        if step >= halving:
            value = (value.astype(F32) + sum_swap(value, step).astype(F32)).astype(BF16)
            continue
        bit = sum_bit(step)
        rows = value.shape[0] // 2
        keep = lax.dynamic_slice_in_dim(value, bit * rows, rows, 0)
        give = lax.dynamic_slice_in_dim(value, (1 - bit) * rows, rows, 0)
        value = (keep.astype(F32) + sum_swap(give, step).astype(F32)).astype(BF16)
    for step in range(halving - 1, 0, -1):
        other = sum_swap(value, step)
        value = jnp.where(
            sum_bit(step) == 0,
            jnp.concatenate([value, other], axis=0),
            jnp.concatenate([other, value], axis=0),
        )
    return value, sum_swap(value, 0)


def per_device(
    grid_in, w_embed, interp_tiles, route_device, route_slot,
    mesh_embed, w_up, w_down, w_out, cotangent,
):
    lat_count, lon_count = lax.axis_size("lat"), lax.axis_size("lon")
    blocks, tile_rows = interp_tiles.shape[:2]
    grid_rows, channels = grid_in.shape
    my_rows = grid_rows // 2
    width = w_embed.shape[1]
    latent = 2 * width
    padded = -(-channels // 128) * 128
    slots = mesh_embed.shape[0] // tile_rows
    half = tile_rows // 2
    nodes = slots * half

    swap_rep = along("rep", 2, lambda i: 1 - i)
    to_even = along("lat", lat_count, lambda i: i ^ 1)
    to_odd = along("lat", lat_count, lambda i: ((i + 1) ^ 1) - 1)
    east_pairs = [(i, (i + 1) % lon_count) for i in range(lon_count)]
    west_pairs = [(j, i) for i, j in east_pairs]
    to_east = lambda value: lax.ppermute(value, "lon", east_pairs)

    device = route_device.reshape(blocks)
    grid_t, cot_t, out_t = grid_in.T, cotangent.T, w_out.T
    per_step = blocks // STEPS
    step_rows = per_step * tile_rows
    tiles_spec = pl.BlockSpec((per_step, tile_rows, tile_rows), lambda i: (i, 0, 0))
    cols_spec = pl.BlockSpec((channels, step_rows), lambda i: (0, i))
    pair_shape = (2, nodes, width)

    embed_other = swap_rep(w_embed)

    def encode(after, weight, limit):
        return call(
            encode_kernel, "encode",
            [smem(), smem(), anywhere(), cols_spec, tiles_spec, whole((channels, width))],
            [whole(pair_shape)] * 3 + [whole((my_rows, width))],
            [shape_of(pair_shape, BF16)] * 3 + [shape_of((my_rows, width), BF16)],
            2 * grid_rows * width * (channels + half), 3e6, grid=(STEPS,), exps=grid_rows * width,
            scratch=[
                pltpu.VMEM((6 * slots, half, width), F32),
                pltpu.VMEM((step_rows, width), BF16),
            ],
            limit=limit,
        )(device, route_slot, after, grid_t, interp_tiles, weight)

    own_a, even_a, odd_a, hidden_a = encode(w_embed, w_embed, VMEM_ALL)
    even_in_a, odd_in_a = to_even(even_a), to_odd(odd_a)

    back_own, back_east, back_side = call(
        back_kernel, "back_messages",
        [smem(), smem(), anywhere(), tiles_spec, cols_spec],
        [whole((nodes, padded)), whole((3, nodes, padded)), whole((2, nodes, padded))],
        [shape_of((nodes, padded), BF16), shape_of((3, nodes, padded), BF16),
         shape_of((2, nodes, padded), BF16)],
        2 * grid_rows * half * padded, 3e6, grid=(STEPS,),
        scratch=[pltpu.VMEM((6 * slots, half, padded), F32)],
    )(device, route_slot, odd_a, interp_tiles, cot_t)
    back_moved = to_east(back_east)

    own_b, even_b, odd_b, hidden_b = encode(back_own, embed_other, VMEM_BYTES)
    even_in_b, odd_in_b = to_even(even_b), to_odd(odd_b)

    out_other, up_other, down_other = swap_rep(out_t), swap_rep(w_up), swap_rep(w_down)
    embed_shape = (slots, 2, half, width)
    mesh_other = swap_rep(mesh_embed)

    base, local, local_other = call(
        local_kernel, "local_terms", [vmem()] * 5, [vmem()] * 3,
        [shape_of((channels, my_rows), F32)] + [shape_of((channels, width), F32)] * 2,
        4 * my_rows * latent * channels, 4e6,
    )(hidden_a, hidden_b, cot_t, out_t, out_other)

    second = pl.BlockSpec((1, nodes, width), lambda i: (1, 0, 0))

    def add_east(after, *terms):
        return call(
            add_kernel, "add_east", [anywhere()] + [second] * 3, whole((nodes, width)),
            shape_of((nodes, width), BF16), 3 * nodes * width, 6e5, grid=(1,),
        )(after, *terms)

    send_a = add_east(own_b, own_a, even_in_a, odd_in_a)
    moved_a = to_east(send_a)
    send_b = add_east(moved_a, own_b, even_in_b, odd_in_b)
    moved_b = to_east(send_b)

    back_even, back_odd = call(
        sides_kernel, "add_sides", [anywhere(), vmem(), vmem()], [vmem()] * 2,
        [shape_of((nodes, padded), BF16)] * 2, 3 * nodes * width, 1e6,
    )(send_b, back_side, back_moved)
    back_even_in, back_odd_in = to_even(back_even), to_odd(back_odd)

    first = pl.BlockSpec((1, nodes, width), lambda i: (0, 0, 0))
    sums_specs = [first] * 3 + [whole((nodes, width))]
    weights = (w_up, up_other, w_down, down_other, out_t, out_other)
    back_spec = whole((nodes, padded))
    proj, keep, give, mesh_keep, mesh_give = call(
        node_kernel, "node_update_and_gradients",
        sums_specs * 2 + [whole(embed_shape)] * 2
        + [back_spec, pl.BlockSpec((1, nodes, padded), lambda i: (0, 0, 0)), back_spec, back_spec]
        + [whole((channels, width))] * 2 + [whole(w.shape) for w in weights],
        [whole((nodes, padded))] + [whole((2 * latent, width))] * 2 + [whole((nodes, width))] * 2,
        [shape_of((nodes, padded), BF16), shape_of((2 * latent, width), F32),
         shape_of((2 * latent, width), BF16), shape_of((nodes, width), F32),
         shape_of((nodes, width), BF16)],
        15 * nodes * latent * latent, 9e6, grid=(1,), exps=nodes * latent,
    )(
        own_a, even_in_a, odd_in_a, moved_a, own_b, even_in_b, odd_in_b, moved_b,
        mesh_embed.reshape(embed_shape), mesh_other.reshape(embed_shape),
        back_own, back_moved, back_even_in, back_odd_in, local, local_other, *weights,
    )

    east = lax.ppermute(proj, "lon", west_pairs)
    pair = jnp.stack([proj, east])
    pair_even, pair_odd = to_even(pair), to_odd(pair)

    terms = call(
        terms_kernel, "sum_terms", [anywhere()] + [vmem()] * 2, vmem(),
        shape_of((2 * latent, width), BF16), 2 * latent * width, 2e6,
    )(pair, keep, swap_rep(give))
    mine, theirs = summed(terms)

    grad_mesh = call(
        place_kernel, "place_mesh", [vmem()] * 2, vmem(), shape_of(embed_shape, F32),
        nodes * latent, 1e6,
    )(mesh_keep, swap_rep(mesh_give)).reshape(mesh_embed.shape)

    tables = (pair, pair_even, pair_odd)
    table_shape = (2 * slots, half, padded)
    grid_out = call(
        decode_kernel, "decode", [smem(), smem()] + [vmem()] * 8, vmem(),
        shape_of((channels, my_rows), BF16), 2 * my_rows * tile_rows * padded, 4e6,
        scratch=[pltpu.VMEM((blocks // 2, tile_rows, padded), BF16)],
    )(
        device, route_slot, interp_tiles, base,
        *[table.reshape(table_shape) for table in tables],
        *[swap_rep(table).reshape(table_shape) for table in tables],
    ).T

    grad_up, grad_down, grad_out = call(
        finish_kernel, "finish", [vmem()] * 4, [vmem()] * 3,
        [shape_of((latent, width), F32), shape_of((width, latent), F32),
         shape_of((channels, width), F32)],
        2 * width * latent * channels, 1e6,
    )(mine, theirs, out_t, out_other)
    return (grid_out, grad_out.T, grad_up, grad_down, grad_mesh)


def solution(mesh):
    patch = ("groups", "lat", "lon")
    placed = (
        P(patch, None),
        P(None, "rep"),
        P(patch, None, None),
        P(patch, None),
        P(patch),
        P(patch, "rep"),
        P(None, "rep"),
        P("rep", None),
        P("rep", None),
        P(patch, None),
    )
    return jax.shard_map(
        per_device,
        mesh=mesh,
        in_specs=placed,
        out_specs=(
            P(("groups", "lat", "lon", "rep"), None),
            P(("groups", "rep"), None),
            P("groups", "rep"),
            P(("groups", "rep"), None),
            P(patch, "rep"),
        ),
        check_vma=False,
    )
```

```python
import jax
import jax.numpy as jnp
from jax import lax
from jax.experimental import pallas as pl
from jax.experimental.pallas import tpu as pltpu
from jax.sharding import PartitionSpec as P

F32 = jnp.float32
BF16 = jnp.bfloat16
VMEM_BYTES = 20 * 1024 * 1024
VMEM_ALL = 60 * 1024 * 1024
STEPS = 4
HALVING = 3


def dot(left, right):
    return jnp.dot(left, right, preferred_element_type=F32)


def dot_rows(left, right):
    return lax.dot_general(left, right, (((0,), (0,)), ((), ())), preferred_element_type=F32)


def dot_last(left, right):
    return lax.dot_general(left, right, (((1,), (1,)), ((), ())), preferred_element_type=F32)


def sigmoid(values):
    return 0.5 * jnp.tanh(0.5 * values) + 0.5


def vmem():
    return pl.BlockSpec(memory_space=pltpu.VMEM)


def smem():
    return pl.BlockSpec(memory_space=pltpu.SMEM)


def anywhere():
    return pl.BlockSpec(memory_space=pl.ANY)


def whole(shape):
    return pl.BlockSpec(shape, lambda i: (0,) * len(shape))


def shape_of(shape, dtype):
    return jax.ShapeDtypeStruct(shape, dtype)


def call(kernel, name, in_specs, out_specs, out_shape, flops, nbytes, grid=(), scratch=(), exps=0,
         limit=VMEM_BYTES, weight=1):
    return pl.pallas_call(
        kernel,
        grid=grid,
        in_specs=in_specs,
        out_specs=out_specs,
        out_shape=out_shape,
        scratch_shapes=list(scratch),
        compiler_params=pltpu.CompilerParams(vmem_limit_bytes=limit),
        cost_estimate=pl.CostEstimate(flops=int(weight), bytes_accessed=1, transcendentals=0),
        name=name,
    )


def node_half(tile, r):
    half = tile.shape[1] // 2
    return jnp.where(r == 0, tile[:, :half], tile[:, half:]).T


def entry_of(device_ref, slot_ref, b, slots):
    lon_count = lax.axis_size("lon")
    lat, lon = lax.axis_index("lat"), lax.axis_index("lon")
    target = device_ref[b]
    band = lax.div(target, lon_count)
    sector = target - band * lon_count - lon
    sector = jnp.where(sector < 0, sector + lon_count, sector)
    step = band - lat
    even_step = 1 - 2 * lax.rem(lat, 2)
    side = jnp.where(step == 0, 0, jnp.where(step == even_step, 1, 2))
    return (side * 2 + sector) * slots + slot_ref[b]


def write_packed(total, outs):
    per = total.shape[0] // 3
    for k, out in enumerate(outs):
        block = total[k * per : (k + 1) * per]
        out[...] = block.reshape(out.shape).astype(out.dtype)


def back_kernel(
    device_ref, slot_ref, tiles_ref, cot_ref, own_ref, east_ref, side_ref,
    total, tiles, cots, tile_sems, cot_sems,
):
    blocks, rows = tiles.shape[0], tiles.shape[1]
    count = blocks // STEPS
    slots = total.shape[0] // 6
    channels = cots.shape[0]
    r = lax.axis_index("rep")
    copies = []
    for k in range(STEPS):
        part = pl.ds(k * count, count)
        cols = pl.ds(k * count * rows, count * rows)
        copies.append((
            pltpu.make_async_copy(tiles_ref.at[part], tiles.at[part], tile_sems.at[k]),
            pltpu.make_async_copy(cot_ref.at[:, cols], cots.at[:, cols], cot_sems.at[k]),
        ))
        for copy in copies[-1]:
            copy.start()
    total[...] = jnp.zeros_like(total)
    for b in range(blocks):
        if b % count == 0:
            for copy in copies[b // count]:
                copy.wait()
        at = entry_of(device_ref, slot_ref, b, slots)
        cot = cots[:, b * rows : (b + 1) * rows]
        total[at, :, :channels] += dot_last(node_half(tiles[b], r), cot)
    for k, out in ((0, own_ref), (2, side_ref.at[0]), (4, side_ref.at[1])):
        out[...] = total[k * slots : (k + 1) * slots].reshape(out.shape).astype(out.dtype)
    for k in range(3):
        block = total[(2 * k + 1) * slots : (2 * k + 2) * slots]
        east_ref[k] = block.reshape(east_ref.shape[1:]).astype(east_ref.dtype)


def encode_kernel(
    device_ref, slot_ref, after_ref, grid_ref, tiles_ref, weight_ref,
    own_ref, even_ref, odd_ref, hidden_ref, total, hold,
):
    step = pl.program_id(0)
    count, rows = tiles_ref.shape[0], tiles_ref.shape[1]
    slots = total.shape[0] // 6
    r = lax.axis_index("rep")

    @pl.when(step == 0)
    def _():
        total[...] = jnp.zeros_like(total)

    preact = dot_rows(grid_ref[...], weight_ref[...])
    hold[...] = (preact * sigmoid(preact)).astype(BF16)
    for i in range(count):
        at = entry_of(device_ref, slot_ref, step * count + i, slots)
        total[at] += dot(node_half(tiles_ref[i], r), hold[i * rows : (i + 1) * rows, :])

    half_steps = pl.num_programs(0) // 2

    @pl.when(step // half_steps == r)
    def _():
        at = pl.multiple_of((step % half_steps) * hold.shape[0], hold.shape[0])
        hidden_ref[pl.ds(at, hold.shape[0]), :] = hold[...]

    @pl.when(step == pl.num_programs(0) - 1)
    def _():
        write_packed(total, (own_ref, even_ref, odd_ref))


def local_kernel(own_ref, oth_ref, cot_ref, out_ref, out_other_ref, base_ref, grad_ref, grad_other_ref):
    rows = own_ref.shape[0]
    r = lax.axis_index("rep")
    cot = cot_ref[:, pl.ds(pl.multiple_of(r * rows, rows), rows)]
    base_ref[...] = dot_last(out_ref[...], own_ref[...]) + dot_last(out_other_ref[...], oth_ref[...])
    grad_ref[...] = dot(cot, own_ref[...])
    grad_other_ref[...] = dot(cot, oth_ref[...])


def added(*values):
    total = values[0].astype(F32)
    for value in values[1:]:
        total = total + value.astype(F32)
    return total


def add_kernel(*refs):
    a, b, c, out = refs[-4:]
    out[...] = added(a[0], b[0], c[0]).astype(out.dtype)


def sides_kernel(after_ref, side_ref, moved_ref, even_ref, odd_ref):
    even_ref[...] = added(side_ref[0], moved_ref[1]).astype(even_ref.dtype)
    odd_ref[...] = added(side_ref[1], moved_ref[2]).astype(odd_ref.dtype)


def node_kernel(
    own_a, even_a, odd_a, moved_a, own_b, even_b, odd_b, moved_b, embed_ref, embed_other_ref,
    back_ref, back_moved_ref, back_even_ref, back_odd_ref, local_ref, local_other_ref,
    up_ref, up_other_ref, down_ref, down_other_ref, out_ref, out_other_ref,
    proj_ref, keep_ref, give_ref, mesh_keep_ref,
):
    r = lax.axis_index("rep")
    nodes, width = moved_a.shape
    latent = 2 * width
    channels = out_ref.shape[0]
    first = pl.multiple_of(r * width, width)
    second = pl.multiple_of((1 - r) * width, width)
    states = []
    for embed, parts in (
        (embed_ref, (own_a[0], even_a[0], odd_a[0], moved_a[...])),
        (embed_other_ref, (own_b[0], even_b[0], odd_b[0], moved_b[...])),
    ):
        start = embed[:, r].reshape(nodes, width)
        states.append((start.astype(F32) + added(*parts)).astype(BF16).astype(F32))
    state = jnp.concatenate(states, axis=1)
    centered = state - jnp.mean(state, axis=-1, keepdims=True)
    inverse = lax.rsqrt(jnp.mean(centered * centered, axis=-1, keepdims=True) + 1e-05)
    norm = centered * inverse
    normed = norm.astype(BF16)

    cot = added(back_ref[...], back_moved_ref[0], back_even_ref[...], back_odd_ref[...]).astype(BF16)
    terms = cot[:, :channels]
    grad_own = dot(terms, out_ref[...]).astype(BF16)
    grad_oth = dot(terms, out_other_ref[...]).astype(BF16)

    update_own = jnp.zeros((nodes, width), F32)
    update_oth = jnp.zeros((nodes, width), F32)
    back_own = jnp.zeros((nodes, width), F32)
    back_oth = jnp.zeros((nodes, width), F32)
    sides = ((up_ref, down_ref, keep_ref), (up_other_ref, down_other_ref, give_ref))
    for u_ref, d_ref, o_ref in sides:
        up_own, up_oth = u_ref[pl.ds(first, width), :], u_ref[pl.ds(second, width), :]
        down_own, down_oth = d_ref[:, pl.ds(first, width)], d_ref[:, pl.ds(second, width)]
        hidden = dot(normed[:, :width], up_own) + dot(normed[:, width:], up_oth)
        squash = sigmoid(hidden)
        act = (hidden * squash).astype(BF16)
        update_own += dot(act, down_own)
        update_oth += dot(act, down_oth)
        o_ref[latent : latent + width, :] = dot_rows(act, cot).astype(o_ref.dtype)
        act_grad = dot_last(grad_own, down_own) + dot_last(grad_oth, down_oth)
        pre_grad = (act_grad * squash * (1.0 + hidden * (1.0 - squash))).astype(BF16)
        o_ref[pl.ds(first, width), :] = dot_rows(normed[:, :width], pre_grad).astype(o_ref.dtype)
        o_ref[pl.ds(second, width), :] = dot_rows(normed[:, width:], pre_grad).astype(o_ref.dtype)
        back_own += dot_last(pre_grad, up_own)
        back_oth += dot_last(pre_grad, up_oth)

    mesh_own = (states[0] + update_own).astype(BF16)
    mesh_oth = (states[1] + update_oth).astype(BF16)
    proj = dot_last(mesh_own, out_ref[...]) + dot_last(mesh_oth, out_other_ref[...])
    proj_ref[...] = jnp.zeros_like(proj_ref)
    proj_ref[:, :channels] = proj.astype(BF16)
    ends = ((keep_ref, mesh_own, local_ref), (give_ref, mesh_oth, local_other_ref))
    start = latent + width
    for o_ref, mesh, local in ends:
        grad = dot_rows(cot, mesh)
        o_ref[start : 2 * latent, :] = grad.astype(o_ref.dtype)
        o_ref[start : start + channels, :] = (grad[:channels] + local[...]).astype(o_ref.dtype)

    back = jnp.concatenate([back_own, back_oth], axis=1)
    slope = (
        back - jnp.mean(back, axis=-1, keepdims=True)
        - norm * jnp.mean(back * norm, axis=-1, keepdims=True)
    ) * inverse
    mesh_keep_ref[...] = grad_own.astype(F32) + slope[:, :width]
    give_ref[2 * latent :, :] = (grad_oth.astype(F32) + slope[:, width:]).astype(give_ref.dtype)


def terms_kernel(keep_ref, mesh_keep_ref, got_ref, out_ref, mesh_ref):
    r = lax.axis_index("rep")
    rows = keep_ref.shape[0]
    part = mesh_ref.shape[:1] + mesh_ref.shape[2:]
    out_ref[...] = added(keep_ref[...], got_ref[:rows, :]).astype(out_ref.dtype)
    mesh_ref[:, r] = mesh_keep_ref[...].reshape(part)
    mesh_ref[:, 1 - r] = got_ref[rows:, :].astype(F32).reshape(part)


def first_sum_kernel(after_ref, terms_ref, got_ref, out_ref):
    rows = got_ref.shape[0]
    keep = terms_ref[pl.ds(pl.multiple_of(sum_bit(0) * rows, rows), rows), :]
    out_ref[...] = added(keep, got_ref[...]).astype(out_ref.dtype)


def pair_kernel(proj_ref, east_ref, pair_ref):
    pair_ref[0] = proj_ref[...]
    pair_ref[1] = east_ref[...]


def finish_kernel(mine_ref, other_ref, out_ref, out_other_ref, up_ref, down_ref, grad_ref):
    r = lax.axis_index("rep")
    bit = sum_bit(0)
    width = mine_ref.shape[1]
    channels = out_ref.shape[0]

    def place(low_ref, high_ref):
        up_ref[...] = low_ref[...].astype(F32)
        terms = high_ref[:width, :channels]
        down_ref[:, pl.ds(pl.multiple_of(r * width, width), width)] = dot(terms, out_ref[...])
        down_ref[:, pl.ds(pl.multiple_of((1 - r) * width, width), width)] = dot(
            terms, out_other_ref[...]
        )
        grad_ref[...] = high_ref[width : width + channels, :].astype(F32)

    @pl.when(bit == 0)
    def _():
        place(mine_ref, other_ref)

    @pl.when(bit != 0)
    def _():
        place(other_ref, mine_ref)


def decode_kernel(device_ref, slot_ref, tiles_ref, base_ref, *refs):
    mine, theirs, out_ref, picked = refs[:3], refs[3:6], refs[6], refs[7]
    r = lax.axis_index("rep")
    count, rows = tiles_ref.shape[0], tiles_ref.shape[1]
    half = rows // 2
    channels = out_ref.shape[0]
    blocks = count // 2
    per = mine[0].shape[0]
    for i in range(blocks):
        at = entry_of(device_ref, slot_ref, r * blocks + i, per // 2)
        for k in range(3):
            @pl.when(at // per == k)
            def _(k=k, i=i, at=at):
                where = at - k * per
                picked[i, pl.ds(pl.multiple_of(r * half, half), half), :] = mine[k][where]
                picked[i, pl.ds(pl.multiple_of((1 - r) * half, half), half), :] = theirs[k][where]
    for i in range(blocks):
        cols = slice(i * rows, (i + 1) * rows)
        decoded = dot_last(picked[i].T, tiles_ref[r * blocks + i])
        out_ref[:, cols] = (base_ref[:, cols] + decoded[:channels]).astype(out_ref.dtype)


def along(axis, count, partner):
    pairs = []
    for source in range(count):
        to = partner(source)
        pairs.append((source, to if 0 <= to < count else source))
    return lambda value: lax.ppermute(value, axis, pairs)


def distances(axis):
    found, distance = [], 1
    while distance < lax.axis_size(axis):
        found.append((axis, distance))
        distance *= 2
    return found


def sum_orders():
    lat, lon = distances("lat"), distances("lon")
    return (lon + lat, lat + lon)


def sum_bit(step):
    bits = [
        lax.rem(lax.div(lax.axis_index(axis), distance), 2)
        for axis, distance in (order[step] for order in sum_orders())
    ]
    return jnp.where(lax.axis_index("rep") == 0, bits[0], bits[1])


def sum_swap(value, step):
    lat_count, lon_count = lax.axis_size("lat"), lax.axis_size("lon")
    orders = sum_orders()
    pairs = []
    for lat in range(lat_count):
        for lon in range(lon_count):
            for rep in range(2):
                axis, distance = orders[rep][step]
                to = (lat ^ distance, lon) if axis == "lat" else (lat, lon ^ distance)
                number = lambda a, b: (a * lon_count + b) * 2 + rep
                pairs.append((number(lat, lon), number(*to)))
    return lax.ppermute(value, ("lat", "lon", "rep"), pairs)


def given_half(value, step):
    rows = value.shape[0] // 2
    return lax.dynamic_slice_in_dim(value, (1 - sum_bit(step)) * rows, rows, 0)


def summed(value):
    count = len(sum_orders()[0])
    halving = min(count - 1, HALVING)
    for step in range(1, count):
        if step >= halving:
            value = (value.astype(F32) + sum_swap(value, step).astype(F32)).astype(BF16)
            continue
        rows = value.shape[0] // 2
        keep = lax.dynamic_slice_in_dim(value, sum_bit(step) * rows, rows, 0)
        got = sum_swap(given_half(value, step), step)
        value = (keep.astype(F32) + got.astype(F32)).astype(BF16)
    for step in range(halving - 1, 0, -1):
        other = sum_swap(value, step)
        value = jnp.where(
            sum_bit(step) == 0,
            jnp.concatenate([value, other], axis=0),
            jnp.concatenate([other, value], axis=0),
        )
    return value, sum_swap(value, 0)


def per_device(
    grid_in, w_embed, interp_tiles, route_device, route_slot,
    mesh_embed, w_up, w_down, w_out, cotangent,
):
    lat_count, lon_count = lax.axis_size("lat"), lax.axis_size("lon")
    blocks, tile_rows = interp_tiles.shape[:2]
    grid_rows, channels = grid_in.shape
    my_rows = grid_rows // 2
    width = w_embed.shape[1]
    latent = 2 * width
    padded = -(-channels // 128) * 128
    slots = mesh_embed.shape[0] // tile_rows
    half = tile_rows // 2
    nodes = slots * half

    swap_rep = along("rep", 2, lambda i: 1 - i)
    to_even = along("lat", lat_count, lambda i: i ^ 1)
    to_odd = along("lat", lat_count, lambda i: ((i + 1) ^ 1) - 1)
    east_pairs = [(i, (i + 1) % lon_count) for i in range(lon_count)]
    west_pairs = [(j, i) for i, j in east_pairs]
    to_east = lambda value: lax.ppermute(value, "lon", east_pairs)

    device = route_device.reshape(blocks)
    grid_t, cot_t, out_t = grid_in.T, cotangent.T, w_out.T
    per_step = blocks // STEPS
    step_rows = per_step * tile_rows
    tiles_spec = pl.BlockSpec((per_step, tile_rows, tile_rows), lambda i: (i, 0, 0))
    cols_spec = pl.BlockSpec((channels, step_rows), lambda i: (0, i))
    pair_shape = (2, nodes, width)

    embed_other = swap_rep(w_embed)

    def encode(after, weight, limit):
        return call(
            encode_kernel, "encode",
            [smem(), smem(), anywhere(), cols_spec, tiles_spec, whole((channels, width))],
            [whole(pair_shape)] * 3 + [whole((my_rows, width))],
            [shape_of(pair_shape, BF16)] * 3 + [shape_of((my_rows, width), BF16)],
            2 * grid_rows * width * (channels + half), 3e6, grid=(STEPS,), exps=grid_rows * width,
            scratch=[
                pltpu.VMEM((6 * slots, half, width), F32),
                pltpu.VMEM((step_rows, width), BF16),
            ],
            limit=limit,
        )(device, route_slot, after, grid_t, interp_tiles, weight)

    back_own, back_east, back_side = call(
        back_kernel, "back_messages",
        [smem(), smem(), anywhere(), anywhere()],
        [vmem()] * 3,
        [shape_of((nodes, padded), BF16), shape_of((3, nodes, padded), BF16),
         shape_of((2, nodes, padded), BF16)],
        2 * grid_rows * half * padded, 3e6,
        scratch=[
            pltpu.VMEM((6 * slots, half, padded), F32),
            pltpu.VMEM(interp_tiles.shape, BF16),
            pltpu.VMEM(cot_t.shape, BF16),
            pltpu.SemaphoreType.DMA((STEPS,)),
            pltpu.SemaphoreType.DMA((STEPS,)),
        ],
        limit=VMEM_ALL,
    )(device, route_slot, interp_tiles, cot_t)
    back_moved = to_east(back_east)

    own_a, even_a, odd_a, hidden_a = encode(back_own, w_embed, VMEM_BYTES)
    even_in_a, odd_in_a = to_even(even_a), to_odd(odd_a)
    own_b, even_b, odd_b, hidden_b = encode(own_a, embed_other, VMEM_BYTES)
    even_in_b, odd_in_b = to_even(even_b), to_odd(odd_b)

    out_other, up_other, down_other = swap_rep(out_t), swap_rep(w_up), swap_rep(w_down)
    embed_shape = (slots, 2, half, width)
    mesh_other = swap_rep(mesh_embed)

    base, local, local_other = call(
        local_kernel, "local_terms", [vmem()] * 5, [vmem()] * 3,
        [shape_of((channels, my_rows), F32)] + [shape_of((channels, width), F32)] * 2,
        4 * my_rows * latent * channels, 4e6,
    )(hidden_a, hidden_b, cot_t, out_t, out_other)

    second = pl.BlockSpec((1, nodes, width), lambda i: (1, 0, 0))

    def add_east(after, *terms):
        return call(
            add_kernel, "add_east", [anywhere()] + [second] * 3, whole((nodes, width)),
            shape_of((nodes, width), BF16), 3 * nodes * width, 6e5, grid=(1,),
        )(after, *terms)

    send_a = add_east(back_moved, own_a, even_in_a, odd_in_a)
    moved_a = to_east(send_a)
    send_b = add_east(moved_a, own_b, even_in_b, odd_in_b)
    moved_b = to_east(send_b)

    back_even, back_odd = call(
        sides_kernel, "add_sides", [anywhere(), vmem(), vmem()], [vmem()] * 2,
        [shape_of((nodes, padded), BF16)] * 2, 3 * nodes * width, 1e6,
    )(send_b, back_side, back_moved)
    back_even_in, back_odd_in = to_even(back_even), to_odd(back_odd)

    first = pl.BlockSpec((1, nodes, width), lambda i: (0, 0, 0))
    sums_specs = [first] * 3 + [whole((nodes, width))]
    weights = (w_up, up_other, w_down, down_other, out_t, out_other)
    back_spec = whole((nodes, padded))
    proj, keep, give, mesh_keep = call(
        node_kernel, "node_update_and_gradients",
        sums_specs * 2 + [whole(embed_shape)] * 2
        + [back_spec, pl.BlockSpec((1, nodes, padded), lambda i: (0, 0, 0)), back_spec, back_spec]
        + [whole((channels, width))] * 2 + [whole(w.shape) for w in weights],
        [whole((nodes, padded)), whole((2 * latent, width)), whole((2 * latent + nodes, width)),
         whole((nodes, width))],
        [shape_of((nodes, padded), BF16), shape_of((2 * latent, width), F32),
         shape_of((2 * latent + nodes, width), BF16), shape_of((nodes, width), F32)],
        15 * nodes * latent * latent, 9e6, grid=(1,), exps=nodes * latent,
    )(
        own_a, even_in_a, odd_in_a, moved_a, own_b, even_in_b, odd_in_b, moved_b,
        mesh_embed.reshape(embed_shape), mesh_other.reshape(embed_shape),
        back_own, back_moved, back_even_in, back_odd_in, local, local_other, *weights,
    )

    east = lax.ppermute(proj, "lon", west_pairs)
    terms, grad_mesh = call(
        terms_kernel, "sum_terms", [vmem()] * 3, [vmem()] * 2,
        [shape_of((2 * latent, width), BF16), shape_of(embed_shape, F32)],
        2 * latent * width, 2e6,
    )(keep, mesh_keep, swap_rep(give))
    grad_mesh = grad_mesh.reshape(mesh_embed.shape)
    pair = call(
        pair_kernel, "pair_nodes", [vmem()] * 2, vmem(), shape_of((2, nodes, padded), BF16),
        1, 1, weight=5e9,
    )(proj, east)
    halved = call(
        first_sum_kernel, "first_sum", [anywhere()] + [vmem()] * 2, vmem(),
        shape_of((latent, width), BF16), 2 * latent * width, 1e6,
    )(pair, terms, sum_swap(given_half(terms, 0), 0))
    pair_even, pair_odd = to_even(pair), to_odd(pair)
    mine, theirs = summed(halved)

    tables = (pair, pair_even, pair_odd)
    table_shape = (2 * slots, half, padded)
    grid_out = call(
        decode_kernel, "decode", [smem(), smem()] + [vmem()] * 8, vmem(),
        shape_of((channels, my_rows), BF16), 2 * my_rows * tile_rows * padded, 4e6,
        scratch=[pltpu.VMEM((blocks // 2, tile_rows, padded), BF16)],
    )(
        device, route_slot, interp_tiles, base,
        *[table.reshape(table_shape) for table in tables],
        *[swap_rep(table).reshape(table_shape) for table in tables],
    ).T

    grad_up, grad_down, grad_out = call(
        finish_kernel, "finish", [vmem()] * 4, [vmem()] * 3,
        [shape_of((latent, width), F32), shape_of((width, latent), F32),
         shape_of((channels, width), F32)],
        2 * width * latent * channels, 1e6,
    )(mine, theirs, out_t, out_other)
    return (grid_out, grad_out.T, grad_up, grad_down, grad_mesh)


def solution(mesh):
    patch = ("groups", "lat", "lon")
    placed = (
        P(patch, None),
        P(None, "rep"),
        P(patch, None, None),
        P(patch, None),
        P(patch),
        P(patch, "rep"),
        P(None, "rep"),
        P("rep", None),
        P("rep", None),
        P(patch, None),
    )
    return jax.shard_map(
        per_device,
        mesh=mesh,
        in_specs=placed,
        out_specs=(
            P(("groups", "lat", "lon", "rep"), None),
            P(("groups", "rep"), None),
            P("groups", "rep"),
            P(("groups", "rep"), None),
            P(patch, "rep"),
        ),
        check_vma=False,
    )
```

```python
import jax
import jax.numpy as jnp
from jax import lax
from jax.experimental import pallas as pl
from jax.experimental.pallas import tpu as pltpu
from jax.sharding import PartitionSpec as P

F32 = jnp.float32
BF16 = jnp.bfloat16
VMEM_BYTES = 20 * 1024 * 1024
STEPS = 4
HALVING = 3


def dot(left, right):
    return jnp.dot(left, right, preferred_element_type=F32)


def dot_rows(left, right):
    return lax.dot_general(left, right, (((0,), (0,)), ((), ())), preferred_element_type=F32)


def dot_last(left, right):
    return lax.dot_general(left, right, (((1,), (1,)), ((), ())), preferred_element_type=F32)


def sigmoid(values):
    return 0.5 * jnp.tanh(0.5 * values) + 0.5


def vmem():
    return pl.BlockSpec(memory_space=pltpu.VMEM)


def smem():
    return pl.BlockSpec(memory_space=pltpu.SMEM)


def anywhere():
    return pl.BlockSpec(memory_space=pl.ANY)


def whole(shape):
    return pl.BlockSpec(shape, lambda i: (0,) * len(shape))


def shape_of(shape, dtype):
    return jax.ShapeDtypeStruct(shape, dtype)


def call(kernel, name, in_specs, out_specs, out_shape, flops, nbytes, grid=(), scratch=(), exps=0,
         limit=VMEM_BYTES, weight=1):
    return pl.pallas_call(
        kernel,
        grid=grid,
        in_specs=in_specs,
        out_specs=out_specs,
        out_shape=out_shape,
        scratch_shapes=list(scratch),
        compiler_params=pltpu.CompilerParams(vmem_limit_bytes=limit),
        cost_estimate=pl.CostEstimate(flops=int(weight), bytes_accessed=1, transcendentals=0),
        name=name,
    )


def node_half(tile, r):
    half = tile.shape[1] // 2
    return jnp.where(r == 0, tile[:, :half], tile[:, half:]).T


def entry_of(device_ref, slot_ref, b, slots):
    lon_count = lax.axis_size("lon")
    lat, lon = lax.axis_index("lat"), lax.axis_index("lon")
    target = device_ref[b]
    band = lax.div(target, lon_count)
    sector = target - band * lon_count - lon
    sector = jnp.where(sector < 0, sector + lon_count, sector)
    step = band - lat
    even_step = 1 - 2 * lax.rem(lat, 2)
    side = jnp.where(step == 0, 0, jnp.where(step == even_step, 1, 2))
    return (side * 2 + sector) * slots + slot_ref[b]


def write_packed(total, outs):
    per = total.shape[0] // 3
    for k, out in enumerate(outs):
        block = total[k * per : (k + 1) * per]
        out[...] = block.reshape(out.shape).astype(out.dtype)


def back_kernel(
    device_ref, slot_ref, tiles_ref, cot_ref, own_ref, east_ref, side_ref,
    total, tiles, cots, tile_sems, cot_sems,
):
    blocks, rows = tiles.shape[0], tiles.shape[1]
    count = blocks // STEPS
    slots = total.shape[0] // 6
    channels = cots.shape[0]
    r = lax.axis_index("rep")
    copies = []
    for k in range(STEPS):
        part = pl.ds(k * count, count)
        cols = pl.ds(k * count * rows, count * rows)
        copies.append((
            pltpu.make_async_copy(tiles_ref.at[part], tiles.at[part], tile_sems.at[k]),
            pltpu.make_async_copy(cot_ref.at[:, cols], cots.at[:, cols], cot_sems.at[k]),
        ))
        for copy in copies[-1]:
            copy.start()
    total[...] = jnp.zeros_like(total)
    for b in range(blocks):
        if b % count == 0:
            for copy in copies[b // count]:
                copy.wait()
        at = entry_of(device_ref, slot_ref, b, slots)
        cot = cots[:, b * rows : (b + 1) * rows]
        total[at, :, :channels] += dot_last(node_half(tiles[b], r), cot)
    for k, out in ((0, own_ref), (2, side_ref.at[0]), (4, side_ref.at[1])):
        out[...] = total[k * slots : (k + 1) * slots].reshape(out.shape).astype(out.dtype)
    for k in range(3):
        block = total[(2 * k + 1) * slots : (2 * k + 2) * slots]
        east_ref[k] = block.reshape(east_ref.shape[1:]).astype(east_ref.dtype)


def encode_kernel(
    device_ref, slot_ref, after_ref, grid_ref, tiles_ref, weight_ref,
    own_ref, even_ref, odd_ref, hidden_ref, total, hold,
):
    step = pl.program_id(0)
    count, rows = tiles_ref.shape[0], tiles_ref.shape[1]
    slots = total.shape[0] // 6
    r = lax.axis_index("rep")

    @pl.when(step == 0)
    def _():
        total[...] = jnp.zeros_like(total)

    preact = dot_rows(grid_ref[...], weight_ref[...])
    hold[...] = (preact * sigmoid(preact)).astype(BF16)
    for i in range(count):
        at = entry_of(device_ref, slot_ref, step * count + i, slots)
        total[at] += dot(node_half(tiles_ref[i], r), hold[i * rows : (i + 1) * rows, :])

    half_steps = pl.num_programs(0) // 2

    @pl.when(step // half_steps == r)
    def _():
        at = pl.multiple_of((step % half_steps) * hold.shape[0], hold.shape[0])
        hidden_ref[pl.ds(at, hold.shape[0]), :] = hold[...]

    @pl.when(step == pl.num_programs(0) - 1)
    def _():
        write_packed(total, (own_ref, even_ref, odd_ref))


def local_kernel(own_ref, oth_ref, cot_ref, out_ref, out_other_ref, base_ref, grad_ref, grad_other_ref):
    rows = own_ref.shape[0]
    r = lax.axis_index("rep")
    cot = cot_ref[:, pl.ds(pl.multiple_of(r * rows, rows), rows)]
    base_ref[...] = dot_last(out_ref[...], own_ref[...]) + dot_last(out_other_ref[...], oth_ref[...])
    grad_ref[...] = dot(cot, own_ref[...])
    grad_other_ref[...] = dot(cot, oth_ref[...])


def added(*values):
    total = values[0].astype(F32)
    for value in values[1:]:
        total = total + value.astype(F32)
    return total


def add_kernel(*refs):
    a, b, c, out = refs[-4:]
    out[...] = added(a[0], b[0], c[0]).astype(out.dtype)


def sides_kernel(after_ref, side_ref, moved_ref, even_ref, odd_ref):
    even_ref[...] = added(side_ref[0], moved_ref[1]).astype(even_ref.dtype)
    odd_ref[...] = added(side_ref[1], moved_ref[2]).astype(odd_ref.dtype)


def node_kernel(
    own_a, even_a, odd_a, moved_a, own_b, even_b, odd_b, moved_b, embed_ref, embed_other_ref,
    back_ref, back_moved_ref, back_even_ref, back_odd_ref, local_ref, local_other_ref,
    up_ref, up_other_ref, down_ref, down_other_ref, out_ref, out_other_ref,
    proj_ref, keep_ref, give_ref,
):
    r = lax.axis_index("rep")
    nodes, width = moved_a.shape
    latent = 2 * width
    channels = out_ref.shape[0]
    first = pl.multiple_of(r * width, width)
    second = pl.multiple_of((1 - r) * width, width)
    states = []
    for embed, parts in (
        (embed_ref, (own_a[0], even_a[0], odd_a[0], moved_a[...])),
        (embed_other_ref, (own_b[0], even_b[0], odd_b[0], moved_b[...])),
    ):
        start = embed[:, r].reshape(nodes, width)
        states.append((start.astype(F32) + added(*parts)).astype(BF16).astype(F32))
    state = jnp.concatenate(states, axis=1)
    centered = state - jnp.mean(state, axis=-1, keepdims=True)
    inverse = lax.rsqrt(jnp.mean(centered * centered, axis=-1, keepdims=True) + 1e-05)
    norm = centered * inverse
    normed = norm.astype(BF16)

    cot = added(back_ref[...], back_moved_ref[0], back_even_ref[...], back_odd_ref[...]).astype(BF16)
    terms = cot[:, :channels]
    grad_own = dot(terms, out_ref[...]).astype(BF16)
    grad_oth = dot(terms, out_other_ref[...]).astype(BF16)

    update_own = jnp.zeros((nodes, width), F32)
    update_oth = jnp.zeros((nodes, width), F32)
    back_own = jnp.zeros((nodes, width), F32)
    back_oth = jnp.zeros((nodes, width), F32)
    sides = ((up_ref, down_ref, keep_ref), (up_other_ref, down_other_ref, give_ref))
    for u_ref, d_ref, o_ref in sides:
        up_own, up_oth = u_ref[pl.ds(first, width), :], u_ref[pl.ds(second, width), :]
        down_own, down_oth = d_ref[:, pl.ds(first, width)], d_ref[:, pl.ds(second, width)]
        hidden = dot(normed[:, :width], up_own) + dot(normed[:, width:], up_oth)
        squash = sigmoid(hidden)
        act = (hidden * squash).astype(BF16)
        update_own += dot(act, down_own)
        update_oth += dot(act, down_oth)
        o_ref[latent : latent + width, :] = dot_rows(act, cot).astype(o_ref.dtype)
        act_grad = dot_last(grad_own, down_own) + dot_last(grad_oth, down_oth)
        pre_grad = (act_grad * squash * (1.0 + hidden * (1.0 - squash))).astype(BF16)
        o_ref[pl.ds(first, width), :] = dot_rows(normed[:, :width], pre_grad).astype(o_ref.dtype)
        o_ref[pl.ds(second, width), :] = dot_rows(normed[:, width:], pre_grad).astype(o_ref.dtype)
        back_own += dot_last(pre_grad, up_own)
        back_oth += dot_last(pre_grad, up_oth)

    mesh_own = (states[0] + update_own).astype(BF16)
    mesh_oth = (states[1] + update_oth).astype(BF16)
    proj = dot_last(mesh_own, out_ref[...]) + dot_last(mesh_oth, out_other_ref[...])
    proj_ref[...] = jnp.zeros_like(proj_ref)
    proj_ref[:, :channels] = proj.astype(BF16)
    ends = ((keep_ref, mesh_own, local_ref), (give_ref, mesh_oth, local_other_ref))
    start = latent + width
    for o_ref, mesh, local in ends:
        grad = dot_rows(cot, mesh)
        o_ref[start : 2 * latent, :] = grad.astype(o_ref.dtype)
        o_ref[start : start + channels, :] = (grad[:channels] + local[...]).astype(o_ref.dtype)

    back = jnp.concatenate([back_own, back_oth], axis=1)
    slope = (
        back - jnp.mean(back, axis=-1, keepdims=True)
        - norm * jnp.mean(back * norm, axis=-1, keepdims=True)
    ) * inverse
    keep_ref[2 * latent :, :] = grad_own.astype(F32) + slope[:, :width]
    give_ref[2 * latent :, :] = (grad_oth.astype(F32) + slope[:, width:]).astype(give_ref.dtype)


def terms_kernel(keep_ref, got_ref, out_ref, mesh_ref):
    r = lax.axis_index("rep")
    rows = out_ref.shape[0]
    part = mesh_ref.shape[:1] + mesh_ref.shape[2:]
    out_ref[...] = added(keep_ref[:rows, :], got_ref[:rows, :]).astype(out_ref.dtype)
    mesh_ref[:, r] = keep_ref[rows:, :].reshape(part)
    mesh_ref[:, 1 - r] = got_ref[rows:, :].astype(F32).reshape(part)


def first_sum_kernel(after_ref, terms_ref, got_ref, out_ref):
    rows = got_ref.shape[0]
    keep = terms_ref[pl.ds(pl.multiple_of(sum_bit(0) * rows, rows), rows), :]
    out_ref[...] = added(keep, got_ref[...]).astype(out_ref.dtype)


def pair_kernel(proj_ref, east_ref, pair_ref):
    pair_ref[0] = proj_ref[...]
    pair_ref[1] = east_ref[...]


def finish_kernel(mine_ref, other_ref, out_ref, out_other_ref, up_ref, down_ref, grad_ref):
    r = lax.axis_index("rep")
    bit = sum_bit(0)
    width = mine_ref.shape[1]
    channels = out_ref.shape[0]

    def place(low_ref, high_ref):
        up_ref[...] = low_ref[...].astype(F32)
        terms = high_ref[:width, :channels]
        down_ref[:, pl.ds(pl.multiple_of(r * width, width), width)] = dot(terms, out_ref[...])
        down_ref[:, pl.ds(pl.multiple_of((1 - r) * width, width), width)] = dot(
            terms, out_other_ref[...]
        )
        grad_ref[...] = high_ref[width : width + channels, :].astype(F32)

    @pl.when(bit == 0)
    def _():
        place(mine_ref, other_ref)

    @pl.when(bit != 0)
    def _():
        place(other_ref, mine_ref)


def pick_kernel(device_ref, slot_ref, pair_ref, even_ref, odd_ref, mine_ref, theirs_ref):
    r = lax.axis_index("rep")
    tables = (pair_ref, even_ref, odd_ref)
    blocks = mine_ref.shape[0]
    per = pair_ref.shape[0]
    for out_ref, first in ((mine_ref, r * blocks), (theirs_ref, (1 - r) * blocks)):
        for i in range(blocks):
            at = entry_of(device_ref, slot_ref, first + i, per // 2)
            for k, table in enumerate(tables):
                @pl.when(at // per == k)
                def _(k=k, i=i, at=at, table=table, out_ref=out_ref):
                    out_ref[i] = table[at - k * per]


def decode_kernel(tiles_ref, base_ref, mine_ref, got_ref, out_ref, picked):
    r = lax.axis_index("rep")
    blocks, half = mine_ref.shape[:2]
    rows = tiles_ref.shape[1]
    channels = out_ref.shape[0]
    own = pl.ds(pl.multiple_of(r * half, half), half)
    other = pl.ds(pl.multiple_of((1 - r) * half, half), half)
    for i in range(blocks):
        picked[i, own, :] = mine_ref[i]
        picked[i, other, :] = got_ref[i]
    for i in range(blocks):
        cols = slice(i * rows, (i + 1) * rows)
        decoded = dot_last(picked[i].T, tiles_ref[r * blocks + i])
        out_ref[:, cols] = (base_ref[:, cols] + decoded[:channels]).astype(out_ref.dtype)


def along(axis, count, partner):
    pairs = []
    for source in range(count):
        to = partner(source)
        pairs.append((source, to if 0 <= to < count else source))
    return lambda value: lax.ppermute(value, axis, pairs)


def distances(axis):
    found, distance = [], 1
    while distance < lax.axis_size(axis):
        found.append((axis, distance))
        distance *= 2
    return found


def sum_orders():
    lat, lon = distances("lat"), distances("lon")
    return (lon + lat, lat + lon)


def sum_bit(step):
    bits = [
        lax.rem(lax.div(lax.axis_index(axis), distance), 2)
        for axis, distance in (order[step] for order in sum_orders())
    ]
    return jnp.where(lax.axis_index("rep") == 0, bits[0], bits[1])


def sum_swap(value, step):
    lat_count, lon_count = lax.axis_size("lat"), lax.axis_size("lon")
    orders = sum_orders()
    pairs = []
    for lat in range(lat_count):
        for lon in range(lon_count):
            for rep in range(2):
                axis, distance = orders[rep][step]
                to = (lat ^ distance, lon) if axis == "lat" else (lat, lon ^ distance)
                number = lambda a, b: (a * lon_count + b) * 2 + rep
                pairs.append((number(lat, lon), number(*to)))
    return lax.ppermute(value, ("lat", "lon", "rep"), pairs)


def given_half(value, step):
    rows = value.shape[0] // 2
    return lax.dynamic_slice_in_dim(value, (1 - sum_bit(step)) * rows, rows, 0)


def summed(value):
    count = len(sum_orders()[0])
    halving = min(count - 1, HALVING)
    for step in range(1, count):
        if step >= halving:
            value = (value.astype(F32) + sum_swap(value, step).astype(F32)).astype(BF16)
            continue
        rows = value.shape[0] // 2
        keep = lax.dynamic_slice_in_dim(value, sum_bit(step) * rows, rows, 0)
        got = sum_swap(given_half(value, step), step)
        value = (keep.astype(F32) + got.astype(F32)).astype(BF16)
    for step in range(halving - 1, 0, -1):
        other = sum_swap(value, step)
        value = jnp.where(
            sum_bit(step) == 0,
            jnp.concatenate([value, other], axis=0),
            jnp.concatenate([other, value], axis=0),
        )
    return value, sum_swap(value, 0)


def per_device(
    grid_in, w_embed, interp_tiles, route_device, route_slot,
    mesh_embed, w_up, w_down, w_out, cotangent,
):
    lat_count, lon_count = lax.axis_size("lat"), lax.axis_size("lon")
    blocks, tile_rows = interp_tiles.shape[:2]
    grid_rows, channels = grid_in.shape
    my_rows = grid_rows // 2
    width = w_embed.shape[1]
    latent = 2 * width
    padded = -(-channels // 128) * 128
    slots = mesh_embed.shape[0] // tile_rows
    half = tile_rows // 2
    nodes = slots * half

    swap_rep = along("rep", 2, lambda i: 1 - i)
    to_even = along("lat", lat_count, lambda i: i ^ 1)
    to_odd = along("lat", lat_count, lambda i: ((i + 1) ^ 1) - 1)
    east_pairs = [(i, (i + 1) % lon_count) for i in range(lon_count)]
    west_pairs = [(j, i) for i, j in east_pairs]
    to_east = lambda value: lax.ppermute(value, "lon", east_pairs)

    in_hbm = lambda value: pltpu.with_memory_space_constraint(value, pltpu.HBM)
    device, slot = route_device.reshape(blocks), route_slot
    grid_t, cot_t, out_t = grid_in.T, cotangent.T, w_out.T
    routes = (in_hbm(device), in_hbm(slot))
    tiles_in, grid_in_t, cot_in_t = in_hbm(interp_tiles), in_hbm(grid_t), in_hbm(cot_t)
    per_step = blocks // STEPS
    step_rows = per_step * tile_rows
    tiles_spec = pl.BlockSpec((per_step, tile_rows, tile_rows), lambda i: (i, 0, 0))
    cols_spec = pl.BlockSpec((channels, step_rows), lambda i: (0, i))
    pair_shape = (2, nodes, width)

    embed_other = swap_rep(w_embed)

    def encode(after, weight, limit):
        return call(
            encode_kernel, "encode",
            [smem(), smem(), anywhere(), cols_spec, tiles_spec, whole((channels, width))],
            [whole(pair_shape)] * 3 + [whole((my_rows, width))],
            [shape_of(pair_shape, BF16)] * 3 + [shape_of((my_rows, width), BF16)],
            2 * grid_rows * width * (channels + half), 3e6, grid=(STEPS,), exps=grid_rows * width,
            scratch=[
                pltpu.VMEM((6 * slots, half, width), F32),
                pltpu.VMEM((step_rows, width), BF16),
            ],
            limit=limit,
        )(*routes, after, grid_in_t, tiles_in, weight)

    back_own, back_east, back_side = call(
        back_kernel, "back_messages",
        [smem(), smem(), anywhere(), anywhere()],
        [vmem()] * 3,
        [shape_of((nodes, padded), BF16), shape_of((3, nodes, padded), BF16),
         shape_of((2, nodes, padded), BF16)],
        2 * grid_rows * half * padded, 3e6,
        scratch=[
            pltpu.VMEM((6 * slots, half, padded), F32),
            pltpu.VMEM(interp_tiles.shape, BF16),
            pltpu.VMEM(cot_t.shape, BF16),
            pltpu.SemaphoreType.DMA((STEPS,)),
            pltpu.SemaphoreType.DMA((STEPS,)),
        ],
    )(*routes, tiles_in, cot_in_t)
    back_moved = to_east(back_east)

    own_a, even_a, odd_a, hidden_a = encode(back_own, in_hbm(w_embed), VMEM_BYTES)
    even_in_a, odd_in_a = to_even(even_a), to_odd(odd_a)
    own_b, even_b, odd_b, hidden_b = encode(own_a, embed_other, VMEM_BYTES)
    even_in_b, odd_in_b = to_even(even_b), to_odd(odd_b)

    out_other, up_other, down_other = swap_rep(out_t), swap_rep(w_up), swap_rep(w_down)
    embed_shape = (slots, 2, half, width)
    mesh_other = swap_rep(mesh_embed)

    base, local, local_other = call(
        local_kernel, "local_terms", [vmem()] * 5, [vmem()] * 3,
        [shape_of((channels, my_rows), F32)] + [shape_of((channels, width), F32)] * 2,
        4 * my_rows * latent * channels, 4e6,
    )(hidden_a, hidden_b, cot_t, out_t, out_other)

    second = pl.BlockSpec((1, nodes, width), lambda i: (1, 0, 0))

    def add_east(after, *terms):
        return call(
            add_kernel, "add_east", [anywhere()] + [second] * 3, whole((nodes, width)),
            shape_of((nodes, width), BF16), 3 * nodes * width, 6e5, grid=(1,),
        )(after, *terms)

    send_a = add_east(back_moved, own_a, even_in_a, odd_in_a)
    moved_a = to_east(send_a)
    send_b = add_east(moved_a, own_b, even_in_b, odd_in_b)
    moved_b = to_east(send_b)

    back_even, back_odd = call(
        sides_kernel, "add_sides", [anywhere(), vmem(), vmem()], [vmem()] * 2,
        [shape_of((nodes, padded), BF16)] * 2, 3 * nodes * width, 1e6,
    )(send_b, back_side, back_moved)
    back_even_in, back_odd_in = to_even(back_even), to_odd(back_odd)

    first = pl.BlockSpec((1, nodes, width), lambda i: (0, 0, 0))
    sums_specs = [first] * 3 + [whole((nodes, width))]
    weights = (w_up, up_other, w_down, down_other, out_t, out_other)
    back_spec = whole((nodes, padded))
    proj, keep, give = call(
        node_kernel, "node_update_and_gradients",
        sums_specs * 2 + [whole(embed_shape)] * 2
        + [back_spec, pl.BlockSpec((1, nodes, padded), lambda i: (0, 0, 0)), back_spec, back_spec]
        + [whole((channels, width))] * 2 + [whole(w.shape) for w in weights],
        [whole((nodes, padded))] + [whole((2 * latent + nodes, width))] * 2,
        [shape_of((nodes, padded), BF16), shape_of((2 * latent + nodes, width), F32),
         shape_of((2 * latent + nodes, width), BF16)],
        15 * nodes * latent * latent, 9e6, grid=(1,), exps=nodes * latent,
    )(
        own_a, even_in_a, odd_in_a, moved_a, own_b, even_in_b, odd_in_b, moved_b,
        mesh_embed.reshape(embed_shape), mesh_other.reshape(embed_shape),
        back_own, back_moved, back_even_in, back_odd_in, local, local_other, *weights,
    )

    east = lax.ppermute(proj, "lon", west_pairs)
    terms, grad_mesh = call(
        terms_kernel, "sum_terms", [vmem()] * 2, [vmem()] * 2,
        [shape_of((2 * latent, width), BF16), shape_of(embed_shape, F32)],
        2 * latent * width, 2e6,
    )(keep, swap_rep(give))
    grad_mesh = grad_mesh.reshape(mesh_embed.shape)
    pair = call(
        pair_kernel, "pair_nodes", [vmem()] * 2, vmem(), shape_of((2, nodes, padded), BF16),
        1, 1, weight=5e9,
    )(proj, east)
    halved = call(
        first_sum_kernel, "first_sum", [anywhere()] + [vmem()] * 2, vmem(),
        shape_of((latent, width), BF16), 2 * latent * width, 1e6,
    )(pair, terms, sum_swap(given_half(terms, 0), 0))
    pair_even, pair_odd = to_even(pair), to_odd(pair)
    mine, theirs = summed(halved)

    table_shape = (2 * slots, half, padded)
    mine_picked, theirs_picked = call(
        pick_kernel, "pick_nodes", [smem()] * 2 + [vmem()] * 3, [vmem()] * 2,
        [shape_of((blocks // 2, half, padded), BF16)] * 2, 1, 1, weight=5e9,
    )(device, slot, *[table.reshape(table_shape) for table in (pair, pair_even, pair_odd)])
    grid_out = call(
        decode_kernel, "decode", [vmem()] * 4, vmem(),
        shape_of((channels, my_rows), BF16), 2 * my_rows * tile_rows * padded, 4e6,
        scratch=[pltpu.VMEM((blocks // 2, tile_rows, padded), BF16)],
    )(interp_tiles, base, mine_picked, swap_rep(theirs_picked)).T

    grad_up, grad_down, grad_out = call(
        finish_kernel, "finish", [vmem()] * 4, [vmem()] * 3,
        [shape_of((latent, width), F32), shape_of((width, latent), F32),
         shape_of((channels, width), F32)],
        2 * width * latent * channels, 1e6,
    )(mine, theirs, out_t, out_other)
    return (grid_out, grad_out.T, grad_up, grad_down, grad_mesh)


def solution(mesh):
    patch = ("groups", "lat", "lon")
    placed = (
        P(patch, None),
        P(None, "rep"),
        P(patch, None, None),
        P(patch, None),
        P(patch),
        P(patch, "rep"),
        P(None, "rep"),
        P("rep", None),
        P("rep", None),
        P(patch, None),
    )
    return jax.shard_map(
        per_device,
        mesh=mesh,
        in_specs=placed,
        out_specs=(
            P(("groups", "lat", "lon", "rep"), None),
            P(("groups", "rep"), None),
            P("groups", "rep"),
            P(("groups", "rep"), None),
            P(patch, "rep"),
        ),
        check_vma=False,
    )
```

```python
import functools

import jax
import jax.numpy as jnp
from jax import lax
from jax.experimental import pallas as pl
from jax.experimental.pallas import tpu as pltpu
from jax.sharding import PartitionSpec as P

F32 = jnp.float32
BF16 = jnp.bfloat16
VMEM_BYTES = 20 * 1024 * 1024
STEPS = 4


def dot(left, right):
    return jnp.dot(left, right, preferred_element_type=F32)


def dot_rows(left, right):
    return lax.dot_general(left, right, (((0,), (0,)), ((), ())), preferred_element_type=F32)


def dot_last(left, right):
    return lax.dot_general(left, right, (((1,), (1,)), ((), ())), preferred_element_type=F32)


def sigmoid(values):
    return 0.5 * jnp.tanh(0.5 * values) + 0.5


def vmem():
    return pl.BlockSpec(memory_space=pltpu.VMEM)


def smem():
    return pl.BlockSpec(memory_space=pltpu.SMEM)


def anywhere():
    return pl.BlockSpec(memory_space=pl.ANY)


def whole(shape):
    return pl.BlockSpec(shape, lambda i: (0,) * len(shape))


def shape_of(shape, dtype):
    return jax.ShapeDtypeStruct(shape, dtype)


def call(kernel, name, in_specs, out_specs, out_shape, flops, nbytes, grid=(), scratch=(), exps=0,
         limit=VMEM_BYTES, weight=1):
    return pl.pallas_call(
        kernel,
        grid=grid,
        in_specs=in_specs,
        out_specs=out_specs,
        out_shape=out_shape,
        scratch_shapes=list(scratch),
        compiler_params=pltpu.CompilerParams(vmem_limit_bytes=limit),
        cost_estimate=pl.CostEstimate(flops=int(weight), bytes_accessed=1, transcendentals=0),
        name=name,
    )


def node_half(tile, r):
    half = tile.shape[1] // 2
    return jnp.where(r == 0, tile[:, :half], tile[:, half:]).T


def entry_of(device_ref, slot_ref, b, slots):
    lon_count = lax.axis_size("lon")
    lat, lon = lax.axis_index("lat"), lax.axis_index("lon")
    target = device_ref[b]
    band = lax.div(target, lon_count)
    sector = target - band * lon_count - lon
    sector = jnp.where(sector < 0, sector + lon_count, sector)
    step = band - lat
    even_step = 1 - 2 * lax.rem(lat, 2)
    side = jnp.where(step == 0, 0, jnp.where(step == even_step, 1, 2))
    return (side * 2 + sector) * slots + slot_ref[b]


def write_packed(total, outs):
    per = total.shape[0] // 3
    for k, out in enumerate(outs):
        block = total[k * per : (k + 1) * per]
        out[...] = block.reshape(out.shape).astype(out.dtype)


def chunk_copies(source_ref, target, sems, columns):
    copies = []
    for k in range(STEPS):
        size = target.shape[1 if columns else 0] // STEPS
        part = pl.ds(k * size, size)
        at = (slice(None), part) if columns else (part,)
        copies.append(pltpu.make_async_copy(source_ref.at[at], target.at[at], sems.at[k]))
    return copies


def started(groups, k):
    if k == 0:
        for group in groups:
            for copy in group[:2]:
                copy.start()
    elif k + 1 < STEPS:
        for group in groups:
            group[k + 1].start()


def waited(groups, k):
    for group in groups:
        group[k].wait()


def back_kernel(
    device_ref, slot_ref, tiles_ref, cot_ref, own_ref, east_ref, side_ref, total, cots, sems,
):
    blocks, rows = tiles_ref.shape[0], tiles_ref.shape[2]
    slots = total.shape[0] // 6
    channels = cots.shape[0]
    groups = [chunk_copies(cot_ref, cots, sems, True)]
    started(groups, 0)
    total[...] = jnp.zeros_like(total)
    for k in range(STEPS):
        if k > 0:
            started(groups, k)
        waited(groups, k)
        for b in range(k * blocks // STEPS, (k + 1) * blocks // STEPS):
            at = entry_of(device_ref, slot_ref, b, slots)
            cot = cots[:, b * rows : (b + 1) * rows]
            total[at, :, :channels] += dot_last(tiles_ref[b], cot)
    for k, out in ((0, own_ref), (2, side_ref.at[0]), (4, side_ref.at[1])):
        out[...] = total[k * slots : (k + 1) * slots].reshape(out.shape).astype(out.dtype)
    for k in range(3):
        block = total[(2 * k + 1) * slots : (2 * k + 2) * slots]
        east_ref[k] = block.reshape(east_ref.shape[1:]).astype(east_ref.dtype)


def encode_kernel(first, device_ref, slot_ref, after_ref, grid_ref, tiles_ref, weight_ref, *refs):
    outs, (total, grids, grid_sems), scratch = refs[:4], refs[4 + first : 7 + first], refs[7 + first :]
    own_ref, even_ref, odd_ref, hidden_ref = outs
    slots = total.shape[0] // 6
    r = lax.axis_index("rep")
    groups = [chunk_copies(grid_ref, grids, grid_sems, True)]
    if first:
        halves_ref, (tiles, tile_sems) = refs[4], scratch
        groups.append(chunk_copies(tiles_ref, tiles, tile_sems, False))
    else:
        halves_ref = tiles_ref
    blocks, _, rows = halves_ref.shape
    started(groups, 0)
    total[...] = jnp.zeros_like(total)
    weight = weight_ref[...].T
    cols = blocks * rows // STEPS
    for k in range(STEPS):
        if k > 0:
            started(groups, k)
        waited(groups, k)
        preact = dot(weight, grids[:, k * cols : (k + 1) * cols])
        hidden = (preact * sigmoid(preact)).astype(BF16)

        @pl.when(r == k // (STEPS // 2))
        def _(k=k, hidden=hidden):
            at = (k % (STEPS // 2)) * cols
            hidden_ref[:, at : at + cols] = hidden

        for i in range(blocks // STEPS):
            b = k * blocks // STEPS + i
            if first:
                halves_ref[b] = node_half(tiles[b], r)
            at = entry_of(device_ref, slot_ref, b, slots)
            total[at] += dot_last(halves_ref[b], hidden[:, i * rows : (i + 1) * rows])
    write_packed(total, (own_ref, even_ref, odd_ref))


def local_kernel(own_ref, oth_ref, cot_ref, out_ref, out_other_ref, base_ref, grad_ref, grad_other_ref):
    cols = own_ref.shape[1]
    r = lax.axis_index("rep")
    cot = cot_ref[:, pl.ds(pl.multiple_of(r * cols, cols), cols)]
    base_ref[...] = dot(out_ref[...], own_ref[...]) + dot(out_other_ref[...], oth_ref[...])
    grad_ref[...] = dot_last(cot, own_ref[...])
    grad_other_ref[...] = dot_last(cot, oth_ref[...])


def added(*values):
    total = values[0].astype(F32)
    for value in values[1:]:
        total = total + value.astype(F32)
    return total


def add_kernel(*refs):
    a, b, c, out = refs[-4:]
    out[...] = added(a[0], b[0], c[0]).astype(out.dtype)


def sides_kernel(after_ref, side_ref, moved_ref, even_ref, odd_ref):
    even_ref[...] = added(side_ref[0], moved_ref[1]).astype(even_ref.dtype)
    odd_ref[...] = added(side_ref[1], moved_ref[2]).astype(odd_ref.dtype)


def node_kernel(
    own_a, even_a, odd_a, moved_a, own_b, even_b, odd_b, moved_b, embed_ref, embed_other_ref,
    back_ref, back_moved_ref, back_even_ref, back_odd_ref, local_ref, local_other_ref,
    up_ref, up_other_ref, down_ref, down_other_ref, out_ref, out_other_ref,
    proj_ref, keep_ref, give_ref,
):
    r = lax.axis_index("rep")
    nodes, width = moved_a.shape
    latent = 2 * width
    channels = out_ref.shape[0]
    first = pl.multiple_of(r * width, width)
    second = pl.multiple_of((1 - r) * width, width)
    states = []
    for embed, parts in (
        (embed_ref, (own_a[0], even_a[0], odd_a[0], moved_a[...])),
        (embed_other_ref, (own_b[0], even_b[0], odd_b[0], moved_b[...])),
    ):
        start = embed[:, r].reshape(nodes, width)
        states.append((start.astype(F32) + added(*parts)).astype(BF16).astype(F32))
    state = jnp.concatenate(states, axis=1)
    centered = state - jnp.mean(state, axis=-1, keepdims=True)
    inverse = lax.rsqrt(jnp.mean(centered * centered, axis=-1, keepdims=True) + 1e-05)
    norm = centered * inverse
    normed = norm.astype(BF16)

    cot = added(back_ref[...], back_moved_ref[0], back_even_ref[...], back_odd_ref[...]).astype(BF16)
    terms = cot[:, :channels]
    grad_own = dot(terms, out_ref[...]).astype(BF16)
    grad_oth = dot(terms, out_other_ref[...]).astype(BF16)

    update_own = jnp.zeros((nodes, width), F32)
    update_oth = jnp.zeros((nodes, width), F32)
    back_own = jnp.zeros((nodes, width), F32)
    back_oth = jnp.zeros((nodes, width), F32)
    sides = ((up_ref, down_ref, keep_ref), (up_other_ref, down_other_ref, give_ref))
    for u_ref, d_ref, o_ref in sides:
        up_own, up_oth = u_ref[pl.ds(first, width), :], u_ref[pl.ds(second, width), :]
        down_own, down_oth = d_ref[:, pl.ds(first, width)], d_ref[:, pl.ds(second, width)]
        hidden = dot(normed[:, :width], up_own) + dot(normed[:, width:], up_oth)
        squash = sigmoid(hidden)
        act = (hidden * squash).astype(BF16)
        update_own += dot(act, down_own)
        update_oth += dot(act, down_oth)
        o_ref[latent : latent + width, :] = dot_rows(act, cot).astype(o_ref.dtype)
        act_grad = dot_last(grad_own, down_own) + dot_last(grad_oth, down_oth)
        pre_grad = (act_grad * squash * (1.0 + hidden * (1.0 - squash))).astype(BF16)
        o_ref[pl.ds(first, width), :] = dot_rows(normed[:, :width], pre_grad).astype(o_ref.dtype)
        o_ref[pl.ds(second, width), :] = dot_rows(normed[:, width:], pre_grad).astype(o_ref.dtype)
        back_own += dot_last(pre_grad, up_own)
        back_oth += dot_last(pre_grad, up_oth)

    mesh_own = (states[0] + update_own).astype(BF16)
    mesh_oth = (states[1] + update_oth).astype(BF16)
    proj = dot_last(mesh_own, out_ref[...]) + dot_last(mesh_oth, out_other_ref[...])
    proj_ref[...] = jnp.zeros_like(proj_ref)
    proj_ref[:, :channels] = proj.astype(BF16)
    ends = ((keep_ref, mesh_own, local_ref), (give_ref, mesh_oth, local_other_ref))
    start = latent + width
    for o_ref, mesh, local in ends:
        grad = dot_rows(cot, mesh)
        o_ref[start : 2 * latent, :] = grad.astype(o_ref.dtype)
        o_ref[start : start + channels, :] = (grad[:channels] + local[...]).astype(o_ref.dtype)

    back = jnp.concatenate([back_own, back_oth], axis=1)
    slope = (
        back - jnp.mean(back, axis=-1, keepdims=True)
        - norm * jnp.mean(back * norm, axis=-1, keepdims=True)
    ) * inverse
    keep_ref[2 * latent :, :] = grad_own.astype(F32) + slope[:, :width]
    give_ref[2 * latent :, :] = (grad_oth.astype(F32) + slope[:, width:]).astype(give_ref.dtype)


def terms_kernel(keep_ref, got_ref, out_ref, mesh_ref):
    r = lax.axis_index("rep")
    rows = out_ref.shape[0]
    part = mesh_ref.shape[:1] + mesh_ref.shape[2:]
    out_ref[...] = added(keep_ref[:rows, :], got_ref[:rows, :]).astype(out_ref.dtype)
    mesh_ref[:, r] = keep_ref[rows:, :].reshape(part)
    mesh_ref[:, 1 - r] = got_ref[rows:, :].astype(F32).reshape(part)


def first_sum_kernel(after_ref, terms_ref, got_ref, out_ref):
    rows = got_ref.shape[0]
    keep = terms_ref[pl.ds(pl.multiple_of(sum_bit(0) * rows, rows), rows), :]
    out_ref[...] = added(keep, got_ref[...]).astype(out_ref.dtype)


def second_sum_kernel(even_ref, odd_ref, value_ref, got_ref, out_ref):
    rows = got_ref.shape[0]
    keep = value_ref[pl.ds(pl.multiple_of(sum_bit(1) * rows, rows), rows), :]
    out_ref[...] = added(keep, got_ref[...]).astype(out_ref.dtype)


def pair_kernel(proj_ref, east_ref, pair_ref):
    pair_ref[0] = proj_ref[...]
    pair_ref[1] = east_ref[...]


def finish_kernel(mine_ref, other_ref, out_ref, out_other_ref, up_ref, down_ref, grad_ref):
    r = lax.axis_index("rep")
    bit = sum_bit(0)
    width = mine_ref.shape[1]
    channels = out_ref.shape[0]

    def place(low_ref, high_ref):
        up_ref[...] = low_ref[...].astype(F32)
        terms = high_ref[:width, :channels]
        down_ref[:, pl.ds(pl.multiple_of(r * width, width), width)] = dot(terms, out_ref[...])
        down_ref[:, pl.ds(pl.multiple_of((1 - r) * width, width), width)] = dot(
            terms, out_other_ref[...]
        )
        grad_ref[...] = high_ref[width : width + channels, :].astype(F32)

    @pl.when(bit == 0)
    def _():
        place(mine_ref, other_ref)

    @pl.when(bit != 0)
    def _():
        place(other_ref, mine_ref)


def pick_kernel(device_ref, slot_ref, pair_ref, even_ref, odd_ref, mine_ref, theirs_ref):
    r = lax.axis_index("rep")
    tables = (pair_ref, even_ref, odd_ref)
    blocks = mine_ref.shape[0]
    per = pair_ref.shape[0]
    for out_ref, first in ((mine_ref, r * blocks), (theirs_ref, (1 - r) * blocks)):
        for i in range(blocks):
            at = entry_of(device_ref, slot_ref, first + i, per // 2)
            for k, table in enumerate(tables):
                @pl.when(at // per == k)
                def _(k=k, i=i, at=at, table=table, out_ref=out_ref):
                    out_ref[i] = table[at - k * per]


def decode_kernel(tiles_ref, base_ref, mine_ref, got_ref, out_ref, picked):
    r = lax.axis_index("rep")
    blocks, half = mine_ref.shape[:2]
    rows = tiles_ref.shape[1]
    channels = out_ref.shape[0]
    own = pl.ds(pl.multiple_of(r * half, half), half)
    other = pl.ds(pl.multiple_of((1 - r) * half, half), half)
    for i in range(blocks):
        picked[i, own, :] = mine_ref[i]
        picked[i, other, :] = got_ref[i]
    for i in range(blocks):
        cols = slice(i * rows, (i + 1) * rows)
        decoded = dot_last(picked[i].T, tiles_ref[r * blocks + i])
        out_ref[:, cols] = (base_ref[:, cols] + decoded[:channels]).astype(out_ref.dtype)


def along(axis, count, partner):
    pairs = []
    for source in range(count):
        to = partner(source)
        pairs.append((source, to if 0 <= to < count else source))
    return lambda value: lax.ppermute(value, axis, pairs)


def distances(axis):
    found, distance = [], 1
    while distance < lax.axis_size(axis):
        found.append((axis, distance))
        distance *= 2
    return found


def sum_orders():
    lat, lon = distances("lat"), distances("lon")
    return (lon + lat, lat + lon)


def sum_bit(step):
    bits = [
        lax.rem(lax.div(lax.axis_index(axis), distance), 2)
        for axis, distance in (order[step] for order in sum_orders())
    ]
    return jnp.where(lax.axis_index("rep") == 0, bits[0], bits[1])


def sum_swap(value, step):
    lat_count, lon_count = lax.axis_size("lat"), lax.axis_size("lon")
    orders = sum_orders()
    pairs = []
    for lat in range(lat_count):
        for lon in range(lon_count):
            for rep in range(2):
                axis, distance = orders[rep][step]
                to = (lat ^ distance, lon) if axis == "lat" else (lat, lon ^ distance)
                number = lambda a, b: (a * lon_count + b) * 2 + rep
                pairs.append((number(lat, lon), number(*to)))
    return lax.ppermute(value, ("lat", "lon", "rep"), pairs)


def given_half(value, step):
    rows = value.shape[0] // 2
    return lax.dynamic_slice_in_dim(value, (1 - sum_bit(step)) * rows, rows, 0)


def summed(value):
    for step in range(2, len(sum_orders()[0])):
        value = (value.astype(F32) + sum_swap(value, step).astype(F32)).astype(BF16)
    other = sum_swap(value, 1)
    value = jnp.where(
        sum_bit(1) == 0,
        jnp.concatenate([value, other], axis=0),
        jnp.concatenate([other, value], axis=0),
    )
    return value, sum_swap(value, 0)


def per_device(
    grid_in, w_embed, interp_tiles, route_device, route_slot,
    mesh_embed, w_up, w_down, w_out, cotangent,
):
    lat_count, lon_count = lax.axis_size("lat"), lax.axis_size("lon")
    blocks, tile_rows = interp_tiles.shape[:2]
    grid_rows, channels = grid_in.shape
    my_rows = grid_rows // 2
    width = w_embed.shape[1]
    latent = 2 * width
    padded = -(-channels // 128) * 128
    slots = mesh_embed.shape[0] // tile_rows
    half = tile_rows // 2
    nodes = slots * half

    swap_rep = along("rep", 2, lambda i: 1 - i)
    to_even = along("lat", lat_count, lambda i: i ^ 1)
    to_odd = along("lat", lat_count, lambda i: ((i + 1) ^ 1) - 1)
    east_pairs = [(i, (i + 1) % lon_count) for i in range(lon_count)]
    west_pairs = [(j, i) for i, j in east_pairs]
    to_east = lambda value: lax.ppermute(value, "lon", east_pairs)

    in_hbm = lambda value: pltpu.with_memory_space_constraint(value, pltpu.HBM)
    device, slot = route_device.reshape(blocks), route_slot
    grid_t, cot_t, out_t = grid_in.T, cotangent.T, w_out.T
    routes = (in_hbm(device), in_hbm(slot))
    tiles_in, grid_in_t, cot_in_t = in_hbm(interp_tiles), in_hbm(grid_t), in_hbm(cot_t)
    pair_shape, halves_shape = (2, nodes, width), (blocks, half, tile_rows)
    total = pltpu.VMEM((6 * slots, half, width), F32)
    sems = pltpu.SemaphoreType.DMA((STEPS,))

    embed_other = swap_rep(w_embed)

    def encode(after, tiles, weight, first):
        shapes = [pair_shape] * 3 + [(width, my_rows)] + [halves_shape] * first
        return call(
            functools.partial(encode_kernel, first), "encode",
            [smem(), smem(), anywhere(), anywhere(), anywhere() if first else vmem(), vmem()],
            [vmem()] * len(shapes), [shape_of(shape, BF16) for shape in shapes], 1, 1,
            scratch=[total, pltpu.VMEM(grid_t.shape, BF16), sems]
            + [pltpu.VMEM(interp_tiles.shape, BF16), sems] * first,
        )(*routes, after, grid_in_t, tiles, weight)

    own_a, even_a, odd_a, hidden_a, halves = encode(w_embed, tiles_in, in_hbm(w_embed), True)
    even_in_a, odd_in_a = to_even(even_a), to_odd(odd_a)

    back_own, back_east, back_side = call(
        back_kernel, "back_messages",
        [smem(), smem(), vmem(), anywhere()],
        [vmem()] * 3,
        [shape_of((nodes, padded), BF16), shape_of((3, nodes, padded), BF16),
         shape_of((2, nodes, padded), BF16)],
        1, 1,
        scratch=[
            pltpu.VMEM((6 * slots, half, padded), F32), pltpu.VMEM(cot_t.shape, BF16), sems,
        ],
    )(*routes, halves, cot_in_t)
    back_moved = to_east(back_east)

    own_b, even_b, odd_b, hidden_b = encode(back_own, halves, embed_other, False)
    even_in_b, odd_in_b = to_even(even_b), to_odd(odd_b)

    out_other, up_other, down_other = swap_rep(out_t), swap_rep(w_up), swap_rep(w_down)
    embed_shape = (slots, 2, half, width)
    mesh_other = swap_rep(mesh_embed)

    base, local, local_other = call(
        local_kernel, "local_terms", [vmem()] * 5, [vmem()] * 3,
        [shape_of((channels, my_rows), F32)] + [shape_of((channels, width), F32)] * 2,
        4 * my_rows * latent * channels, 4e6,
    )(hidden_a, hidden_b, cot_t, out_t, out_other)

    second = pl.BlockSpec((1, nodes, width), lambda i: (1, 0, 0))

    def add_east(after, *terms):
        return call(
            add_kernel, "add_east", [anywhere()] + [second] * 3, whole((nodes, width)),
            shape_of((nodes, width), BF16), 3 * nodes * width, 6e5, grid=(1,),
        )(after, *terms)

    send_a = add_east(own_b, own_a, even_in_a, odd_in_a)
    moved_a = to_east(send_a)
    send_b = add_east(moved_a, own_b, even_in_b, odd_in_b)
    moved_b = to_east(send_b)

    back_even, back_odd = call(
        sides_kernel, "add_sides", [anywhere(), vmem(), vmem()], [vmem()] * 2,
        [shape_of((nodes, padded), BF16)] * 2, 3 * nodes * width, 1e6,
    )(send_b, back_side, back_moved)
    back_even_in, back_odd_in = to_even(back_even), to_odd(back_odd)

    first = pl.BlockSpec((1, nodes, width), lambda i: (0, 0, 0))
    sums_specs = [first] * 3 + [whole((nodes, width))]
    weights = (w_up, up_other, w_down, down_other, out_t, out_other)
    back_spec = whole((nodes, padded))
    proj, keep, give = call(
        node_kernel, "node_update_and_gradients",
        sums_specs * 2 + [whole(embed_shape)] * 2
        + [back_spec, pl.BlockSpec((1, nodes, padded), lambda i: (0, 0, 0)), back_spec, back_spec]
        + [whole((channels, width))] * 2 + [whole(w.shape) for w in weights],
        [whole((nodes, padded))] + [whole((2 * latent + nodes, width))] * 2,
        [shape_of((nodes, padded), BF16), shape_of((2 * latent + nodes, width), F32),
         shape_of((2 * latent + nodes, width), BF16)],
        15 * nodes * latent * latent, 9e6, grid=(1,), exps=nodes * latent,
    )(
        own_a, even_in_a, odd_in_a, moved_a, own_b, even_in_b, odd_in_b, moved_b,
        mesh_embed.reshape(embed_shape), mesh_other.reshape(embed_shape),
        back_own, back_moved, back_even_in, back_odd_in, local, local_other, *weights,
    )

    east = lax.ppermute(proj, "lon", west_pairs)
    terms, grad_mesh = call(
        terms_kernel, "sum_terms", [vmem()] * 2, [vmem()] * 2,
        [shape_of((2 * latent, width), BF16), shape_of(embed_shape, F32)],
        2 * latent * width, 2e6,
    )(keep, swap_rep(give))
    grad_mesh = grad_mesh.reshape(mesh_embed.shape)
    pair = call(
        pair_kernel, "pair_nodes", [vmem()] * 2, vmem(), shape_of((2, nodes, padded), BF16),
        1, 1, weight=5e9,
    )(proj, east)
    halved = call(
        first_sum_kernel, "first_sum", [anywhere()] + [vmem()] * 2, vmem(),
        shape_of((latent, width), BF16), 2 * latent * width, 1e6,
    )(pair, terms, sum_swap(given_half(terms, 0), 0))
    pair_even, pair_odd = to_even(pair), to_odd(pair)
    quarter = call(
        second_sum_kernel, "second_sum", [anywhere()] * 2 + [vmem()] * 2, vmem(),
        shape_of((width, width), BF16), 1, 1,
    )(pair_even, pair_odd, halved, sum_swap(given_half(halved, 1), 1))
    mine, theirs = summed(quarter)

    table_shape = (2 * slots, half, padded)
    mine_picked, theirs_picked = call(
        pick_kernel, "pick_nodes", [smem()] * 2 + [vmem()] * 3, [vmem()] * 2,
        [shape_of((blocks // 2, half, padded), BF16)] * 2, 1, 1, weight=5e9,
    )(device, slot, *[table.reshape(table_shape) for table in (pair, pair_even, pair_odd)])
    grid_out = call(
        decode_kernel, "decode", [vmem()] * 4, vmem(),
        shape_of((channels, my_rows), BF16), 2 * my_rows * tile_rows * padded, 4e6,
        scratch=[pltpu.VMEM((blocks // 2, tile_rows, padded), BF16)],
    )(interp_tiles, base, mine_picked, swap_rep(theirs_picked)).T

    grad_up, grad_down, grad_out = call(
        finish_kernel, "finish", [vmem()] * 4, [vmem()] * 3,
        [shape_of((latent, width), F32), shape_of((width, latent), F32),
         shape_of((channels, width), F32)],
        2 * width * latent * channels, 1e6,
    )(mine, theirs, out_t, out_other)
    return (grid_out, grad_out.T, grad_up, grad_down, grad_mesh)


def solution(mesh):
    patch = ("groups", "lat", "lon")
    placed = (
        P(patch, None),
        P(None, "rep"),
        P(patch, None, None),
        P(patch, None),
        P(patch),
        P(patch, "rep"),
        P(None, "rep"),
        P("rep", None),
        P("rep", None),
        P(patch, None),
    )
    return jax.shard_map(
        per_device,
        mesh=mesh,
        in_specs=placed,
        out_specs=(
            P(("groups", "lat", "lon", "rep"), None),
            P(("groups", "rep"), None),
            P("groups", "rep"),
            P(("groups", "rep"), None),
            P(patch, "rep"),
        ),
        check_vma=False,
    )
```

```python
import functools

import jax
import jax.numpy as jnp
from jax import lax
from jax.experimental import pallas as pl
from jax.experimental.pallas import tpu as pltpu
from jax.sharding import PartitionSpec as P

F32 = jnp.float32
BF16 = jnp.bfloat16
VMEM_BYTES = 20 * 1024 * 1024
STEPS = 4


def dot(left, right):
    return jnp.dot(left, right, preferred_element_type=F32)


def dot_rows(left, right):
    return lax.dot_general(left, right, (((0,), (0,)), ((), ())), preferred_element_type=F32)


def dot_last(left, right):
    return lax.dot_general(left, right, (((1,), (1,)), ((), ())), preferred_element_type=F32)


def sigmoid(values):
    return 0.5 * jnp.tanh(0.5 * values) + 0.5


def vmem():
    return pl.BlockSpec(memory_space=pltpu.VMEM)


def smem():
    return pl.BlockSpec(memory_space=pltpu.SMEM)


def anywhere():
    return pl.BlockSpec(memory_space=pl.ANY)


def whole(shape):
    return pl.BlockSpec(shape, lambda i: (0,) * len(shape))


def shape_of(shape, dtype):
    return jax.ShapeDtypeStruct(shape, dtype)


def call(kernel, name, in_specs, out_specs, out_shape, flops, nbytes, grid=(), scratch=(), exps=0,
         limit=VMEM_BYTES, weight=1):
    return pl.pallas_call(
        kernel,
        grid=grid,
        in_specs=in_specs,
        out_specs=out_specs,
        out_shape=out_shape,
        scratch_shapes=list(scratch),
        compiler_params=pltpu.CompilerParams(vmem_limit_bytes=limit),
        cost_estimate=pl.CostEstimate(flops=int(weight), bytes_accessed=1, transcendentals=0),
        name=name,
    )


def node_half(tile, r):
    half = tile.shape[1] // 2
    return jnp.where(r == 0, tile[:, :half], tile[:, half:]).T


def entry_of(device_ref, slot_ref, b, slots):
    lon_count = lax.axis_size("lon")
    lat, lon = lax.axis_index("lat"), lax.axis_index("lon")
    target = device_ref[b]
    band = lax.div(target, lon_count)
    sector = target - band * lon_count - lon
    sector = jnp.where(sector < 0, sector + lon_count, sector)
    step = band - lat
    even_step = 1 - 2 * lax.rem(lat, 2)
    side = jnp.where(step == 0, 0, jnp.where(step == even_step, 1, 2))
    return (side * 2 + sector) * slots + slot_ref[b]


def write_packed(total, outs):
    per = total.shape[0] // 3
    for k, out in enumerate(outs):
        block = total[k * per : (k + 1) * per]
        out[...] = block.reshape(out.shape).astype(out.dtype)


def back_kernel(
    device_ref, slot_ref, tiles_ref, cot_ref, own_ref, east_ref, side_ref,
    total, tiles, cots, tile_sems, cot_sems,
):
    blocks, rows = tiles.shape[0], tiles.shape[1]
    count = blocks // STEPS
    slots = total.shape[0] // 6
    channels = cots.shape[0]
    r = lax.axis_index("rep")
    copies = []
    for k in range(STEPS):
        part = pl.ds(k * count, count)
        cols = pl.ds(k * count * rows, count * rows)
        copies.append((
            pltpu.make_async_copy(tiles_ref.at[part], tiles.at[part], tile_sems.at[k]),
            pltpu.make_async_copy(cot_ref.at[:, cols], cots.at[:, cols], cot_sems.at[k]),
        ))
        for copy in copies[-1]:
            copy.start()
    total[...] = jnp.zeros_like(total)
    for b in range(blocks):
        if b % count == 0:
            for copy in copies[b // count]:
                copy.wait()
        at = entry_of(device_ref, slot_ref, b, slots)
        cot = cots[:, b * rows : (b + 1) * rows]
        total[at, :, :channels] += dot_last(node_half(tiles[b], r), cot)
    for k, out in ((0, own_ref), (2, side_ref.at[0]), (4, side_ref.at[1])):
        out[...] = total[k * slots : (k + 1) * slots].reshape(out.shape).astype(out.dtype)
    for k in range(3):
        block = total[(2 * k + 1) * slots : (2 * k + 2) * slots]
        east_ref[k] = block.reshape(east_ref.shape[1:]).astype(east_ref.dtype)


def encode_kernel(
    device_ref, slot_ref, after_ref, grid_ref, tiles_ref, weight_ref,
    own_ref, even_ref, odd_ref, hidden_ref, total, hold,
):
    blocks, rows = tiles_ref.shape[:2]
    slots = total.shape[0] // 6
    step_rows = blocks * rows // STEPS
    r = lax.axis_index("rep")
    total[...] = jnp.zeros_like(total)
    for k in range(STEPS):
        preact = dot_rows(grid_ref[:, k * step_rows : (k + 1) * step_rows], weight_ref[...])
        hold[k * step_rows : (k + 1) * step_rows, :] = (preact * sigmoid(preact)).astype(BF16)
        for b in range(k * blocks // STEPS, (k + 1) * blocks // STEPS):
            at = entry_of(device_ref, slot_ref, b, slots)
            total[at] += dot(node_half(tiles_ref[b], r), hold[b * rows : (b + 1) * rows, :])
    mine = hidden_ref.shape[0]
    hidden_ref[...] = hold[pl.ds(pl.multiple_of(r * mine, mine), mine), :]
    write_packed(total, (own_ref, even_ref, odd_ref))


def local_kernel(own_ref, oth_ref, cot_ref, out_ref, out_other_ref, base_ref, grad_ref, grad_other_ref):
    rows = own_ref.shape[0]
    r = lax.axis_index("rep")
    cot = cot_ref[:, pl.ds(pl.multiple_of(r * rows, rows), rows)]
    base_ref[...] = dot_last(out_ref[...], own_ref[...]) + dot_last(out_other_ref[...], oth_ref[...])
    grad_ref[...] = dot(cot, own_ref[...])
    grad_other_ref[...] = dot(cot, oth_ref[...])


def added(*values):
    total = values[0].astype(F32)
    for value in values[1:]:
        total = total + value.astype(F32)
    return total


def add_kernel(*refs):
    a, b, c, out = refs[-4:]
    out[...] = added(a[0], b[0], c[0]).astype(out.dtype)


def sides_kernel(after_ref, side_ref, moved_ref, even_ref, odd_ref):
    even_ref[...] = added(side_ref[0], moved_ref[1]).astype(even_ref.dtype)
    odd_ref[...] = added(side_ref[1], moved_ref[2]).astype(odd_ref.dtype)


def node_kernel(
    own_a, even_a, odd_a, moved_a, own_b, even_b, odd_b, moved_b, embed_ref, embed_other_ref,
    back_ref, back_moved_ref, back_even_ref, back_odd_ref, local_ref, local_other_ref,
    up_ref, up_other_ref, down_ref, down_other_ref, out_ref, out_other_ref,
    proj_ref, keep_ref, give_ref,
):
    r = lax.axis_index("rep")
    nodes, width = moved_a.shape
    latent = 2 * width
    channels = out_ref.shape[0]
    first = pl.multiple_of(r * width, width)
    second = pl.multiple_of((1 - r) * width, width)
    states = []
    for embed, parts in (
        (embed_ref, (own_a[0], even_a[0], odd_a[0], moved_a[...])),
        (embed_other_ref, (own_b[0], even_b[0], odd_b[0], moved_b[...])),
    ):
        start = embed[:, r].reshape(nodes, width)
        states.append((start.astype(F32) + added(*parts)).astype(BF16).astype(F32))
    state = jnp.concatenate(states, axis=1)
    centered = state - jnp.mean(state, axis=-1, keepdims=True)
    inverse = lax.rsqrt(jnp.mean(centered * centered, axis=-1, keepdims=True) + 1e-05)
    norm = centered * inverse
    normed = norm.astype(BF16)

    cot = added(back_ref[...], back_moved_ref[0], back_even_ref[...], back_odd_ref[...]).astype(BF16)
    terms = cot[:, :channels]
    grad_own = dot(terms, out_ref[...]).astype(BF16)
    grad_oth = dot(terms, out_other_ref[...]).astype(BF16)

    update_own = jnp.zeros((nodes, width), F32)
    update_oth = jnp.zeros((nodes, width), F32)
    back_own = jnp.zeros((nodes, width), F32)
    back_oth = jnp.zeros((nodes, width), F32)
    sides = ((up_ref, down_ref, keep_ref), (up_other_ref, down_other_ref, give_ref))
    for u_ref, d_ref, o_ref in sides:
        up_own, up_oth = u_ref[pl.ds(first, width), :], u_ref[pl.ds(second, width), :]
        down_own, down_oth = d_ref[:, pl.ds(first, width)], d_ref[:, pl.ds(second, width)]
        hidden = dot(normed[:, :width], up_own) + dot(normed[:, width:], up_oth)
        squash = sigmoid(hidden)
        act = (hidden * squash).astype(BF16)
        update_own += dot(act, down_own)
        update_oth += dot(act, down_oth)
        o_ref[latent : latent + width, :] = dot_rows(act, cot).astype(o_ref.dtype)
        act_grad = dot_last(grad_own, down_own) + dot_last(grad_oth, down_oth)
        pre_grad = (act_grad * squash * (1.0 + hidden * (1.0 - squash))).astype(BF16)
        o_ref[pl.ds(first, width), :] = dot_rows(normed[:, :width], pre_grad).astype(o_ref.dtype)
        o_ref[pl.ds(second, width), :] = dot_rows(normed[:, width:], pre_grad).astype(o_ref.dtype)
        back_own += dot_last(pre_grad, up_own)
        back_oth += dot_last(pre_grad, up_oth)

    mesh_own = (states[0] + update_own).astype(BF16)
    mesh_oth = (states[1] + update_oth).astype(BF16)
    proj = dot_last(mesh_own, out_ref[...]) + dot_last(mesh_oth, out_other_ref[...])
    proj_ref[...] = jnp.zeros_like(proj_ref)
    proj_ref[:, :channels] = proj.astype(BF16)
    ends = ((keep_ref, mesh_own, local_ref), (give_ref, mesh_oth, local_other_ref))
    start = latent + width
    for o_ref, mesh, local in ends:
        grad = dot_rows(cot, mesh)
        o_ref[start : 2 * latent, :] = grad.astype(o_ref.dtype)
        o_ref[start : start + channels, :] = (grad[:channels] + local[...]).astype(o_ref.dtype)

    back = jnp.concatenate([back_own, back_oth], axis=1)
    slope = (
        back - jnp.mean(back, axis=-1, keepdims=True)
        - norm * jnp.mean(back * norm, axis=-1, keepdims=True)
    ) * inverse
    keep_ref[2 * latent :, :] = grad_own.astype(F32) + slope[:, :width]
    give_ref[2 * latent :, :] = (grad_oth.astype(F32) + slope[:, width:]).astype(give_ref.dtype)


def terms_kernel(keep_ref, got_ref, out_ref, mesh_ref):
    r = lax.axis_index("rep")
    rows = out_ref.shape[0]
    part = mesh_ref.shape[:1] + mesh_ref.shape[2:]
    out_ref[...] = added(keep_ref[:rows, :], got_ref[:rows, :]).astype(out_ref.dtype)
    mesh_ref[:, r] = keep_ref[rows:, :].reshape(part)
    mesh_ref[:, 1 - r] = got_ref[rows:, :].astype(F32).reshape(part)


def first_sum_kernel(after_ref, terms_ref, got_ref, out_ref):
    rows = got_ref.shape[0]
    keep = terms_ref[pl.ds(pl.multiple_of(sum_bit(0) * rows, rows), rows), :]
    out_ref[...] = added(keep, got_ref[...]).astype(out_ref.dtype)


def second_sum_kernel(even_ref, odd_ref, value_ref, got_ref, out_ref):
    rows = got_ref.shape[0]
    keep = value_ref[pl.ds(pl.multiple_of(sum_bit(1) * rows, rows), rows), :]
    out_ref[...] = added(keep, got_ref[...]).astype(out_ref.dtype)


def pair_kernel(proj_ref, east_ref, pair_ref):
    pair_ref[0] = proj_ref[...]
    pair_ref[1] = east_ref[...]


def finish_kernel(mine_ref, other_ref, out_ref, out_other_ref, up_ref, down_ref, grad_ref):
    r = lax.axis_index("rep")
    bit = sum_bit(0)
    width = mine_ref.shape[1]
    channels = out_ref.shape[0]

    def place(low_ref, high_ref):
        up_ref[...] = low_ref[...].astype(F32)
        terms = high_ref[:width, :channels]
        down_ref[:, pl.ds(pl.multiple_of(r * width, width), width)] = dot(terms, out_ref[...])
        down_ref[:, pl.ds(pl.multiple_of((1 - r) * width, width), width)] = dot(
            terms, out_other_ref[...]
        )
        grad_ref[...] = high_ref[width : width + channels, :].astype(F32)

    @pl.when(bit == 0)
    def _():
        place(mine_ref, other_ref)

    @pl.when(bit != 0)
    def _():
        place(other_ref, mine_ref)


def pick_kernel(device_ref, slot_ref, pair_ref, even_ref, odd_ref, mine_ref, theirs_ref):
    r = lax.axis_index("rep")
    tables = (pair_ref, even_ref, odd_ref)
    blocks = mine_ref.shape[0]
    per = pair_ref.shape[0]
    for out_ref, first in ((mine_ref, r * blocks), (theirs_ref, (1 - r) * blocks)):
        for i in range(blocks):
            at = entry_of(device_ref, slot_ref, first + i, per // 2)
            for k, table in enumerate(tables):
                @pl.when(at // per == k)
                def _(k=k, i=i, at=at, table=table, out_ref=out_ref):
                    out_ref[i] = table[at - k * per]


def decode_kernel(tiles_ref, base_ref, mine_ref, got_ref, out_ref, picked):
    r = lax.axis_index("rep")
    blocks, half = mine_ref.shape[:2]
    rows = tiles_ref.shape[1]
    channels = out_ref.shape[0]
    own = pl.ds(pl.multiple_of(r * half, half), half)
    other = pl.ds(pl.multiple_of((1 - r) * half, half), half)
    for i in range(blocks):
        picked[i, own, :] = mine_ref[i]
        picked[i, other, :] = got_ref[i]
    for i in range(blocks):
        cols = slice(i * rows, (i + 1) * rows)
        decoded = dot_last(picked[i].T, tiles_ref[r * blocks + i])
        out_ref[:, cols] = (base_ref[:, cols] + decoded[:channels]).astype(out_ref.dtype)


def along(axis, count, partner):
    pairs = []
    for source in range(count):
        to = partner(source)
        pairs.append((source, to if 0 <= to < count else source))
    return lambda value: lax.ppermute(value, axis, pairs)


def distances(axis):
    found, distance = [], 1
    while distance < lax.axis_size(axis):
        found.append((axis, distance))
        distance *= 2
    return found


def sum_orders():
    lat, lon = distances("lat"), distances("lon")
    return (lon + lat, lat + lon)


def sum_bit(step):
    bits = [
        lax.rem(lax.div(lax.axis_index(axis), distance), 2)
        for axis, distance in (order[step] for order in sum_orders())
    ]
    return jnp.where(lax.axis_index("rep") == 0, bits[0], bits[1])


def sum_swap(value, step):
    lat_count, lon_count = lax.axis_size("lat"), lax.axis_size("lon")
    orders = sum_orders()
    pairs = []
    for lat in range(lat_count):
        for lon in range(lon_count):
            for rep in range(2):
                axis, distance = orders[rep][step]
                to = (lat ^ distance, lon) if axis == "lat" else (lat, lon ^ distance)
                number = lambda a, b: (a * lon_count + b) * 2 + rep
                pairs.append((number(lat, lon), number(*to)))
    return lax.ppermute(value, ("lat", "lon", "rep"), pairs)


def given_half(value, step):
    rows = value.shape[0] // 2
    return lax.dynamic_slice_in_dim(value, (1 - sum_bit(step)) * rows, rows, 0)


def summed(value):
    for step in range(2, len(sum_orders()[0])):
        value = (value.astype(F32) + sum_swap(value, step).astype(F32)).astype(BF16)
    other = sum_swap(value, 1)
    value = jnp.where(
        sum_bit(1) == 0,
        jnp.concatenate([value, other], axis=0),
        jnp.concatenate([other, value], axis=0),
    )
    return value, sum_swap(value, 0)


def per_device(
    grid_in, w_embed, interp_tiles, route_device, route_slot,
    mesh_embed, w_up, w_down, w_out, cotangent,
):
    lat_count, lon_count = lax.axis_size("lat"), lax.axis_size("lon")
    blocks, tile_rows = interp_tiles.shape[:2]
    grid_rows, channels = grid_in.shape
    my_rows = grid_rows // 2
    width = w_embed.shape[1]
    latent = 2 * width
    padded = -(-channels // 128) * 128
    slots = mesh_embed.shape[0] // tile_rows
    half = tile_rows // 2
    nodes = slots * half

    swap_rep = along("rep", 2, lambda i: 1 - i)
    to_even = along("lat", lat_count, lambda i: i ^ 1)
    to_odd = along("lat", lat_count, lambda i: ((i + 1) ^ 1) - 1)
    east_pairs = [(i, (i + 1) % lon_count) for i in range(lon_count)]
    west_pairs = [(j, i) for i, j in east_pairs]
    to_east = lambda value: lax.ppermute(value, "lon", east_pairs)

    in_hbm = lambda value: pltpu.with_memory_space_constraint(value, pltpu.HBM)
    in_vmem = lambda value: pltpu.with_memory_space_constraint(value, pltpu.VMEM)
    device, slot = route_device.reshape(blocks), route_slot
    grid_t, cot_t, out_t = grid_in.T, cotangent.T, w_out.T
    routes = (in_hbm(device), in_hbm(slot))
    tiles_in, grid_in_t, cot_in_t = in_hbm(interp_tiles), in_hbm(grid_t), in_hbm(cot_t)
    pair_shape = (2, nodes, width)
    embed_other = swap_rep(w_embed)

    back_own, back_east, back_side = call(
        back_kernel, "back_messages",
        [smem(), smem(), anywhere(), anywhere()],
        [vmem()] * 3,
        [shape_of((nodes, padded), BF16), shape_of((3, nodes, padded), BF16),
         shape_of((2, nodes, padded), BF16)],
        1, 1,
        scratch=[
            pltpu.VMEM((6 * slots, half, padded), F32),
            pltpu.VMEM(interp_tiles.shape, BF16),
            pltpu.VMEM(cot_t.shape, BF16),
            pltpu.SemaphoreType.DMA((STEPS,)),
            pltpu.SemaphoreType.DMA((STEPS,)),
        ],
    )(*routes, tiles_in, cot_in_t)
    back_moved = to_east(back_east)

    def encode(after, weight):
        return call(
            encode_kernel, "encode",
            [smem(), smem(), anywhere()] + [vmem()] * 3,
            [vmem()] * 4,
            [shape_of(pair_shape, BF16)] * 3 + [shape_of((my_rows, width), BF16)],
            1, 1,
            scratch=[
                pltpu.VMEM((6 * slots, half, width), F32), pltpu.VMEM((grid_rows, width), BF16),
            ],
        )(device, slot, after, grid_t, interp_tiles, weight)

    own_a, even_a, odd_a, hidden_a = encode(back_own, w_embed)
    even_in_a, odd_in_a = to_even(even_a), to_odd(odd_a)
    own_b, even_b, odd_b, hidden_b = encode(own_a, embed_other)
    even_in_b, odd_in_b = to_even(even_b), to_odd(odd_b)

    out_other, up_other, down_other = swap_rep(out_t), swap_rep(w_up), swap_rep(w_down)
    embed_shape = (slots, 2, half, width)
    mesh_other = swap_rep(mesh_embed)

    base, local, local_other = call(
        local_kernel, "local_terms", [vmem()] * 5, [vmem()] * 3,
        [shape_of((channels, my_rows), F32)] + [shape_of((channels, width), F32)] * 2,
        4 * my_rows * latent * channels, 4e6,
    )(hidden_a, hidden_b, cot_t, out_t, out_other)

    second = pl.BlockSpec((1, nodes, width), lambda i: (1, 0, 0))

    def add_east(after, *terms):
        return call(
            add_kernel, "add_east", [anywhere()] + [second] * 3, whole((nodes, width)),
            shape_of((nodes, width), BF16), 3 * nodes * width, 6e5, grid=(1,),
        )(after, *terms)

    send_a = add_east(back_moved, own_a, even_in_a, odd_in_a)
    moved_a = to_east(send_a)
    send_b = add_east(moved_a, own_b, even_in_b, odd_in_b)
    moved_b = to_east(send_b)

    back_even, back_odd = call(
        sides_kernel, "add_sides", [anywhere(), vmem(), vmem()], [vmem()] * 2,
        [shape_of((nodes, padded), BF16)] * 2, 3 * nodes * width, 1e6,
    )(send_b, back_side, back_moved)
    back_even_in, back_odd_in = to_even(back_even), to_odd(back_odd)

    first = pl.BlockSpec((1, nodes, width), lambda i: (0, 0, 0))
    sums_specs = [first] * 3 + [whole((nodes, width))]
    weights = (w_up, up_other, w_down, down_other, out_t, out_other)
    back_spec = whole((nodes, padded))
    proj, keep, give = call(
        node_kernel, "node_update_and_gradients",
        sums_specs * 2 + [whole(embed_shape)] * 2
        + [back_spec, pl.BlockSpec((1, nodes, padded), lambda i: (0, 0, 0)), back_spec, back_spec]
        + [whole((channels, width))] * 2 + [whole(w.shape) for w in weights],
        [whole((nodes, padded))] + [whole((2 * latent + nodes, width))] * 2,
        [shape_of((nodes, padded), BF16), shape_of((2 * latent + nodes, width), F32),
         shape_of((2 * latent + nodes, width), BF16)],
        15 * nodes * latent * latent, 9e6, grid=(1,), exps=nodes * latent,
    )(
        own_a, even_in_a, odd_in_a, moved_a, own_b, even_in_b, odd_in_b, moved_b,
        mesh_embed.reshape(embed_shape), mesh_other.reshape(embed_shape),
        back_own, back_moved, back_even_in, back_odd_in, local, local_other, *weights,
    )

    keep, give = in_vmem(keep), in_vmem(give)
    east = lax.ppermute(proj, "lon", west_pairs)
    terms, grad_mesh = call(
        terms_kernel, "sum_terms", [vmem()] * 2, [vmem()] * 2,
        [shape_of((2 * latent, width), BF16), shape_of(embed_shape, F32)],
        2 * latent * width, 2e6,
    )(keep, swap_rep(give))
    grad_mesh = grad_mesh.reshape(mesh_embed.shape)
    pair = call(
        pair_kernel, "pair_nodes", [vmem()] * 2, vmem(), shape_of((2, nodes, padded), BF16),
        1, 1, weight=5e9,
    )(proj, east)
    halved = call(
        first_sum_kernel, "first_sum", [anywhere()] + [vmem()] * 2, vmem(),
        shape_of((latent, width), BF16), 2 * latent * width, 1e6,
    )(pair, terms, sum_swap(given_half(terms, 0), 0))
    pair_even, pair_odd = to_even(pair), to_odd(pair)
    quarter = call(
        second_sum_kernel, "second_sum", [anywhere()] * 2 + [vmem()] * 2, vmem(),
        shape_of((width, width), BF16), 1, 1,
    )(pair_even, pair_odd, halved, sum_swap(given_half(halved, 1), 1))
    mine, theirs = summed(quarter)

    table_shape = (2 * slots, half, padded)
    mine_picked, theirs_picked = call(
        pick_kernel, "pick_nodes", [smem()] * 2 + [vmem()] * 3, [vmem()] * 2,
        [shape_of((blocks // 2, half, padded), BF16)] * 2, 1, 1, weight=5e9,
    )(device, slot, *[table.reshape(table_shape) for table in (pair, pair_even, pair_odd)])
    grid_out = call(
        decode_kernel, "decode", [vmem()] * 4, vmem(),
        shape_of((channels, my_rows), BF16), 2 * my_rows * tile_rows * padded, 4e6,
        scratch=[pltpu.VMEM((blocks // 2, tile_rows, padded), BF16)],
    )(interp_tiles, base, mine_picked, swap_rep(theirs_picked)).T

    grad_up, grad_down, grad_out = call(
        finish_kernel, "finish", [vmem()] * 4, [vmem()] * 3,
        [shape_of((latent, width), F32), shape_of((width, latent), F32),
         shape_of((channels, width), F32)],
        2 * width * latent * channels, 1e6,
    )(mine, theirs, out_t, out_other)
    return (grid_out, grad_out.T, grad_up, grad_down, grad_mesh)


def solution(mesh):
    patch = ("groups", "lat", "lon")
    placed = (
        P(patch, None),
        P(None, "rep"),
        P(patch, None, None),
        P(patch, None),
        P(patch),
        P(patch, "rep"),
        P(None, "rep"),
        P("rep", None),
        P("rep", None),
        P(patch, None),
    )
    return jax.shard_map(
        per_device,
        mesh=mesh,
        in_specs=placed,
        out_specs=(
            P(("groups", "lat", "lon", "rep"), None),
            P(("groups", "rep"), None),
            P("groups", "rep"),
            P(("groups", "rep"), None),
            P(patch, "rep"),
        ),
        check_vma=False,
    )
```

```python
import functools

import jax
import jax.numpy as jnp
from jax import lax
from jax.experimental import pallas as pl
from jax.experimental.pallas import tpu as pltpu
from jax.sharding import PartitionSpec as P

F32 = jnp.float32
BF16 = jnp.bfloat16
VMEM_BYTES = 20 * 1024 * 1024
STEPS = 4


def dot(left, right):
    return jnp.dot(left, right, preferred_element_type=F32)


def dot_rows(left, right):
    return lax.dot_general(left, right, (((0,), (0,)), ((), ())), preferred_element_type=F32)


def dot_last(left, right):
    return lax.dot_general(left, right, (((1,), (1,)), ((), ())), preferred_element_type=F32)


def sigmoid(values):
    return 0.5 * jnp.tanh(0.5 * values) + 0.5


def vmem():
    return pl.BlockSpec(memory_space=pltpu.VMEM)


def smem():
    return pl.BlockSpec(memory_space=pltpu.SMEM)


def anywhere():
    return pl.BlockSpec(memory_space=pl.ANY)


def whole(shape):
    return pl.BlockSpec(shape, lambda i: (0,) * len(shape))


def shape_of(shape, dtype):
    return jax.ShapeDtypeStruct(shape, dtype)


def call(kernel, name, in_specs, out_specs, out_shape, flops, nbytes, grid=(), scratch=(), exps=0,
         limit=VMEM_BYTES, weight=1):
    return pl.pallas_call(
        kernel,
        grid=grid,
        in_specs=in_specs,
        out_specs=out_specs,
        out_shape=out_shape,
        scratch_shapes=list(scratch),
        compiler_params=pltpu.CompilerParams(vmem_limit_bytes=limit),
        cost_estimate=pl.CostEstimate(flops=int(weight), bytes_accessed=1, transcendentals=0),
        name=name,
    )


def node_half(tile, r):
    half = tile.shape[1] // 2
    return jnp.where(r == 0, tile[:, :half], tile[:, half:]).T


def entry_of(device_ref, slot_ref, b, slots):
    lon_count = lax.axis_size("lon")
    lat, lon = lax.axis_index("lat"), lax.axis_index("lon")
    target = device_ref[b]
    band = lax.div(target, lon_count)
    sector = target - band * lon_count - lon
    sector = jnp.where(sector < 0, sector + lon_count, sector)
    step = band - lat
    even_step = 1 - 2 * lax.rem(lat, 2)
    side = jnp.where(step == 0, 0, jnp.where(step == even_step, 1, 2))
    return (side * 2 + sector) * slots + slot_ref[b]


def write_packed(total, outs):
    per = total.shape[0] // 3
    for k, out in enumerate(outs):
        block = total[k * per : (k + 1) * per]
        out[...] = block.reshape(out.shape).astype(out.dtype)


def back_kernel(
    device_ref, slot_ref, tiles_ref, cot_ref, own_ref, east_ref, side_ref,
    total, tiles, cots, tile_sems, cot_sems,
):
    blocks, rows = tiles.shape[0], tiles.shape[1]
    count = blocks // STEPS
    slots = total.shape[0] // 6
    channels = cots.shape[0]
    r = lax.axis_index("rep")
    copies = []
    for k in range(STEPS):
        part = pl.ds(k * count, count)
        cols = pl.ds(k * count * rows, count * rows)
        copies.append((
            pltpu.make_async_copy(tiles_ref.at[part], tiles.at[part], tile_sems.at[k]),
            pltpu.make_async_copy(cot_ref.at[:, cols], cots.at[:, cols], cot_sems.at[k]),
        ))
        for copy in copies[-1]:
            copy.start()
    total[...] = jnp.zeros_like(total)
    for b in range(blocks):
        if b % count == 0:
            for copy in copies[b // count]:
                copy.wait()
        at = entry_of(device_ref, slot_ref, b, slots)
        cot = cots[:, b * rows : (b + 1) * rows]
        total[at, :, :channels] += dot_last(node_half(tiles[b], r), cot)
    for k, out in ((0, own_ref), (2, side_ref.at[0]), (4, side_ref.at[1])):
        out[...] = total[k * slots : (k + 1) * slots].reshape(out.shape).astype(out.dtype)
    for k in range(3):
        block = total[(2 * k + 1) * slots : (2 * k + 2) * slots]
        east_ref[k] = block.reshape(east_ref.shape[1:]).astype(east_ref.dtype)


def encode_kernel(
    device_ref, slot_ref, after_ref, grid_ref, tiles_ref, weight_ref,
    own_ref, even_ref, odd_ref, hidden_ref, total, hold,
):
    blocks, rows = tiles_ref.shape[:2]
    slots = total.shape[0] // 6
    step_rows = blocks * rows // STEPS
    r = lax.axis_index("rep")
    total[...] = jnp.zeros_like(total)
    for k in range(STEPS):
        preact = dot_rows(grid_ref[:, k * step_rows : (k + 1) * step_rows], weight_ref[...])
        hold[k * step_rows : (k + 1) * step_rows, :] = (preact * sigmoid(preact)).astype(BF16)
        for b in range(k * blocks // STEPS, (k + 1) * blocks // STEPS):
            at = entry_of(device_ref, slot_ref, b, slots)
            total[at] += dot(node_half(tiles_ref[b], r), hold[b * rows : (b + 1) * rows, :])
    mine = hidden_ref.shape[0]
    hidden_ref[...] = hold[pl.ds(pl.multiple_of(r * mine, mine), mine), :]
    write_packed(total, (own_ref, even_ref, odd_ref))


def local_kernel(own_ref, oth_ref, cot_ref, out_ref, out_other_ref, base_ref, grad_ref, grad_other_ref):
    rows = own_ref.shape[0]
    r = lax.axis_index("rep")
    cot = cot_ref[:, pl.ds(pl.multiple_of(r * rows, rows), rows)]
    base_ref[...] = dot_last(out_ref[...], own_ref[...]) + dot_last(out_other_ref[...], oth_ref[...])
    grad_ref[...] = dot(cot, own_ref[...])
    grad_other_ref[...] = dot(cot, oth_ref[...])


def added(*values):
    total = values[0].astype(F32)
    for value in values[1:]:
        total = total + value.astype(F32)
    return total


def add_kernel(*refs):
    a, b, c, out = refs[-4:]
    out[...] = added(a[0], b[0], c[0]).astype(out.dtype)


def sides_kernel(after_ref, side_ref, moved_ref, even_ref, odd_ref):
    even_ref[...] = added(side_ref[0], moved_ref[1]).astype(even_ref.dtype)
    odd_ref[...] = added(side_ref[1], moved_ref[2]).astype(odd_ref.dtype)


def node_kernel(
    own_a, even_a, odd_a, moved_a, own_b, even_b, odd_b, moved_b, embed_ref, embed_other_ref,
    back_ref, back_moved_ref, back_even_ref, back_odd_ref, local_ref, local_other_ref,
    up_ref, up_other_ref, down_ref, down_other_ref, out_ref, out_other_ref,
    proj_ref, keep_ref, give_ref, mesh_give_ref, mesh_ref, mesh_half, mesh_sem,
):
    r = lax.axis_index("rep")
    nodes, width = moved_a.shape
    latent = 2 * width
    channels = out_ref.shape[0]
    first = pl.multiple_of(r * width, width)
    second = pl.multiple_of((1 - r) * width, width)
    states = []
    for embed, parts in (
        (embed_ref, (own_a[0], even_a[0], odd_a[0], moved_a[...])),
        (embed_other_ref, (own_b[0], even_b[0], odd_b[0], moved_b[...])),
    ):
        start = embed[:, r].reshape(nodes, width)
        states.append((start.astype(F32) + added(*parts)).astype(BF16).astype(F32))
    state = jnp.concatenate(states, axis=1)
    centered = state - jnp.mean(state, axis=-1, keepdims=True)
    inverse = lax.rsqrt(jnp.mean(centered * centered, axis=-1, keepdims=True) + 1e-05)
    norm = centered * inverse
    normed = norm.astype(BF16)

    cot = added(back_ref[...], back_moved_ref[0], back_even_ref[...], back_odd_ref[...]).astype(BF16)
    terms = cot[:, :channels]
    grad_own = dot(terms, out_ref[...]).astype(BF16)
    grad_oth = dot(terms, out_other_ref[...]).astype(BF16)

    update_own = jnp.zeros((nodes, width), F32)
    update_oth = jnp.zeros((nodes, width), F32)
    back_own = jnp.zeros((nodes, width), F32)
    back_oth = jnp.zeros((nodes, width), F32)
    sides = ((up_ref, down_ref, keep_ref), (up_other_ref, down_other_ref, give_ref))
    for u_ref, d_ref, o_ref in sides:
        up_own, up_oth = u_ref[pl.ds(first, width), :], u_ref[pl.ds(second, width), :]
        down_own, down_oth = d_ref[:, pl.ds(first, width)], d_ref[:, pl.ds(second, width)]
        hidden = dot(normed[:, :width], up_own) + dot(normed[:, width:], up_oth)
        squash = sigmoid(hidden)
        act = (hidden * squash).astype(BF16)
        update_own += dot(act, down_own)
        update_oth += dot(act, down_oth)
        o_ref[latent : latent + width, :] = dot_rows(act, cot).astype(o_ref.dtype)
        act_grad = dot_last(grad_own, down_own) + dot_last(grad_oth, down_oth)
        pre_grad = (act_grad * squash * (1.0 + hidden * (1.0 - squash))).astype(BF16)
        o_ref[pl.ds(first, width), :] = dot_rows(normed[:, :width], pre_grad).astype(o_ref.dtype)
        o_ref[pl.ds(second, width), :] = dot_rows(normed[:, width:], pre_grad).astype(o_ref.dtype)
        back_own += dot_last(pre_grad, up_own)
        back_oth += dot_last(pre_grad, up_oth)

    mesh_own = (states[0] + update_own).astype(BF16)
    mesh_oth = (states[1] + update_oth).astype(BF16)
    proj = dot_last(mesh_own, out_ref[...]) + dot_last(mesh_oth, out_other_ref[...])
    proj_ref[...] = jnp.zeros_like(proj_ref)
    proj_ref[:, :channels] = proj.astype(BF16)
    ends = ((keep_ref, mesh_own, local_ref), (give_ref, mesh_oth, local_other_ref))
    start = latent + width
    for o_ref, mesh, local in ends:
        grad = dot_rows(cot, mesh)
        o_ref[start : 2 * latent, :] = grad.astype(o_ref.dtype)
        o_ref[start : start + channels, :] = (grad[:channels] + local[...]).astype(o_ref.dtype)

    back = jnp.concatenate([back_own, back_oth], axis=1)
    slope = (
        back - jnp.mean(back, axis=-1, keepdims=True)
        - norm * jnp.mean(back * norm, axis=-1, keepdims=True)
    ) * inverse
    mesh_half[...] = (grad_own.astype(F32) + slope[:, :width]).reshape(mesh_half.shape)
    mesh_give_ref[...] = (grad_oth.astype(F32) + slope[:, width:]).astype(mesh_give_ref.dtype)
    copy = pltpu.make_async_copy(mesh_half, mesh_ref.at[:, r], mesh_sem)
    copy.start()
    copy.wait()


def place_kernel(got_ref, filled_ref, mesh_ref, mesh_half, mesh_sem):
    r = lax.axis_index("rep")
    mesh_half[...] = got_ref[...].astype(F32).reshape(mesh_half.shape)
    copy = pltpu.make_async_copy(mesh_half, mesh_ref.at[:, 1 - r], mesh_sem)
    copy.start()
    copy.wait()


def put_halves(value, step, keep_ref, give_ref, hold):
    rows = keep_ref.shape[0]
    bit = sum_bit(step)
    hold[...] = value
    keep_ref[...] = hold[pl.ds(pl.multiple_of(bit * rows, rows), rows), :].astype(keep_ref.dtype)
    give_ref[...] = hold[pl.ds(pl.multiple_of((1 - bit) * rows, rows), rows), :].astype(
        give_ref.dtype
    )


def terms_kernel(keep_ref, got_ref, *refs):
    outs, hold = refs[:4], refs[4]
    rows = hold.shape[0]
    for chain in range(2):
        part = slice(chain * rows, (chain + 1) * rows)
        put_halves(added(keep_ref[part, :], got_ref[part, :]), 0, *outs[2 * chain :][:2], hold)


def halving_kernel(step, kept_ref, got_ref, *refs):
    keep_ref, give_ref, hold = refs[-3:]
    put_halves(added(kept_ref[...], got_ref[...]), step, keep_ref, give_ref, hold)


def whole_kernel(kept_ref, got_ref, *refs):
    refs[-1][...] = added(kept_ref[...], got_ref[...]).astype(refs[-1].dtype)


def join_kernel(step, mine_ref, got_ref, *refs):
    out_ref = refs[-1]
    rows = mine_ref.shape[0]
    bit = sum_bit(step)
    out_ref[pl.ds(pl.multiple_of(bit * rows, rows), rows), :] = mine_ref[...].astype(out_ref.dtype)
    out_ref[pl.ds(pl.multiple_of((1 - bit) * rows, rows), rows), :] = got_ref[...].astype(
        out_ref.dtype
    )


def finish_outer_kernel(after_ref, mine_ref, other_ref, out_ref, out_other_ref, down_ref, grad_ref):
    r = lax.axis_index("rep")
    low = sum_bit(0) == 0
    width = mine_ref.shape[1]
    channels = out_ref.shape[0]
    mine, other = mine_ref[...], other_ref[...]
    terms = jnp.where(low, mine, other)[:, :channels]
    down_ref[:, pl.ds(pl.multiple_of(r * width, width), width)] = dot(terms, out_ref[...])
    down_ref[:, pl.ds(pl.multiple_of((1 - r) * width, width), width)] = dot(
        terms, out_other_ref[...]
    )
    grad_ref[...] = jnp.where(low, other, mine)[:channels].astype(F32)


def pair_kernel(after_ref, proj_ref, east_ref, pair_ref):
    pair_ref[0] = proj_ref[...]
    pair_ref[1] = east_ref[...]


def pick_kernel(device_ref, slot_ref, pair_ref, even_ref, odd_ref, mine_ref, theirs_ref):
    r = lax.axis_index("rep")
    tables = (pair_ref, even_ref, odd_ref)
    blocks = mine_ref.shape[0]
    per = pair_ref.shape[0]
    for out_ref, first in ((mine_ref, r * blocks), (theirs_ref, (1 - r) * blocks)):
        for i in range(blocks):
            at = entry_of(device_ref, slot_ref, first + i, per // 2)
            for k, table in enumerate(tables):
                @pl.when(at // per == k)
                def _(k=k, i=i, at=at, table=table, out_ref=out_ref):
                    out_ref[i] = table[at - k * per]


def decode_kernel(tiles_ref, base_ref, mine_ref, got_ref, out_ref, picked):
    r = lax.axis_index("rep")
    blocks, half = mine_ref.shape[:2]
    rows = tiles_ref.shape[1]
    channels = out_ref.shape[0]
    own = pl.ds(pl.multiple_of(r * half, half), half)
    other = pl.ds(pl.multiple_of((1 - r) * half, half), half)
    for i in range(blocks):
        picked[i, own, :] = mine_ref[i]
        picked[i, other, :] = got_ref[i]
    for i in range(blocks):
        cols = slice(i * rows, (i + 1) * rows)
        decoded = dot_last(picked[i].T, tiles_ref[r * blocks + i])
        out_ref[:, cols] = (base_ref[:, cols] + decoded[:channels]).astype(out_ref.dtype)


def along(axis, count, partner):
    pairs = []
    for source in range(count):
        to = partner(source)
        pairs.append((source, to if 0 <= to < count else source))
    return lambda value: lax.ppermute(value, axis, pairs)


def distances(axis):
    found, distance = [], 1
    while distance < lax.axis_size(axis):
        found.append((axis, distance))
        distance *= 2
    return found


def sum_orders():
    lat, lon = distances("lat"), distances("lon")
    return (lon + lat, lat + lon)


def sum_bit(step):
    bits = [
        lax.rem(lax.div(lax.axis_index(axis), distance), 2)
        for axis, distance in (order[step] for order in sum_orders())
    ]
    return jnp.where(lax.axis_index("rep") == 0, bits[0], bits[1])


def sum_swap(value, step):
    lat_count, lon_count = lax.axis_size("lat"), lax.axis_size("lon")
    orders = sum_orders()
    pairs = []
    for lat in range(lat_count):
        for lon in range(lon_count):
            for rep in range(2):
                axis, distance = orders[rep][step]
                to = (lat ^ distance, lon) if axis == "lat" else (lat, lon ^ distance)
                number = lambda a, b: (a * lon_count + b) * 2 + rep
                pairs.append((number(lat, lon), number(*to)))
    return lax.ppermute(value, ("lat", "lon", "rep"), pairs)


def per_device(
    grid_in, w_embed, interp_tiles, route_device, route_slot,
    mesh_embed, w_up, w_down, w_out, cotangent,
):
    lat_count, lon_count = lax.axis_size("lat"), lax.axis_size("lon")
    blocks, tile_rows = interp_tiles.shape[:2]
    grid_rows, channels = grid_in.shape
    my_rows = grid_rows // 2
    width = w_embed.shape[1]
    latent = 2 * width
    padded = -(-channels // 128) * 128
    slots = mesh_embed.shape[0] // tile_rows
    half = tile_rows // 2
    nodes = slots * half

    swap_rep = along("rep", 2, lambda i: 1 - i)
    to_even = along("lat", lat_count, lambda i: i ^ 1)
    to_odd = along("lat", lat_count, lambda i: ((i + 1) ^ 1) - 1)
    east_pairs = [(i, (i + 1) % lon_count) for i in range(lon_count)]
    west_pairs = [(j, i) for i, j in east_pairs]
    to_east = lambda value: lax.ppermute(value, "lon", east_pairs)

    in_hbm = lambda value: pltpu.with_memory_space_constraint(value, pltpu.HBM)
    device, slot = route_device.reshape(blocks), route_slot
    grid_t, cot_t, out_t = grid_in.T, cotangent.T, w_out.T
    routes = (in_hbm(device), in_hbm(slot))
    tiles_in, grid_in_t, cot_in_t = in_hbm(interp_tiles), in_hbm(grid_t), in_hbm(cot_t)
    pair_shape = (2, nodes, width)
    embed_other = swap_rep(w_embed)

    back_own, back_east, back_side = call(
        back_kernel, "back_messages",
        [smem(), smem(), anywhere(), anywhere()],
        [vmem()] * 3,
        [shape_of((nodes, padded), BF16), shape_of((3, nodes, padded), BF16),
         shape_of((2, nodes, padded), BF16)],
        1, 1,
        scratch=[
            pltpu.VMEM((6 * slots, half, padded), F32),
            pltpu.VMEM(interp_tiles.shape, BF16),
            pltpu.VMEM(cot_t.shape, BF16),
            pltpu.SemaphoreType.DMA((STEPS,)),
            pltpu.SemaphoreType.DMA((STEPS,)),
        ],
    )(*routes, tiles_in, cot_in_t)
    back_moved = to_east(back_east)

    def encode(after, weight):
        return call(
            encode_kernel, "encode",
            [smem(), smem(), anywhere()] + [vmem()] * 3,
            [vmem()] * 4,
            [shape_of(pair_shape, BF16)] * 3 + [shape_of((my_rows, width), BF16)],
            1, 1,
            scratch=[
                pltpu.VMEM((6 * slots, half, width), F32), pltpu.VMEM((grid_rows, width), BF16),
            ],
        )(device, slot, after, grid_t, interp_tiles, weight)

    own_a, even_a, odd_a, hidden_a = encode(back_own, in_hbm(w_embed))
    even_in_a, odd_in_a = to_even(even_a), to_odd(odd_a)
    own_b, even_b, odd_b, hidden_b = encode(own_a, embed_other)
    even_in_b, odd_in_b = to_even(even_b), to_odd(odd_b)

    out_other, up_other, down_other = swap_rep(out_t), swap_rep(w_up), swap_rep(w_down)
    embed_shape = (slots, 2, half, width)
    mesh_other = swap_rep(mesh_embed)

    base, local, local_other = call(
        local_kernel, "local_terms", [vmem()] * 5, [vmem()] * 3,
        [shape_of((channels, my_rows), F32)] + [shape_of((channels, width), F32)] * 2,
        4 * my_rows * latent * channels, 4e6,
    )(hidden_a, hidden_b, cot_t, out_t, out_other)

    second = pl.BlockSpec((1, nodes, width), lambda i: (1, 0, 0))

    def add_east(after, *terms):
        return call(
            add_kernel, "add_east", [anywhere()] + [second] * 3, whole((nodes, width)),
            shape_of((nodes, width), BF16), 3 * nodes * width, 6e5, grid=(1,),
        )(after, *terms)

    send_a = add_east(back_moved, own_a, even_in_a, odd_in_a)
    moved_a = to_east(send_a)
    send_b = add_east(moved_a, own_b, even_in_b, odd_in_b)
    moved_b = to_east(send_b)

    back_even, back_odd = call(
        sides_kernel, "add_sides", [anywhere(), vmem(), vmem()], [vmem()] * 2,
        [shape_of((nodes, padded), BF16)] * 2, 3 * nodes * width, 1e6,
    )(send_b, back_side, back_moved)
    back_even_in, back_odd_in = to_even(back_even), to_odd(back_odd)

    first = pl.BlockSpec((1, nodes, width), lambda i: (0, 0, 0))
    sums_specs = [first] * 3 + [whole((nodes, width))]
    weights = (w_up, up_other, w_down, down_other, out_t, out_other)
    back_spec = whole((nodes, padded))
    mesh_scratch = [pltpu.VMEM((slots, half, width), F32), pltpu.SemaphoreType.DMA]
    proj, keep, give, mesh_give, mesh_filled = call(
        node_kernel, "node_update_and_gradients",
        sums_specs * 2 + [whole(embed_shape)] * 2
        + [back_spec, pl.BlockSpec((1, nodes, padded), lambda i: (0, 0, 0)), back_spec, back_spec]
        + [whole((channels, width))] * 2 + [whole(w.shape) for w in weights],
        [whole((nodes, padded))] + [whole((2 * latent, width))] * 2
        + [whole((nodes, width)), anywhere()],
        [shape_of((nodes, padded), BF16), shape_of((2 * latent, width), F32),
         shape_of((2 * latent, width), BF16), shape_of((nodes, width), BF16),
         shape_of(embed_shape, F32)],
        15 * nodes * latent * latent, 9e6, grid=(1,), exps=nodes * latent, scratch=mesh_scratch,
    )(
        own_a, even_in_a, odd_in_a, moved_a, own_b, even_in_b, odd_in_b, moved_b,
        mesh_embed.reshape(embed_shape), mesh_other.reshape(embed_shape),
        back_own, back_moved, back_even_in, back_odd_in, local, local_other, *weights,
    )

    east = lax.ppermute(proj, "lon", west_pairs)
    hold = lambda rows: [pltpu.VMEM((rows, width), F32)]
    up_keep, up_give, outer_keep, outer_give = call(
        terms_kernel, "sum_terms", [vmem()] * 2, [vmem()] * 4,
        [shape_of((width, width), BF16)] * 4, 1, 1, scratch=hold(latent), weight=5e9,
    )(keep, swap_rep(give))

    count = len(sum_orders()[0])
    chains = [[outer_keep, outer_give], [up_keep, up_give]]
    latest = None

    def step_call(kernel, name, chain, step, out_rows, scratch=()):
        kept, given = chain[0], chain[-1]
        after = [latest] if latest is not None else []
        if chain is chains[1]:
            after += [[pair], [pair_even, pair_odd]][step] if step < 2 and len(chain) == 2 else []
        made = call(
            kernel, name, [vmem()] * 2 + [anywhere()] * len(after), [vmem()] * len(out_rows),
            [shape_of((rows, width), BF16) for rows in out_rows], 1, 1, scratch=scratch,
        )(kept, sum_swap(given, step), *after)
        return list(made)

    for step in range(count):
        for c in range(2):
            rows = chains[c][0].shape[0]
            if step == 0 and c == 1:
                pair = call(
                    pair_kernel, "pair_nodes", [anywhere()] + [vmem()] * 2, vmem(), shape_of((2, nodes, padded), BF16),
                    1, 1,
                )(up_give, proj, east)
                pair_even, pair_odd = to_even(pair), to_odd(pair)
            if step == 0:
                chains[c] = step_call(
                    functools.partial(halving_kernel, 1), "halve", chains[c], step,
                    [rows // 2] * 2, hold(rows),
                )
            else:
                chains[c] = step_call(whole_kernel, "add_whole", chains[c], step, [rows])
            latest = chains[c][-1]
    for c in range(2):
        rows = chains[c][0].shape[0]
        chains[c] = step_call(
            functools.partial(join_kernel, 1), "join", chains[c], 1, [2 * rows]
        )
        latest = chains[c][-1]
    (outer_mine,), (up_mine,) = chains
    outer_theirs, up_theirs = sum_swap(outer_mine, 0), sum_swap(up_mine, 0)

    grad_mesh = pl.pallas_call(
        place_kernel,
        in_specs=[vmem(), anywhere()],
        out_specs=anywhere(),
        out_shape=shape_of(embed_shape, F32),
        scratch_shapes=mesh_scratch,
        input_output_aliases={1: 0},
        compiler_params=pltpu.CompilerParams(vmem_limit_bytes=VMEM_BYTES),
        cost_estimate=pl.CostEstimate(flops=1, bytes_accessed=1, transcendentals=0),
        name="place_mesh",
    )(swap_rep(mesh_give), mesh_filled).reshape(mesh_embed.shape)

    table_shape = (2 * slots, half, padded)
    mine_picked, theirs_picked = call(
        pick_kernel, "pick_nodes", [smem()] * 2 + [vmem()] * 3, [vmem()] * 2,
        [shape_of((blocks // 2, half, padded), BF16)] * 2, 1, 1, weight=5e9,
    )(device, slot, *[table.reshape(table_shape) for table in (pair, pair_even, pair_odd)])
    grid_out_t = call(
        decode_kernel, "decode", [vmem()] * 4, vmem(),
        shape_of((channels, my_rows), BF16), 2 * my_rows * tile_rows * padded, 4e6,
        scratch=[pltpu.VMEM((blocks // 2, tile_rows, padded), BF16)],
    )(interp_tiles, base, mine_picked, swap_rep(theirs_picked))

    grad_down, grad_out = call(
        finish_outer_kernel, "finish_outer", [anywhere()] + [vmem()] * 4, [vmem()] * 2,
        [shape_of((width, latent), F32), shape_of((channels, width), F32)], 1, 1,
    )(grid_out_t, outer_mine, outer_theirs, out_t, out_other)
    grad_up = call(
        functools.partial(join_kernel, 0), "finish_up", [vmem()] * 2, vmem(),
        shape_of((latent, width), F32), 1, 1,
    )(up_mine, up_theirs)
    return (grid_out_t.T, grad_out.T, grad_up, grad_down, grad_mesh)


def solution(mesh):
    patch = ("groups", "lat", "lon")
    placed = (
        P(patch, None),
        P(None, "rep"),
        P(patch, None, None),
        P(patch, None),
        P(patch),
        P(patch, "rep"),
        P(None, "rep"),
        P("rep", None),
        P("rep", None),
        P(patch, None),
    )
    return jax.shard_map(
        per_device,
        mesh=mesh,
        in_specs=placed,
        out_specs=(
            P(("groups", "lat", "lon", "rep"), None),
            P(("groups", "rep"), None),
            P("groups", "rep"),
            P(("groups", "rep"), None),
            P(patch, "rep"),
        ),
        check_vma=False,
    )
```

```python
import functools

import jax
import jax.numpy as jnp
from jax import lax
from jax.experimental import pallas as pl
from jax.experimental.pallas import tpu as pltpu
from jax.sharding import PartitionSpec as P

F32 = jnp.float32
BF16 = jnp.bfloat16
VMEM_BYTES = 20 * 1024 * 1024
STEPS = 4


def dot(left, right):
    return jnp.dot(left, right, preferred_element_type=F32)


def dot_rows(left, right):
    return lax.dot_general(left, right, (((0,), (0,)), ((), ())), preferred_element_type=F32)


def dot_last(left, right):
    return lax.dot_general(left, right, (((1,), (1,)), ((), ())), preferred_element_type=F32)


def sigmoid(values):
    return 0.5 * jnp.tanh(0.5 * values) + 0.5


def vmem():
    return pl.BlockSpec(memory_space=pltpu.VMEM)


def smem():
    return pl.BlockSpec(memory_space=pltpu.SMEM)


def anywhere():
    return pl.BlockSpec(memory_space=pl.ANY)


def whole(shape):
    return pl.BlockSpec(shape, lambda i: (0,) * len(shape))


def shape_of(shape, dtype):
    return jax.ShapeDtypeStruct(shape, dtype)


def call(kernel, name, in_specs, out_specs, out_shape, flops, nbytes, grid=(), scratch=(), exps=0,
         limit=VMEM_BYTES, weight=1):
    return pl.pallas_call(
        kernel,
        grid=grid,
        in_specs=in_specs,
        out_specs=out_specs,
        out_shape=out_shape,
        scratch_shapes=list(scratch),
        compiler_params=pltpu.CompilerParams(vmem_limit_bytes=limit),
        cost_estimate=pl.CostEstimate(flops=int(weight), bytes_accessed=1, transcendentals=0),
        name=name,
    )


def node_half(tile, r):
    half = tile.shape[1] // 2
    return jnp.where(r == 0, tile[:, :half], tile[:, half:]).T


def entry_of(device_ref, slot_ref, b, slots):
    lon_count = lax.axis_size("lon")
    lat, lon = lax.axis_index("lat"), lax.axis_index("lon")
    target = device_ref[b]
    band = lax.div(target, lon_count)
    sector = target - band * lon_count - lon
    sector = jnp.where(sector < 0, sector + lon_count, sector)
    step = band - lat
    even_step = 1 - 2 * lax.rem(lat, 2)
    side = jnp.where(step == 0, 0, jnp.where(step == even_step, 1, 2))
    return (side * 2 + sector) * slots + slot_ref[b]


def write_packed(total, outs):
    per = total.shape[0] // 3
    for k, out in enumerate(outs):
        block = total[k * per : (k + 1) * per]
        out[...] = block.reshape(out.shape).astype(out.dtype)


def back_kernel(
    device_ref, slot_ref, tiles_ref, cot_ref, own_ref, east_ref, side_ref,
    total, tiles, cots, tile_sems, cot_sems,
):
    blocks, rows = tiles.shape[0], tiles.shape[1]
    count = blocks // STEPS
    slots = total.shape[0] // 6
    channels = cots.shape[0]
    r = lax.axis_index("rep")
    copies = []
    for k in range(STEPS):
        part = pl.ds(k * count, count)
        cols = pl.ds(k * count * rows, count * rows)
        copies.append((
            pltpu.make_async_copy(tiles_ref.at[part], tiles.at[part], tile_sems.at[k]),
            pltpu.make_async_copy(cot_ref.at[:, cols], cots.at[:, cols], cot_sems.at[k]),
        ))
        for copy in copies[-1]:
            copy.start()
    total[...] = jnp.zeros_like(total)
    for b in range(blocks):
        if b % count == 0:
            for copy in copies[b // count]:
                copy.wait()
        at = entry_of(device_ref, slot_ref, b, slots)
        cot = cots[:, b * rows : (b + 1) * rows]
        total[at, :, :channels] += dot_last(node_half(tiles[b], r), cot)
    for k, out in ((0, own_ref), (2, side_ref.at[0]), (4, side_ref.at[1])):
        out[...] = total[k * slots : (k + 1) * slots].reshape(out.shape).astype(out.dtype)
    for k in range(3):
        block = total[(2 * k + 1) * slots : (2 * k + 2) * slots]
        east_ref[k] = block.reshape(east_ref.shape[1:]).astype(east_ref.dtype)


def encode_kernel(
    device_ref, slot_ref, after_ref, grid_ref, tiles_ref, weight_ref,
    own_ref, even_ref, odd_ref, hidden_ref, total, hold,
):
    blocks, rows = tiles_ref.shape[:2]
    slots = total.shape[0] // 6
    step_rows = blocks * rows // STEPS
    r = lax.axis_index("rep")
    total[...] = jnp.zeros_like(total)
    for k in range(STEPS):
        preact = dot_rows(grid_ref[:, k * step_rows : (k + 1) * step_rows], weight_ref[...])
        hold[k * step_rows : (k + 1) * step_rows, :] = (preact * sigmoid(preact)).astype(BF16)
        for b in range(k * blocks // STEPS, (k + 1) * blocks // STEPS):
            at = entry_of(device_ref, slot_ref, b, slots)
            total[at] += dot(node_half(tiles_ref[b], r), hold[b * rows : (b + 1) * rows, :])
    mine = hidden_ref.shape[0]
    hidden_ref[...] = hold[pl.ds(pl.multiple_of(r * mine, mine), mine), :]
    write_packed(total, (own_ref, even_ref, odd_ref))


def local_kernel(
    own_ref, oth_ref, cot_ref, out_ref, out_other_ref,
    base_ref, grad_ref, grad_other_ref,
):
    rows = own_ref.shape[0]
    r = lax.axis_index("rep")
    cot = cot_ref[:, pl.ds(pl.multiple_of(r * rows, rows), rows)]
    base_ref[...] = dot_last(out_ref[...], own_ref[...]) + dot_last(out_other_ref[...], oth_ref[...])
    grad_ref[...] = dot(cot, own_ref[...])
    grad_other_ref[...] = dot(cot, oth_ref[...])


def added(*values):
    total = values[0].astype(F32)
    for value in values[1:]:
        total = total + value.astype(F32)
    return total


def add_kernel(*refs):
    a, b, c, out = refs[-4:]
    out[...] = added(a[0], b[0], c[0]).astype(out.dtype)


def sides_kernel(after_ref, side_ref, moved_ref, even_ref, odd_ref):
    even_ref[...] = added(side_ref[0], moved_ref[1]).astype(even_ref.dtype)
    odd_ref[...] = added(side_ref[1], moved_ref[2]).astype(odd_ref.dtype)


def node_kernel(
    own_a, even_a, odd_a, moved_a, own_b, even_b, odd_b, moved_b, embed_ref, embed_other_ref,
    back_ref, back_moved_ref, back_even_ref, back_odd_ref, local_ref, local_other_ref,
    up_ref, up_other_ref, down_ref, down_other_ref, out_ref, out_other_ref,
    proj_ref, keep_ref, give_ref, mesh_give_ref, mesh_ref, mesh_half, mesh_sem,
):
    r = lax.axis_index("rep")
    nodes, width = moved_a.shape
    latent = 2 * width
    channels = out_ref.shape[0]
    first = pl.multiple_of(r * width, width)
    second = pl.multiple_of((1 - r) * width, width)
    states = []
    for embed, parts in (
        (embed_ref, (own_a[0], even_a[0], odd_a[0], moved_a[...])),
        (embed_other_ref, (own_b[0], even_b[0], odd_b[0], moved_b[...])),
    ):
        start = embed[:, r].reshape(nodes, width)
        states.append((start.astype(F32) + added(*parts)).astype(BF16).astype(F32))
    state = jnp.concatenate(states, axis=1)
    centered = state - jnp.mean(state, axis=-1, keepdims=True)
    inverse = lax.rsqrt(jnp.mean(centered * centered, axis=-1, keepdims=True) + 1e-05)
    norm = centered * inverse
    normed = norm.astype(BF16)

    cot = added(back_ref[...], back_moved_ref[0], back_even_ref[...], back_odd_ref[...]).astype(BF16)
    terms = cot[:, :channels]
    grad_own = dot(terms, out_ref[...]).astype(BF16)
    grad_oth = dot(terms, out_other_ref[...]).astype(BF16)

    update_own = jnp.zeros((nodes, width), F32)
    update_oth = jnp.zeros((nodes, width), F32)
    back_own = jnp.zeros((nodes, width), F32)
    back_oth = jnp.zeros((nodes, width), F32)
    sides = ((up_ref, down_ref, keep_ref), (up_other_ref, down_other_ref, give_ref))
    for u_ref, d_ref, o_ref in sides:
        up_own, up_oth = u_ref[pl.ds(first, width), :], u_ref[pl.ds(second, width), :]
        down_own, down_oth = d_ref[:, pl.ds(first, width)], d_ref[:, pl.ds(second, width)]
        hidden = dot(normed[:, :width], up_own) + dot(normed[:, width:], up_oth)
        squash = sigmoid(hidden)
        act = (hidden * squash).astype(BF16)
        update_own += dot(act, down_own)
        update_oth += dot(act, down_oth)
        o_ref[latent : latent + width, :] = dot_rows(act, cot).astype(o_ref.dtype)
        act_grad = dot_last(grad_own, down_own) + dot_last(grad_oth, down_oth)
        pre_grad = (act_grad * squash * (1.0 + hidden * (1.0 - squash))).astype(BF16)
        o_ref[pl.ds(first, width), :] = dot_rows(normed[:, :width], pre_grad).astype(o_ref.dtype)
        o_ref[pl.ds(second, width), :] = dot_rows(normed[:, width:], pre_grad).astype(o_ref.dtype)
        back_own += dot_last(pre_grad, up_own)
        back_oth += dot_last(pre_grad, up_oth)

    mesh_own = (states[0] + update_own).astype(BF16)
    mesh_oth = (states[1] + update_oth).astype(BF16)
    proj = dot_last(mesh_own, out_ref[...]) + dot_last(mesh_oth, out_other_ref[...])
    proj_ref[...] = jnp.zeros_like(proj_ref)
    proj_ref[:, :channels] = proj.astype(BF16)
    ends = ((keep_ref, mesh_own, local_ref), (give_ref, mesh_oth, local_other_ref))
    start = latent + width
    for o_ref, mesh, local in ends:
        grad = dot_rows(cot, mesh)
        o_ref[start : 2 * latent, :] = grad.astype(o_ref.dtype)
        o_ref[start : start + channels, :] = (grad[:channels] + local[...]).astype(o_ref.dtype)

    back = jnp.concatenate([back_own, back_oth], axis=1)
    slope = (
        back - jnp.mean(back, axis=-1, keepdims=True)
        - norm * jnp.mean(back * norm, axis=-1, keepdims=True)
    ) * inverse
    mesh_half[...] = (grad_own.astype(F32) + slope[:, :width]).reshape(mesh_half.shape)
    mesh_give_ref[...] = (grad_oth.astype(F32) + slope[:, width:]).astype(mesh_give_ref.dtype)
    copy = pltpu.make_async_copy(mesh_half, mesh_ref.at[:, r], mesh_sem)
    copy.start()
    copy.wait()


def place_kernel(got_ref, filled_ref, mesh_ref, mesh_half, mesh_sem):
    r = lax.axis_index("rep")
    mesh_half[...] = got_ref[...].astype(F32).reshape(mesh_half.shape)
    copy = pltpu.make_async_copy(mesh_half, mesh_ref.at[:, 1 - r], mesh_sem)
    copy.start()
    copy.wait()


def put_halves(value, step, keep_ref, give_ref, hold):
    rows = keep_ref.shape[0]
    bit = sum_bit(step)
    hold[...] = value
    keep_ref[...] = hold[pl.ds(pl.multiple_of(bit * rows, rows), rows), :].astype(keep_ref.dtype)
    give_ref[...] = hold[pl.ds(pl.multiple_of((1 - bit) * rows, rows), rows), :].astype(
        give_ref.dtype
    )


def terms_kernel(keep_ref, got_ref, *refs):
    outs, hold = refs[:4], refs[4]
    rows = hold.shape[0]
    for chain in range(2):
        part = slice(chain * rows, (chain + 1) * rows)
        put_halves(added(keep_ref[part, :], got_ref[part, :]), 0, *outs[2 * chain :][:2], hold)


def halving_kernel(step, kept_ref, got_ref, *refs):
    keep_ref, give_ref, hold = refs[-3:]
    put_halves(added(kept_ref[...], got_ref[...]), step, keep_ref, give_ref, hold)


def whole_kernel(kept_ref, got_ref, *refs):
    refs[-1][...] = added(kept_ref[...], got_ref[...]).astype(refs[-1].dtype)


def join_kernel(step, mine_ref, got_ref, *refs):
    out_ref = refs[-1]
    rows = mine_ref.shape[0]
    bit = sum_bit(step)
    out_ref[pl.ds(pl.multiple_of(bit * rows, rows), rows), :] = mine_ref[...].astype(out_ref.dtype)
    out_ref[pl.ds(pl.multiple_of((1 - bit) * rows, rows), rows), :] = got_ref[...].astype(
        out_ref.dtype
    )


def finish_outer_kernel(after_ref, mine_ref, other_ref, out_ref, out_other_ref, down_ref, grad_ref):
    r = lax.axis_index("rep")
    low = sum_bit(0) == 0
    width = mine_ref.shape[1]
    channels = out_ref.shape[0]
    mine, other = mine_ref[...], other_ref[...]
    terms = jnp.where(low, mine, other)[:, :channels]
    down_ref[:, pl.ds(pl.multiple_of(r * width, width), width)] = dot(terms, out_ref[...])
    down_ref[:, pl.ds(pl.multiple_of((1 - r) * width, width), width)] = dot(
        terms, out_other_ref[...]
    )
    grad_ref[...] = jnp.where(low, other, mine)[:channels].astype(F32)


def pack_kernel(after_ref, proj_ref, even_ref, odd_ref, out_ref):
    for k, part in enumerate((proj_ref, even_ref, odd_ref)):
        out_ref[k] = part[...]


def pick_kernel(device_ref, slot_ref, after_ref, own_ref, east_ref, mine_ref, theirs_ref):
    r = lax.axis_index("rep")
    blocks = mine_ref.shape[0]
    slots = own_ref.shape[0] // 3
    for out_ref, first in ((mine_ref, r * blocks), (theirs_ref, (1 - r) * blocks)):
        for i in range(blocks):
            at = entry_of(device_ref, slot_ref, first + i, slots)
            side = lax.div(at, 2 * slots)
            rest = at - side * 2 * slots

            @pl.when(rest < slots)
            def _(i=i, at=side * slots + rest, out_ref=out_ref):
                out_ref[i] = own_ref[at]

            @pl.when(rest >= slots)
            def _(i=i, at=side * slots + rest - slots, out_ref=out_ref):
                out_ref[i] = east_ref[at]


def decode_kernel(tiles_ref, base_ref, mine_ref, got_ref, out_ref, picked):
    r = lax.axis_index("rep")
    blocks, half = mine_ref.shape[:2]
    rows = tiles_ref.shape[1]
    channels = out_ref.shape[0]
    own = pl.ds(pl.multiple_of(r * half, half), half)
    other = pl.ds(pl.multiple_of((1 - r) * half, half), half)
    for i in range(blocks):
        picked[i, own, :] = mine_ref[i]
        picked[i, other, :] = got_ref[i]
    for i in range(blocks):
        cols = slice(i * rows, (i + 1) * rows)
        decoded = dot_last(picked[i].T, tiles_ref[r * blocks + i])
        out_ref[:, cols] = (base_ref[:, cols] + decoded[:channels]).astype(out_ref.dtype)


def along(axis, count, partner):
    pairs = []
    for source in range(count):
        to = partner(source)
        pairs.append((source, to if 0 <= to < count else source))
    return lambda value: lax.ppermute(value, axis, pairs)


def distances(axis):
    found, distance = [], 1
    while distance < lax.axis_size(axis):
        found.append((axis, distance))
        distance *= 2
    return found


def sum_orders():
    lat, lon = distances("lat"), distances("lon")
    return (lon + lat, lat + lon)


def sum_bit(step):
    bits = [
        lax.rem(lax.div(lax.axis_index(axis), distance), 2)
        for axis, distance in (order[step] for order in sum_orders())
    ]
    return jnp.where(lax.axis_index("rep") == 0, bits[0], bits[1])


def sum_swap(value, step):
    lat_count, lon_count = lax.axis_size("lat"), lax.axis_size("lon")
    orders = sum_orders()
    pairs = []
    for lat in range(lat_count):
        for lon in range(lon_count):
            for rep in range(2):
                axis, distance = orders[rep][step]
                to = (lat ^ distance, lon) if axis == "lat" else (lat, lon ^ distance)
                number = lambda a, b: (a * lon_count + b) * 2 + rep
                pairs.append((number(lat, lon), number(*to)))
    return lax.ppermute(value, ("lat", "lon", "rep"), pairs)


def per_device(
    grid_in, w_embed, interp_tiles, route_device, route_slot,
    mesh_embed, w_up, w_down, w_out, cotangent,
):
    lat_count, lon_count = lax.axis_size("lat"), lax.axis_size("lon")
    blocks, tile_rows = interp_tiles.shape[:2]
    grid_rows, channels = grid_in.shape
    my_rows = grid_rows // 2
    width = w_embed.shape[1]
    latent = 2 * width
    padded = -(-channels // 128) * 128
    slots = mesh_embed.shape[0] // tile_rows
    half = tile_rows // 2
    nodes = slots * half

    swap_rep = along("rep", 2, lambda i: 1 - i)
    to_even = along("lat", lat_count, lambda i: i ^ 1)
    to_odd = along("lat", lat_count, lambda i: ((i + 1) ^ 1) - 1)
    east_pairs = [(i, (i + 1) % lon_count) for i in range(lon_count)]
    west_pairs = [(j, i) for i, j in east_pairs]
    to_east = lambda value: lax.ppermute(value, "lon", east_pairs)

    in_hbm = lambda value: pltpu.with_memory_space_constraint(value, pltpu.HBM)
    device, slot = route_device.reshape(blocks), route_slot
    grid_t, cot_t, out_t = grid_in.T, cotangent.T, w_out.T
    routes = (in_hbm(device), in_hbm(slot))
    tiles_in, grid_in_t, cot_in_t = in_hbm(interp_tiles), in_hbm(grid_t), in_hbm(cot_t)
    pair_shape = (2, nodes, width)
    embed_other = swap_rep(w_embed)

    back_own, back_east, back_side = call(
        back_kernel, "back_messages",
        [smem(), smem(), anywhere(), anywhere()],
        [vmem()] * 3,
        [shape_of((nodes, padded), BF16), shape_of((3, nodes, padded), BF16),
         shape_of((2, nodes, padded), BF16)],
        1, 1,
        scratch=[
            pltpu.VMEM((6 * slots, half, padded), F32),
            pltpu.VMEM(interp_tiles.shape, BF16),
            pltpu.VMEM(cot_t.shape, BF16),
            pltpu.SemaphoreType.DMA((STEPS,)),
            pltpu.SemaphoreType.DMA((STEPS,)),
        ],
    )(*routes, tiles_in, cot_in_t)
    back_moved = to_east(back_east)

    def encode(after, weight):
        return call(
            encode_kernel, "encode",
            [smem(), smem(), anywhere()] + [vmem()] * 3,
            [vmem()] * 4,
            [shape_of(pair_shape, BF16)] * 3 + [shape_of((my_rows, width), BF16)],
            1, 1,
            scratch=[
                pltpu.VMEM((6 * slots, half, width), F32), pltpu.VMEM((grid_rows, width), BF16),
            ],
        )(*routes, after, grid_t, interp_tiles, weight)

    own_a, even_a, odd_a, hidden_a = encode(back_own, in_hbm(w_embed))
    even_in_a, odd_in_a = to_even(even_a), to_odd(odd_a)
    own_b, even_b, odd_b, hidden_b = encode(own_a, embed_other)
    even_in_b, odd_in_b = to_even(even_b), to_odd(odd_b)

    out_other, up_other, down_other = swap_rep(out_t), swap_rep(w_up), swap_rep(w_down)
    embed_shape = (slots, 2, half, width)
    mesh_other = swap_rep(mesh_embed)

    second = pl.BlockSpec((1, nodes, width), lambda i: (1, 0, 0))

    def add_east(after, *terms):
        return call(
            add_kernel, "add_east", [anywhere()] * len(after) + [second] * 3, whole((nodes, width)),
            shape_of((nodes, width), BF16), 3 * nodes * width, 6e5, grid=(1,),
        )(*after, *terms)

    send_a = add_east((back_moved,), own_a, even_in_a, odd_in_a)
    moved_a = to_east(send_a)

    base, local, local_other = call(
        local_kernel, "local_terms", [vmem()] * 5, [vmem()] * 3,
        [shape_of((channels, my_rows), F32)] + [shape_of((channels, width), F32)] * 2,
        4 * my_rows * latent * channels, 4e6,
    )(hidden_a, hidden_b, cot_t, out_t, out_other)

    send_b = add_east((moved_a,), own_b, even_in_b, odd_in_b)
    moved_b = to_east(send_b)

    back_even, back_odd = call(
        sides_kernel, "add_sides", [anywhere(), vmem(), vmem()], [vmem()] * 2,
        [shape_of((nodes, padded), BF16)] * 2, 3 * nodes * width, 1e6,
    )(send_b, back_side, back_moved)
    back_even_in, back_odd_in = to_even(back_even), to_odd(back_odd)

    first = pl.BlockSpec((1, nodes, width), lambda i: (0, 0, 0))
    sums_specs = [first] * 3 + [whole((nodes, width))]
    weights = (w_up, up_other, w_down, down_other, out_t, out_other)
    back_spec = whole((nodes, padded))
    mesh_scratch = [pltpu.VMEM((slots, half, width), F32), pltpu.SemaphoreType.DMA]
    proj, keep, give, mesh_give, mesh_filled = call(
        node_kernel, "node_update_and_gradients",
        sums_specs * 2 + [whole(embed_shape)] * 2
        + [back_spec, pl.BlockSpec((1, nodes, padded), lambda i: (0, 0, 0)), back_spec, back_spec]
        + [whole((channels, width))] * 2 + [whole(w.shape) for w in weights],
        [whole((nodes, padded))] + [whole((2 * latent, width))] * 2
        + [whole((nodes, width)), anywhere()],
        [shape_of((nodes, padded), BF16), shape_of((2 * latent, width), F32),
         shape_of((2 * latent, width), BF16), shape_of((nodes, width), BF16),
         shape_of(embed_shape, F32)],
        15 * nodes * latent * latent, 9e6, grid=(1,), exps=nodes * latent, scratch=mesh_scratch,
    )(
        own_a, even_in_a, odd_in_a, moved_a, own_b, even_in_b, odd_in_b, moved_b,
        mesh_embed.reshape(embed_shape), mesh_other.reshape(embed_shape),
        back_own, back_moved, back_even_in, back_odd_in, local, local_other, *weights,
    )

    proj_even, proj_odd = to_even(proj), to_odd(proj)
    hold = lambda rows: [pltpu.VMEM((rows, width), F32)]
    up_keep, up_give, outer_keep, outer_give = call(
        terms_kernel, "sum_terms", [vmem()] * 2, [vmem()] * 4,
        [shape_of((width, width), BF16)] * 4, 1, 1, scratch=hold(latent), weight=5e9,
    )(keep, swap_rep(give))

    count = len(sum_orders()[0])
    chains = [[outer_keep, outer_give], [up_keep, up_give]]
    latest = None

    def step_call(kernel, name, chain, step, out_rows, scratch=()):
        kept, given = chain[0], chain[-1]
        after = [latest] if latest is not None else []
        made = call(
            kernel, name, [vmem()] * 2 + [anywhere()] * len(after), [vmem()] * len(out_rows),
            [shape_of((rows, width), BF16) for rows in out_rows], 1, 1, scratch=scratch,
        )(kept, sum_swap(given, step), *after)
        return list(made)

    for step in range(count):
        for c in range(2):
            rows = chains[c][0].shape[0]
            if step == 1 and c == 0:
                trio = call(
                    pack_kernel, "pack_nodes", [anywhere()] + [vmem()] * 3, vmem(),
                    shape_of((3, nodes, padded), BF16), 1, 1,
                )(latest, proj, proj_even, proj_odd)
                east_trio = lax.ppermute(trio, "lon", west_pairs)
            if step == 0:
                chains[c] = step_call(
                    functools.partial(halving_kernel, 1), "halve", chains[c], step,
                    [rows // 2] * 2, hold(rows),
                )
            else:
                chains[c] = step_call(whole_kernel, "add_whole", chains[c], step, [rows])
            latest = chains[c][-1]
    after_pick = chains[1][-1]
    for c in range(2):
        rows = chains[c][0].shape[0]
        chains[c] = step_call(
            functools.partial(join_kernel, 1), "join", chains[c], 1, [2 * rows]
        )
        latest = chains[c][-1]
    (outer_mine,), (up_mine,) = chains
    outer_theirs, up_theirs = sum_swap(outer_mine, 0), sum_swap(up_mine, 0)

    grad_mesh = pl.pallas_call(
        place_kernel,
        in_specs=[vmem(), anywhere()],
        out_specs=anywhere(),
        out_shape=shape_of(embed_shape, F32),
        scratch_shapes=mesh_scratch,
        input_output_aliases={1: 0},
        compiler_params=pltpu.CompilerParams(vmem_limit_bytes=VMEM_BYTES),
        cost_estimate=pl.CostEstimate(flops=1, bytes_accessed=1, transcendentals=0),
        name="place_mesh",
    )(swap_rep(mesh_give), mesh_filled).reshape(mesh_embed.shape)

    table_shape = (3 * slots, half, padded)
    mine_picked, theirs_picked = call(
        pick_kernel, "pick_nodes", [smem()] * 2 + [anywhere()] + [vmem()] * 2, [vmem()] * 2,
        [shape_of((blocks // 2, half, padded), BF16)] * 2, 1, 1,
    )(device, slot, after_pick, trio.reshape(table_shape), east_trio.reshape(table_shape))
    grid_out_t = call(
        decode_kernel, "decode", [vmem()] * 4, vmem(),
        shape_of((channels, my_rows), BF16), 2 * my_rows * tile_rows * padded, 4e6,
        scratch=[pltpu.VMEM((blocks // 2, tile_rows, padded), BF16)],
    )(interp_tiles, base, mine_picked, swap_rep(theirs_picked))

    grad_down, grad_out = call(
        finish_outer_kernel, "finish_outer", [anywhere()] + [vmem()] * 4, [vmem()] * 2,
        [shape_of((width, latent), F32), shape_of((channels, width), F32)], 1, 1,
    )(in_hbm(grid_out_t), outer_mine, outer_theirs, out_t, out_other)
    grad_up = call(
        functools.partial(join_kernel, 0), "finish_up", [vmem()] * 2 + [anywhere()], vmem(),
        shape_of((latent, width), F32), 1, 1,
    )(up_mine, up_theirs, in_hbm(grid_out_t))
    return (grid_out_t.T, grad_out.T, grad_up, grad_down, grad_mesh)


def solution(mesh):
    patch = ("groups", "lat", "lon")
    placed = (
        P(patch, None),
        P(None, "rep"),
        P(patch, None, None),
        P(patch, None),
        P(patch),
        P(patch, "rep"),
        P(None, "rep"),
        P("rep", None),
        P("rep", None),
        P(patch, None),
    )
    return jax.shard_map(
        per_device,
        mesh=mesh,
        in_specs=placed,
        out_specs=(
            P(("groups", "lat", "lon", "rep"), None),
            P(("groups", "rep"), None),
            P("groups", "rep"),
            P(("groups", "rep"), None),
            P(patch, "rep"),
        ),
        check_vma=False,
    )
```

```python
import functools

import jax
import jax.numpy as jnp
from jax import lax
from jax.experimental import pallas as pl
from jax.experimental.pallas import tpu as pltpu
from jax.sharding import PartitionSpec as P

F32 = jnp.float32
BF16 = jnp.bfloat16
VMEM_BYTES = 20 * 1024 * 1024
STEPS = 4


def dot(left, right):
    return jnp.dot(left, right, preferred_element_type=F32)


def dot_rows(left, right):
    return lax.dot_general(left, right, (((0,), (0,)), ((), ())), preferred_element_type=F32)


def dot_last(left, right):
    return lax.dot_general(left, right, (((1,), (1,)), ((), ())), preferred_element_type=F32)


def sigmoid(values):
    return 0.5 * jnp.tanh(0.5 * values) + 0.5


def vmem():
    return pl.BlockSpec(memory_space=pltpu.VMEM)


def smem():
    return pl.BlockSpec(memory_space=pltpu.SMEM)


def anywhere():
    return pl.BlockSpec(memory_space=pl.ANY)


def whole(shape):
    return pl.BlockSpec(shape, lambda i: (0,) * len(shape))


def shape_of(shape, dtype):
    return jax.ShapeDtypeStruct(shape, dtype)


def call(kernel, name, in_specs, out_specs, out_shape, flops, nbytes, grid=(), scratch=(), exps=0,
         limit=VMEM_BYTES, weight=1):
    return pl.pallas_call(
        kernel,
        grid=grid,
        in_specs=in_specs,
        out_specs=out_specs,
        out_shape=out_shape,
        scratch_shapes=list(scratch),
        compiler_params=pltpu.CompilerParams(vmem_limit_bytes=limit),
        cost_estimate=pl.CostEstimate(flops=int(weight), bytes_accessed=1, transcendentals=0),
        name=name,
    )


def node_half(tile, r):
    half = tile.shape[1] // 2
    return jnp.where(r == 0, tile[:, :half], tile[:, half:]).T


def entry_of(device_ref, slot_ref, b, slots):
    lon_count = lax.axis_size("lon")
    lat, lon = lax.axis_index("lat"), lax.axis_index("lon")
    target = device_ref[b]
    band = lax.div(target, lon_count)
    sector = target - band * lon_count - lon
    sector = jnp.where(sector < 0, sector + lon_count, sector)
    step = band - lat
    even_step = 1 - 2 * lax.rem(lat, 2)
    side = jnp.where(step == 0, 0, jnp.where(step == even_step, 1, 2))
    return (side * 2 + sector) * slots + slot_ref[b]


def write_packed(total, outs):
    per = total.shape[0] // 3
    for k, out in enumerate(outs):
        block = total[k * per : (k + 1) * per]
        out[...] = block.reshape(out.shape).astype(out.dtype)


def back_kernel(
    device_ref, slot_ref, tiles_ref, cot_ref, own_ref, east_ref, side_ref,
    total, tiles, cots, tile_sems, cot_sems,
):
    blocks, rows = tiles.shape[0], tiles.shape[1]
    count = blocks // STEPS
    slots = total.shape[0] // 6
    channels = cots.shape[0]
    r = lax.axis_index("rep")
    copies = []
    for k in range(STEPS):
        part = pl.ds(k * count, count)
        cols = pl.ds(k * count * rows, count * rows)
        copies.append((
            pltpu.make_async_copy(tiles_ref.at[part], tiles.at[part], tile_sems.at[k]),
            pltpu.make_async_copy(cot_ref.at[:, cols], cots.at[:, cols], cot_sems.at[k]),
        ))
        for copy in copies[-1]:
            copy.start()
    total[...] = jnp.zeros_like(total)
    for b in range(blocks):
        if b % count == 0:
            for copy in copies[b // count]:
                copy.wait()
        at = entry_of(device_ref, slot_ref, b, slots)
        cot = cots[:, b * rows : (b + 1) * rows]
        total[at, :, :channels] += dot_last(node_half(tiles[b], r), cot)
    for k, out in ((0, own_ref), (2, side_ref.at[0]), (4, side_ref.at[1])):
        out[...] = total[k * slots : (k + 1) * slots].reshape(out.shape).astype(out.dtype)
    for k in range(3):
        block = total[(2 * k + 1) * slots : (2 * k + 2) * slots]
        east_ref[k] = block.reshape(east_ref.shape[1:]).astype(east_ref.dtype)


def encode_kernel(
    device_ref, slot_ref, after_ref, grid_ref, tiles_ref, weight_ref,
    own_ref, even_ref, odd_ref, hidden_ref, total, hold,
):
    blocks, rows = tiles_ref.shape[:2]
    slots = total.shape[0] // 6
    step_rows = blocks * rows // STEPS
    r = lax.axis_index("rep")
    total[...] = jnp.zeros_like(total)
    for k in range(STEPS):
        preact = dot_rows(grid_ref[:, k * step_rows : (k + 1) * step_rows], weight_ref[...])
        hold[k * step_rows : (k + 1) * step_rows, :] = (preact * sigmoid(preact)).astype(BF16)
        for b in range(k * blocks // STEPS, (k + 1) * blocks // STEPS):
            at = entry_of(device_ref, slot_ref, b, slots)
            total[at] += dot(node_half(tiles_ref[b], r), hold[b * rows : (b + 1) * rows, :])
    mine = hidden_ref.shape[0]
    hidden_ref[...] = hold[pl.ds(pl.multiple_of(r * mine, mine), mine), :]
    write_packed(total, (own_ref, even_ref, odd_ref))


def local_kernel(*refs):
    own_ref, oth_ref, cot_ref, out_ref, out_other_ref, base_ref, grad_ref, grad_other_ref = refs[-8:]
    rows = own_ref.shape[0]
    r = lax.axis_index("rep")
    cot = cot_ref[:, pl.ds(pl.multiple_of(r * rows, rows), rows)]
    base_ref[...] = dot_last(out_ref[...], own_ref[...]) + dot_last(out_other_ref[...], oth_ref[...])
    grad_ref[...] = dot(cot, own_ref[...])
    grad_other_ref[...] = dot(cot, oth_ref[...])


def added(*values):
    total = values[0].astype(F32)
    for value in values[1:]:
        total = total + value.astype(F32)
    return total


def add_kernel(*refs):
    a, b, c, out = refs[-4:]
    out[...] = added(a[0], b[0], c[0]).astype(out.dtype)


def sides_kernel(after_ref, side_ref, moved_ref, even_ref, odd_ref):
    even_ref[...] = added(side_ref[0], moved_ref[1]).astype(even_ref.dtype)
    odd_ref[...] = added(side_ref[1], moved_ref[2]).astype(odd_ref.dtype)


def node_kernel(
    own_a, even_a, odd_a, moved_a, own_b, even_b, odd_b, moved_b, embed_ref, embed_other_ref,
    back_ref, back_moved_ref, back_even_ref, back_odd_ref, local_ref, local_other_ref,
    up_ref, up_other_ref, down_ref, down_other_ref, out_ref, out_other_ref,
    proj_ref, keep_ref, give_ref, mesh_give_ref, mesh_ref, mesh_half, mesh_sem,
):
    r = lax.axis_index("rep")
    nodes, width = moved_a.shape
    latent = 2 * width
    channels = out_ref.shape[0]
    first = pl.multiple_of(r * width, width)
    second = pl.multiple_of((1 - r) * width, width)
    states = []
    for embed, parts in (
        (embed_ref, (own_a[0], even_a[0], odd_a[0], moved_a[...])),
        (embed_other_ref, (own_b[0], even_b[0], odd_b[0], moved_b[...])),
    ):
        start = embed[:, r].reshape(nodes, width)
        states.append((start.astype(F32) + added(*parts)).astype(BF16).astype(F32))
    state = jnp.concatenate(states, axis=1)
    centered = state - jnp.mean(state, axis=-1, keepdims=True)
    inverse = lax.rsqrt(jnp.mean(centered * centered, axis=-1, keepdims=True) + 1e-05)
    norm = centered * inverse
    normed = norm.astype(BF16)

    cot = added(back_ref[...], back_moved_ref[0], back_even_ref[...], back_odd_ref[...]).astype(BF16)
    terms = cot[:, :channels]
    grad_own = dot(terms, out_ref[...]).astype(BF16)
    grad_oth = dot(terms, out_other_ref[...]).astype(BF16)

    update_own = jnp.zeros((nodes, width), F32)
    update_oth = jnp.zeros((nodes, width), F32)
    back_own = jnp.zeros((nodes, width), F32)
    back_oth = jnp.zeros((nodes, width), F32)
    sides = ((up_ref, down_ref, keep_ref), (up_other_ref, down_other_ref, give_ref))
    for u_ref, d_ref, o_ref in sides:
        up_own, up_oth = u_ref[pl.ds(first, width), :], u_ref[pl.ds(second, width), :]
        down_own, down_oth = d_ref[:, pl.ds(first, width)], d_ref[:, pl.ds(second, width)]
        hidden = dot(normed[:, :width], up_own) + dot(normed[:, width:], up_oth)
        squash = sigmoid(hidden)
        act = (hidden * squash).astype(BF16)
        update_own += dot(act, down_own)
        update_oth += dot(act, down_oth)
        o_ref[latent : latent + width, :] = dot_rows(act, cot).astype(o_ref.dtype)
        act_grad = dot_last(grad_own, down_own) + dot_last(grad_oth, down_oth)
        pre_grad = (act_grad * squash * (1.0 + hidden * (1.0 - squash))).astype(BF16)
        o_ref[pl.ds(first, width), :] = dot_rows(normed[:, :width], pre_grad).astype(o_ref.dtype)
        o_ref[pl.ds(second, width), :] = dot_rows(normed[:, width:], pre_grad).astype(o_ref.dtype)
        back_own += dot_last(pre_grad, up_own)
        back_oth += dot_last(pre_grad, up_oth)

    back = jnp.concatenate([back_own, back_oth], axis=1)
    slope = (
        back - jnp.mean(back, axis=-1, keepdims=True)
        - norm * jnp.mean(back * norm, axis=-1, keepdims=True)
    ) * inverse
    mesh_half[...] = (grad_own.astype(F32) + slope[:, :width]).reshape(mesh_half.shape)
    mesh_give_ref[...] = (grad_oth.astype(F32) + slope[:, width:]).astype(mesh_give_ref.dtype)
    copy = pltpu.make_async_copy(mesh_half, mesh_ref.at[:, r], mesh_sem)
    copy.start()
    mesh_own = (states[0] + update_own).astype(BF16)
    mesh_oth = (states[1] + update_oth).astype(BF16)
    proj = dot_last(mesh_own, out_ref[...]) + dot_last(mesh_oth, out_other_ref[...])
    proj_ref[...] = jnp.zeros_like(proj_ref)
    proj_ref[:, :channels] = proj.astype(BF16)
    ends = ((keep_ref, mesh_own, local_ref), (give_ref, mesh_oth, local_other_ref))
    start = latent + width
    for o_ref, mesh, local in ends:
        grad = dot_rows(cot, mesh)
        o_ref[start : 2 * latent, :] = grad.astype(o_ref.dtype)
        o_ref[start : start + channels, :] = (grad[:channels] + local[...]).astype(o_ref.dtype)
    copy.wait()


def place_kernel(got_ref, filled_ref, mesh_ref, mesh_half, mesh_sem):
    r = lax.axis_index("rep")
    mesh_half[...] = got_ref[...].astype(F32).reshape(mesh_half.shape)
    copy = pltpu.make_async_copy(mesh_half, mesh_ref.at[:, 1 - r], mesh_sem)
    copy.start()
    copy.wait()


def put_halves(value, step, keep_ref, give_ref, hold):
    rows = keep_ref.shape[0]
    bit = sum_bit(step)
    hold[...] = value
    keep_ref[...] = hold[pl.ds(pl.multiple_of(bit * rows, rows), rows), :].astype(keep_ref.dtype)
    give_ref[...] = hold[pl.ds(pl.multiple_of((1 - bit) * rows, rows), rows), :].astype(
        give_ref.dtype
    )


def terms_kernel(keep_ref, got_ref, *refs):
    outs, hold = refs[:4], refs[4]
    rows = hold.shape[0]
    for chain in range(2):
        part = slice(chain * rows, (chain + 1) * rows)
        put_halves(added(keep_ref[part, :], got_ref[part, :]), 0, *outs[2 * chain :][:2], hold)


def halving_kernel(step, kept_ref, got_ref, *refs):
    keep_ref, give_ref, hold = refs[-3:]
    put_halves(added(kept_ref[...], got_ref[...]), step, keep_ref, give_ref, hold)


def whole_kernel(kept_ref, got_ref, *refs):
    refs[-1][...] = added(kept_ref[...], got_ref[...]).astype(refs[-1].dtype)


def join_kernel(step, mine_ref, got_ref, *refs):
    out_ref = refs[-1]
    rows = mine_ref.shape[0]
    bit = sum_bit(step)
    out_ref[pl.ds(pl.multiple_of(bit * rows, rows), rows), :] = mine_ref[...].astype(out_ref.dtype)
    out_ref[pl.ds(pl.multiple_of((1 - bit) * rows, rows), rows), :] = got_ref[...].astype(
        out_ref.dtype
    )


def finish_outer_kernel(after_ref, mine_ref, other_ref, out_ref, out_other_ref, down_ref, grad_ref):
    r = lax.axis_index("rep")
    low = sum_bit(0) == 0
    width = mine_ref.shape[1]
    channels = out_ref.shape[0]
    mine, other = mine_ref[...], other_ref[...]
    terms = jnp.where(low, mine, other)[:, :channels]
    down_ref[:, pl.ds(pl.multiple_of(r * width, width), width)] = dot(terms, out_ref[...])
    down_ref[:, pl.ds(pl.multiple_of((1 - r) * width, width), width)] = dot(
        terms, out_other_ref[...]
    )
    grad_ref[...] = jnp.where(low, other, mine)[:channels].astype(F32)


def pack_kernel(after_ref, proj_ref, even_ref, odd_ref, out_ref):
    for k, part in enumerate((proj_ref, even_ref, odd_ref)):
        out_ref[k] = part[...]


def hold_kernel(after_ref, value_ref, out_ref):
    out_ref[...] = value_ref[...]


def decode_kernel(device_ref, slot_ref, tiles_ref, base_ref, *refs):
    tables, (out_ref, picked) = refs[:4], refs[4:]
    r = lax.axis_index("rep")
    blocks, rows = picked.shape[:2]
    half = rows // 2
    slots = tables[0].shape[0] // 3
    channels = out_ref.shape[0]
    for i in range(blocks):
        at = entry_of(device_ref, slot_ref, r * blocks + i, slots)
        side = lax.div(at, 2 * slots)
        rest = at - side * 2 * slots
        for east in range(2):
            @pl.when(lax.div(rest, slots) == east)
            def _(i=i, at=side * slots + rest - east * slots, east=east):
                own = pl.ds(pl.multiple_of(r * half, half), half)
                other = pl.ds(pl.multiple_of((1 - r) * half, half), half)
                picked[i, own, :] = tables[east][at]
                picked[i, other, :] = tables[2 + east][at]
    for i in range(blocks):
        cols = slice(i * rows, (i + 1) * rows)
        decoded = dot_last(picked[i].T, tiles_ref[r * blocks + i])
        out_ref[:, cols] = (base_ref[:, cols] + decoded[:channels]).astype(out_ref.dtype)


def along(axis, count, partner):
    pairs = []
    for source in range(count):
        to = partner(source)
        pairs.append((source, to if 0 <= to < count else source))
    return lambda value: lax.ppermute(value, axis, pairs)


def distances(axis):
    found, distance = [], 1
    while distance < lax.axis_size(axis):
        found.append((axis, distance))
        distance *= 2
    return found


def sum_orders():
    lat, lon = distances("lat"), distances("lon")
    return (lon + lat, lat + lon)


def sum_bit(step):
    bits = [
        lax.rem(lax.div(lax.axis_index(axis), distance), 2)
        for axis, distance in (order[step] for order in sum_orders())
    ]
    return jnp.where(lax.axis_index("rep") == 0, bits[0], bits[1])


def sum_swap(value, step):
    lat_count, lon_count = lax.axis_size("lat"), lax.axis_size("lon")
    orders = sum_orders()
    pairs = []
    for lat in range(lat_count):
        for lon in range(lon_count):
            for rep in range(2):
                axis, distance = orders[rep][step]
                to = (lat ^ distance, lon) if axis == "lat" else (lat, lon ^ distance)
                number = lambda a, b: (a * lon_count + b) * 2 + rep
                pairs.append((number(lat, lon), number(*to)))
    return lax.ppermute(value, ("lat", "lon", "rep"), pairs)


def per_device(
    grid_in, w_embed, interp_tiles, route_device, route_slot,
    mesh_embed, w_up, w_down, w_out, cotangent,
):
    lat_count, lon_count = lax.axis_size("lat"), lax.axis_size("lon")
    blocks, tile_rows = interp_tiles.shape[:2]
    grid_rows, channels = grid_in.shape
    my_rows = grid_rows // 2
    width = w_embed.shape[1]
    latent = 2 * width
    padded = -(-channels // 128) * 128
    slots = mesh_embed.shape[0] // tile_rows
    half = tile_rows // 2
    nodes = slots * half

    swap_rep = along("rep", 2, lambda i: 1 - i)
    to_even = along("lat", lat_count, lambda i: i ^ 1)
    to_odd = along("lat", lat_count, lambda i: ((i + 1) ^ 1) - 1)
    east_pairs = [(i, (i + 1) % lon_count) for i in range(lon_count)]
    west_pairs = [(j, i) for i, j in east_pairs]
    to_east = lambda value: lax.ppermute(value, "lon", east_pairs)

    in_hbm = lambda value: pltpu.with_memory_space_constraint(value, pltpu.HBM)
    device, slot = route_device.reshape(blocks), route_slot
    grid_t, cot_t, out_t = grid_in.T, cotangent.T, w_out.T
    routes = (in_hbm(device), in_hbm(slot))
    tiles_in, grid_in_t, cot_in_t = in_hbm(interp_tiles), in_hbm(grid_t), in_hbm(cot_t)
    pair_shape = (2, nodes, width)
    embed_other = swap_rep(w_embed)

    back_own, back_east, back_side = call(
        back_kernel, "back_messages",
        [smem(), smem(), anywhere(), anywhere()],
        [vmem()] * 3,
        [shape_of((nodes, padded), BF16), shape_of((3, nodes, padded), BF16),
         shape_of((2, nodes, padded), BF16)],
        1, 1,
        scratch=[
            pltpu.VMEM((6 * slots, half, padded), F32),
            pltpu.VMEM(interp_tiles.shape, BF16),
            pltpu.VMEM(cot_t.shape, BF16),
            pltpu.SemaphoreType.DMA((STEPS,)),
            pltpu.SemaphoreType.DMA((STEPS,)),
        ],
    )(*routes, tiles_in, cot_in_t)
    back_moved = to_east(back_east)

    def encode(after, weight):
        return call(
            encode_kernel, "encode",
            [smem(), smem(), anywhere()] + [vmem()] * 3,
            [vmem()] * 4,
            [shape_of(pair_shape, BF16)] * 3 + [shape_of((my_rows, width), BF16)],
            1, 1,
            scratch=[
                pltpu.VMEM((6 * slots, half, width), F32), pltpu.VMEM((grid_rows, width), BF16),
            ],
        )(*routes, after, grid_t, interp_tiles, weight)

    own_a, even_a, odd_a, hidden_a = encode(back_own, in_hbm(w_embed))
    even_in_a, odd_in_a = to_even(even_a), to_odd(odd_a)
    own_b, even_b, odd_b, hidden_b = encode(own_a, embed_other)
    even_in_b, odd_in_b = to_even(even_b), to_odd(odd_b)

    out_other, up_other, down_other = swap_rep(out_t), swap_rep(w_up), swap_rep(w_down)
    embed_shape = (slots, 2, half, width)
    mesh_other = swap_rep(mesh_embed)

    second = pl.BlockSpec((1, nodes, width), lambda i: (1, 0, 0))

    def add_east(after, *terms):
        return call(
            add_kernel, "add_east", [anywhere()] * len(after) + [second] * 3, whole((nodes, width)),
            shape_of((nodes, width), BF16), 3 * nodes * width, 6e5, grid=(1,),
        )(*after, *terms)

    send_a = add_east((own_b,), own_a, even_in_a, odd_in_a)
    moved_a = to_east(send_a)

    back_even, back_odd = call(
        sides_kernel, "add_sides", [anywhere(), vmem(), vmem()], [vmem()] * 2,
        [shape_of((nodes, padded), BF16)] * 2, 3 * nodes * width, 1e6,
    )(own_b, back_side, back_moved)
    back_even_in, back_odd_in = to_even(back_even), to_odd(back_odd)

    base, local, local_other = call(
        local_kernel, "local_terms", [anywhere()] * 3 + [vmem()] * 5, [vmem()] * 3,
        [shape_of((channels, my_rows), F32)] + [shape_of((channels, width), F32)] * 2,
        4 * my_rows * latent * channels, 4e6,
    )(moved_a, back_even_in, back_odd_in, hidden_a, hidden_b, cot_t, out_t, out_other)

    send_b = add_east((local,), own_b, even_in_b, odd_in_b)
    moved_b = to_east(send_b)

    first = pl.BlockSpec((1, nodes, width), lambda i: (0, 0, 0))
    sums_specs = [first] * 3 + [whole((nodes, width))]
    weights = (w_up, up_other, w_down, down_other, out_t, out_other)
    back_spec = whole((nodes, padded))
    mesh_scratch = [pltpu.VMEM((slots, half, width), F32), pltpu.SemaphoreType.DMA]
    proj, keep, give, mesh_give, mesh_filled = call(
        node_kernel, "node_update_and_gradients",
        sums_specs * 2 + [whole(embed_shape)] * 2
        + [back_spec, pl.BlockSpec((1, nodes, padded), lambda i: (0, 0, 0)), back_spec, back_spec]
        + [whole((channels, width))] * 2 + [whole(w.shape) for w in weights],
        [whole((nodes, padded))] + [whole((2 * latent, width))] * 2
        + [whole((nodes, width)), anywhere()],
        [shape_of((nodes, padded), BF16), shape_of((2 * latent, width), F32),
         shape_of((2 * latent, width), BF16), shape_of((nodes, width), BF16),
         shape_of(embed_shape, F32)],
        15 * nodes * latent * latent, 9e6, grid=(1,), exps=nodes * latent, scratch=mesh_scratch,
    )(
        own_a, even_in_a, odd_in_a, moved_a, own_b, even_in_b, odd_in_b, moved_b,
        mesh_embed.reshape(embed_shape), mesh_other.reshape(embed_shape),
        back_own, back_moved, back_even_in, back_odd_in, local, local_other, *weights,
    )

    proj_even, proj_odd = to_even(proj), to_odd(proj)
    hold = lambda rows: [pltpu.VMEM((rows, width), F32)]
    up_keep, up_give, outer_keep, outer_give = call(
        terms_kernel, "sum_terms", [vmem()] * 2, [vmem()] * 4,
        [shape_of((width, width), BF16)] * 4, 1, 1, scratch=hold(latent), weight=5e9,
    )(keep, swap_rep(give))

    count = len(sum_orders()[0])
    chains = [[outer_keep, outer_give], [up_keep, up_give]]
    latest = None

    def step_call(kernel, name, chain, step, out_rows, scratch=()):
        kept, given = chain[0], chain[-1]
        after = [latest] if latest is not None else []
        made = call(
            kernel, name, [vmem()] * 2 + [anywhere()] * len(after), [vmem()] * len(out_rows),
            [shape_of((rows, width), BF16) for rows in out_rows], 1, 1, scratch=scratch,
        )(kept, sum_swap(given, step), *after)
        return list(made)

    for step in range(count):
        for c in range(2):
            rows = chains[c][0].shape[0]
            if step == 2 and c == 0:
                trio = call(
                    pack_kernel, "pack_nodes", [anywhere()] + [vmem()] * 3, vmem(),
                    shape_of((3, nodes, padded), BF16), 1, 1,
                )(latest, proj, proj_even, proj_odd)
                east_trio = lax.ppermute(trio, "lon", west_pairs)
            if step == 0:
                chains[c] = step_call(
                    functools.partial(halving_kernel, 1), "halve", chains[c], step,
                    [rows // 2] * 2, hold(rows),
                )
            else:
                chains[c] = step_call(whole_kernel, "add_whole", chains[c], step, [rows])
            latest = chains[c][-1]
    for c in range(2):
        rows = chains[c][0].shape[0]
        chains[c] = step_call(
            functools.partial(join_kernel, 1), "join", chains[c], 1, [2 * rows]
        )
        latest = chains[c][-1]
    (outer_mine,), (up_mine,) = chains
    outer_theirs, up_theirs = sum_swap(outer_mine, 0), sum_swap(up_mine, 0)

    grad_mesh = pl.pallas_call(
        place_kernel,
        in_specs=[vmem(), anywhere()],
        out_specs=anywhere(),
        out_shape=shape_of(embed_shape, F32),
        scratch_shapes=mesh_scratch,
        input_output_aliases={1: 0},
        compiler_params=pltpu.CompilerParams(vmem_limit_bytes=VMEM_BYTES),
        cost_estimate=pl.CostEstimate(flops=1, bytes_accessed=1, transcendentals=0),
        name="place_mesh",
    )(swap_rep(mesh_give), mesh_filled).reshape(mesh_embed.shape)

    table_shape = (3 * slots, half, padded)
    east_trio = call(
        hold_kernel, "hold_nodes", [anywhere(), vmem()], vmem(),
        shape_of((3, nodes, padded), BF16), 1, 1,
    )(outer_mine, east_trio)
    tables = (trio, east_trio, swap_rep(trio), swap_rep(east_trio))
    grid_out_t = call(
        decode_kernel, "decode", [smem()] * 2 + [vmem()] * 6, vmem(),
        shape_of((channels, my_rows), BF16), 1, 1,
        scratch=[pltpu.VMEM((blocks // 2, tile_rows, padded), BF16)],
    )(*routes, interp_tiles, base, *[table.reshape(table_shape) for table in tables])

    grad_down, grad_out = call(
        finish_outer_kernel, "finish_outer", [anywhere()] + [vmem()] * 4, [vmem()] * 2,
        [shape_of((width, latent), F32), shape_of((channels, width), F32)], 1, 1,
    )(in_hbm(grid_out_t), outer_mine, outer_theirs, out_t, out_other)
    grad_up = call(
        functools.partial(join_kernel, 0), "finish_up", [vmem()] * 2 + [anywhere()], vmem(),
        shape_of((latent, width), F32), 1, 1,
    )(up_mine, up_theirs, in_hbm(grid_out_t))
    return (grid_out_t.T, grad_out.T, grad_up, grad_down, grad_mesh)


def solution(mesh):
    patch = ("groups", "lat", "lon")
    placed = (
        P(patch, None),
        P(None, "rep"),
        P(patch, None, None),
        P(patch, None),
        P(patch),
        P(patch, "rep"),
        P(None, "rep"),
        P("rep", None),
        P("rep", None),
        P(patch, None),
    )
    return jax.shard_map(
        per_device,
        mesh=mesh,
        in_specs=placed,
        out_specs=(
            P(("groups", "lat", "lon", "rep"), None),
            P(("groups", "rep"), None),
            P("groups", "rep"),
            P(("groups", "rep"), None),
            P(patch, "rep"),
        ),
        check_vma=False,
    )
```

```python
import functools

import jax
import jax.numpy as jnp
from jax import lax
from jax.experimental import pallas as pl
from jax.experimental.pallas import tpu as pltpu
from jax.sharding import PartitionSpec as P

F32 = jnp.float32
BF16 = jnp.bfloat16
VMEM_BYTES = 20 * 1024 * 1024
STEPS = 4


def dot(left, right):
    return jnp.dot(left, right, preferred_element_type=F32)


def dot_rows(left, right):
    return lax.dot_general(left, right, (((0,), (0,)), ((), ())), preferred_element_type=F32)


def dot_last(left, right):
    return lax.dot_general(left, right, (((1,), (1,)), ((), ())), preferred_element_type=F32)


def sigmoid(values):
    return 0.5 * jnp.tanh(0.5 * values) + 0.5


def vmem():
    return pl.BlockSpec(memory_space=pltpu.VMEM)


def smem():
    return pl.BlockSpec(memory_space=pltpu.SMEM)


def anywhere():
    return pl.BlockSpec(memory_space=pl.ANY)


def whole(shape):
    return pl.BlockSpec(shape, lambda i: (0,) * len(shape))


def shape_of(shape, dtype):
    return jax.ShapeDtypeStruct(shape, dtype)


def call(kernel, name, in_specs, out_specs, out_shape, flops, nbytes, grid=(), scratch=(), exps=0,
         limit=VMEM_BYTES, weight=1):
    return pl.pallas_call(
        kernel,
        grid=grid,
        in_specs=in_specs,
        out_specs=out_specs,
        out_shape=out_shape,
        scratch_shapes=list(scratch),
        compiler_params=pltpu.CompilerParams(vmem_limit_bytes=limit),
        cost_estimate=pl.CostEstimate(flops=int(weight), bytes_accessed=1, transcendentals=0),
        name=name,
    )


def node_half(tile, r):
    half = tile.shape[1] // 2
    return jnp.where(r == 0, tile[:, :half], tile[:, half:]).T


def entry_of(device_ref, slot_ref, b, slots):
    lon_count = lax.axis_size("lon")
    lat, lon = lax.axis_index("lat"), lax.axis_index("lon")
    target = device_ref[b]
    band = lax.div(target, lon_count)
    sector = target - band * lon_count - lon
    sector = jnp.where(sector < 0, sector + lon_count, sector)
    step = band - lat
    even_step = 1 - 2 * lax.rem(lat, 2)
    side = jnp.where(step == 0, 0, jnp.where(step == even_step, 1, 2))
    return (side * 2 + sector) * slots + slot_ref[b]


def write_packed(total, outs):
    per = total.shape[0] // 3
    for k, out in enumerate(outs):
        block = total[k * per : (k + 1) * per]
        out[...] = block.reshape(out.shape).astype(out.dtype)


def back_kernel(
    device_ref, slot_ref, tiles_ref, cot_ref, own_ref, east_ref, side_ref,
    total, tiles, cots, tile_sems, cot_sems,
):
    blocks, rows = tiles.shape[0], tiles.shape[1]
    count = blocks // STEPS
    slots = total.shape[0] // 6
    channels = cots.shape[0]
    r = lax.axis_index("rep")
    copies = []
    for k in range(STEPS):
        part = pl.ds(k * count, count)
        cols = pl.ds(k * count * rows, count * rows)
        copies.append((
            pltpu.make_async_copy(tiles_ref.at[part], tiles.at[part], tile_sems.at[k]),
            pltpu.make_async_copy(cot_ref.at[:, cols], cots.at[:, cols], cot_sems.at[k]),
        ))
        for copy in copies[-1]:
            copy.start()
    total[...] = jnp.zeros_like(total)
    for b in range(blocks):
        if b % count == 0:
            for copy in copies[b // count]:
                copy.wait()
        at = entry_of(device_ref, slot_ref, b, slots)
        cot = cots[:, b * rows : (b + 1) * rows]
        total[at, :, :channels] += dot_last(node_half(tiles[b], r), cot)
    for k, out in ((0, own_ref), (2, side_ref.at[0]), (4, side_ref.at[1])):
        out[...] = total[k * slots : (k + 1) * slots].reshape(out.shape).astype(out.dtype)
    for k in range(3):
        block = total[(2 * k + 1) * slots : (2 * k + 2) * slots]
        east_ref[k] = block.reshape(east_ref.shape[1:]).astype(east_ref.dtype)


def encode_kernel(
    device_ref, slot_ref, after_ref, grid_ref, tiles_ref, weight_ref,
    own_ref, even_ref, odd_ref, hidden_ref, total, hold,
):
    blocks, rows = tiles_ref.shape[:2]
    slots = total.shape[0] // 6
    step_rows = blocks * rows // STEPS
    r = lax.axis_index("rep")
    total[...] = jnp.zeros_like(total)
    for k in range(STEPS):
        preact = dot_rows(grid_ref[:, k * step_rows : (k + 1) * step_rows], weight_ref[...])
        hold[k * step_rows : (k + 1) * step_rows, :] = (preact * sigmoid(preact)).astype(BF16)
        for b in range(k * blocks // STEPS, (k + 1) * blocks // STEPS):
            at = entry_of(device_ref, slot_ref, b, slots)
            total[at] += dot(node_half(tiles_ref[b], r), hold[b * rows : (b + 1) * rows, :])
    mine = hidden_ref.shape[0]
    hidden_ref[...] = hold[pl.ds(pl.multiple_of(r * mine, mine), mine), :]
    write_packed(total, (own_ref, even_ref, odd_ref))


def local_kernel(
    own_ref, oth_ref, cot_ref, out_ref, out_other_ref,
    base_ref, grad_ref, grad_other_ref,
):
    rows = own_ref.shape[0]
    r = lax.axis_index("rep")
    cot = cot_ref[:, pl.ds(pl.multiple_of(r * rows, rows), rows)]
    base_ref[...] = dot_last(out_ref[...], own_ref[...]) + dot_last(out_other_ref[...], oth_ref[...])
    grad_ref[...] = dot(cot, own_ref[...])
    grad_other_ref[...] = dot(cot, oth_ref[...])


def added(*values):
    total = values[0].astype(F32)
    for value in values[1:]:
        total = total + value.astype(F32)
    return total


def add_kernel(*refs):
    a, b, c, out = refs[-4:]
    out[...] = added(a[0], b[0], c[0]).astype(out.dtype)


def sides_kernel(after_ref, side_ref, moved_ref, even_ref, odd_ref):
    even_ref[...] = added(side_ref[0], moved_ref[1]).astype(even_ref.dtype)
    odd_ref[...] = added(side_ref[1], moved_ref[2]).astype(odd_ref.dtype)


def node_kernel(
    own_a, even_a, odd_a, moved_a, own_b, even_b, odd_b, moved_b, embed_ref, embed_other_ref,
    back_ref, back_moved_ref, back_even_ref, back_odd_ref, local_ref, local_other_ref,
    up_ref, up_other_ref, down_ref, down_other_ref, out_ref, out_other_ref,
    proj_ref, keep_ref, give_ref, mesh_give_ref, mesh_ref, mesh_half, mesh_sem,
):
    r = lax.axis_index("rep")
    nodes, width = moved_a.shape
    latent = 2 * width
    channels = out_ref.shape[0]
    first = pl.multiple_of(r * width, width)
    second = pl.multiple_of((1 - r) * width, width)
    states = []
    for embed, parts in (
        (embed_ref, (own_a[0], even_a[0], odd_a[0], moved_a[...])),
        (embed_other_ref, (own_b[0], even_b[0], odd_b[0], moved_b[...])),
    ):
        start = embed[:, r].reshape(nodes, width)
        states.append((start.astype(F32) + added(*parts)).astype(BF16).astype(F32))
    state = jnp.concatenate(states, axis=1)
    centered = state - jnp.mean(state, axis=-1, keepdims=True)
    inverse = lax.rsqrt(jnp.mean(centered * centered, axis=-1, keepdims=True) + 1e-05)
    norm = centered * inverse
    normed = norm.astype(BF16)

    cot = added(back_ref[...], back_moved_ref[0], back_even_ref[...], back_odd_ref[...]).astype(BF16)
    terms = cot[:, :channels]
    grad_own = dot(terms, out_ref[...]).astype(BF16)
    grad_oth = dot(terms, out_other_ref[...]).astype(BF16)

    update_own = jnp.zeros((nodes, width), F32)
    update_oth = jnp.zeros((nodes, width), F32)
    back_own = jnp.zeros((nodes, width), F32)
    back_oth = jnp.zeros((nodes, width), F32)
    sides = ((up_ref, down_ref, keep_ref), (up_other_ref, down_other_ref, give_ref))
    for u_ref, d_ref, o_ref in sides:
        up_own, up_oth = u_ref[pl.ds(first, width), :], u_ref[pl.ds(second, width), :]
        down_own, down_oth = d_ref[:, pl.ds(first, width)], d_ref[:, pl.ds(second, width)]
        hidden = dot(normed[:, :width], up_own) + dot(normed[:, width:], up_oth)
        squash = sigmoid(hidden)
        act = (hidden * squash).astype(BF16)
        update_own += dot(act, down_own)
        update_oth += dot(act, down_oth)
        o_ref[latent : latent + width, :] = dot_rows(act, cot).astype(o_ref.dtype)
        act_grad = dot_last(grad_own, down_own) + dot_last(grad_oth, down_oth)
        pre_grad = (act_grad * squash * (1.0 + hidden * (1.0 - squash))).astype(BF16)
        o_ref[pl.ds(first, width), :] = dot_rows(normed[:, :width], pre_grad).astype(o_ref.dtype)
        o_ref[pl.ds(second, width), :] = dot_rows(normed[:, width:], pre_grad).astype(o_ref.dtype)
        back_own += dot_last(pre_grad, up_own)
        back_oth += dot_last(pre_grad, up_oth)

    mesh_own = (states[0] + update_own).astype(BF16)
    mesh_oth = (states[1] + update_oth).astype(BF16)
    proj = dot_last(mesh_own, out_ref[...]) + dot_last(mesh_oth, out_other_ref[...])
    proj_ref[...] = jnp.zeros_like(proj_ref)
    proj_ref[:, :channels] = proj.astype(BF16)
    ends = ((keep_ref, mesh_own, local_ref), (give_ref, mesh_oth, local_other_ref))
    start = latent + width
    for o_ref, mesh, local in ends:
        grad = dot_rows(cot, mesh)
        o_ref[start : 2 * latent, :] = grad.astype(o_ref.dtype)
        o_ref[start : start + channels, :] = (grad[:channels] + local[...]).astype(o_ref.dtype)

    back = jnp.concatenate([back_own, back_oth], axis=1)
    slope = (
        back - jnp.mean(back, axis=-1, keepdims=True)
        - norm * jnp.mean(back * norm, axis=-1, keepdims=True)
    ) * inverse
    mesh_half[...] = (grad_own.astype(F32) + slope[:, :width]).reshape(mesh_half.shape)
    mesh_give_ref[...] = (grad_oth.astype(F32) + slope[:, width:]).astype(mesh_give_ref.dtype)
    copy = pltpu.make_async_copy(mesh_half, mesh_ref.at[:, r], mesh_sem)
    copy.start()
    copy.wait()


def place_kernel(got_ref, filled_ref, mesh_ref, mesh_half, mesh_sem):
    r = lax.axis_index("rep")
    mesh_half[...] = got_ref[...].astype(F32).reshape(mesh_half.shape)
    copy = pltpu.make_async_copy(mesh_half, mesh_ref.at[:, 1 - r], mesh_sem)
    copy.start()
    copy.wait()


def put_halves(value, step, keep_ref, give_ref, hold):
    rows = keep_ref.shape[0]
    bit = sum_bit(step)
    hold[...] = value
    keep_ref[...] = hold[pl.ds(pl.multiple_of(bit * rows, rows), rows), :].astype(keep_ref.dtype)
    give_ref[...] = hold[pl.ds(pl.multiple_of((1 - bit) * rows, rows), rows), :].astype(
        give_ref.dtype
    )


def terms_kernel(keep_ref, got_ref, *refs):
    outs, hold = refs[:4], refs[4]
    rows = hold.shape[0]
    for chain in range(2):
        part = slice(chain * rows, (chain + 1) * rows)
        put_halves(added(keep_ref[part, :], got_ref[part, :]), 0, *outs[2 * chain :][:2], hold)


def halving_kernel(step, kept_ref, got_ref, *refs):
    keep_ref, give_ref, hold = refs[-3:]
    put_halves(added(kept_ref[...], got_ref[...]), step, keep_ref, give_ref, hold)


def whole_kernel(kept_ref, got_ref, *refs):
    refs[-1][...] = added(kept_ref[...], got_ref[...]).astype(refs[-1].dtype)


def join_kernel(step, mine_ref, got_ref, *refs):
    out_ref = refs[-1]
    rows = mine_ref.shape[0]
    bit = sum_bit(step)
    out_ref[pl.ds(pl.multiple_of(bit * rows, rows), rows), :] = mine_ref[...].astype(out_ref.dtype)
    out_ref[pl.ds(pl.multiple_of((1 - bit) * rows, rows), rows), :] = got_ref[...].astype(
        out_ref.dtype
    )


def finish_outer_kernel(after_ref, mine_ref, other_ref, out_ref, out_other_ref, down_ref, grad_ref):
    r = lax.axis_index("rep")
    low = sum_bit(0) == 0
    width = mine_ref.shape[1]
    channels = out_ref.shape[0]
    mine, other = mine_ref[...], other_ref[...]
    terms = jnp.where(low, mine, other)[:, :channels]
    down_ref[:, pl.ds(pl.multiple_of(r * width, width), width)] = dot(terms, out_ref[...])
    down_ref[:, pl.ds(pl.multiple_of((1 - r) * width, width), width)] = dot(
        terms, out_other_ref[...]
    )
    grad_ref[...] = jnp.where(low, other, mine)[:channels].astype(F32)


def pack_kernel(after_ref, proj_ref, even_ref, odd_ref, out_ref):
    for k, part in enumerate((proj_ref, even_ref, odd_ref)):
        out_ref[k] = part[...]


def pick_kernel(device_ref, slot_ref, after_ref, own_ref, east_ref, mine_ref, theirs_ref):
    r = lax.axis_index("rep")
    blocks = mine_ref.shape[0]
    slots = own_ref.shape[0] // 3
    for out_ref, first in ((mine_ref, r * blocks), (theirs_ref, (1 - r) * blocks)):
        for i in range(blocks):
            at = entry_of(device_ref, slot_ref, first + i, slots)
            side = lax.div(at, 2 * slots)
            rest = at - side * 2 * slots

            @pl.when(rest < slots)
            def _(i=i, at=side * slots + rest, out_ref=out_ref):
                out_ref[i] = own_ref[at]

            @pl.when(rest >= slots)
            def _(i=i, at=side * slots + rest - slots, out_ref=out_ref):
                out_ref[i] = east_ref[at]


def decode_kernel(tiles_ref, base_ref, mine_ref, got_ref, out_ref, picked):
    r = lax.axis_index("rep")
    blocks, half = mine_ref.shape[:2]
    rows = tiles_ref.shape[1]
    channels = out_ref.shape[0]
    own = pl.ds(pl.multiple_of(r * half, half), half)
    other = pl.ds(pl.multiple_of((1 - r) * half, half), half)
    for i in range(blocks):
        picked[i, own, :] = mine_ref[i]
        picked[i, other, :] = got_ref[i]
    for i in range(blocks):
        cols = slice(i * rows, (i + 1) * rows)
        decoded = dot_last(picked[i].T, tiles_ref[r * blocks + i])
        out_ref[:, cols] = (base_ref[:, cols] + decoded[:channels]).astype(out_ref.dtype)


def along(axis, count, partner):
    pairs = []
    for source in range(count):
        to = partner(source)
        pairs.append((source, to if 0 <= to < count else source))
    return lambda value: lax.ppermute(value, axis, pairs)


def distances(axis):
    found, distance = [], 1
    while distance < lax.axis_size(axis):
        found.append((axis, distance))
        distance *= 2
    return found


def sum_orders():
    lat, lon = distances("lat"), distances("lon")
    return (lon + lat, lat + lon)


def sum_bit(step):
    bits = [
        lax.rem(lax.div(lax.axis_index(axis), distance), 2)
        for axis, distance in (order[step] for order in sum_orders())
    ]
    return jnp.where(lax.axis_index("rep") == 0, bits[0], bits[1])


def sum_swap(value, step):
    lat_count, lon_count = lax.axis_size("lat"), lax.axis_size("lon")
    orders = sum_orders()
    pairs = []
    for lat in range(lat_count):
        for lon in range(lon_count):
            for rep in range(2):
                axis, distance = orders[rep][step]
                to = (lat ^ distance, lon) if axis == "lat" else (lat, lon ^ distance)
                number = lambda a, b: (a * lon_count + b) * 2 + rep
                pairs.append((number(lat, lon), number(*to)))
    return lax.ppermute(value, ("lat", "lon", "rep"), pairs)


def per_device(
    grid_in, w_embed, interp_tiles, route_device, route_slot,
    mesh_embed, w_up, w_down, w_out, cotangent,
):
    lat_count, lon_count = lax.axis_size("lat"), lax.axis_size("lon")
    blocks, tile_rows = interp_tiles.shape[:2]
    grid_rows, channels = grid_in.shape
    my_rows = grid_rows // 2
    width = w_embed.shape[1]
    latent = 2 * width
    padded = -(-channels // 128) * 128
    slots = mesh_embed.shape[0] // tile_rows
    half = tile_rows // 2
    nodes = slots * half

    swap_rep = along("rep", 2, lambda i: 1 - i)
    to_even = along("lat", lat_count, lambda i: i ^ 1)
    to_odd = along("lat", lat_count, lambda i: ((i + 1) ^ 1) - 1)
    east_pairs = [(i, (i + 1) % lon_count) for i in range(lon_count)]
    west_pairs = [(j, i) for i, j in east_pairs]
    to_east = lambda value: lax.ppermute(value, "lon", east_pairs)

    in_hbm = lambda value: pltpu.with_memory_space_constraint(value, pltpu.HBM)
    device, slot = route_device.reshape(blocks), route_slot
    grid_t, cot_t, out_t = grid_in.T, cotangent.T, w_out.T
    routes = (in_hbm(device), in_hbm(slot))
    tiles_in, grid_in_t, cot_in_t = in_hbm(interp_tiles), in_hbm(grid_t), in_hbm(cot_t)
    pair_shape = (2, nodes, width)
    embed_other = swap_rep(w_embed)

    back_own, back_east, back_side = call(
        back_kernel, "back_messages",
        [smem(), smem(), anywhere(), anywhere()],
        [vmem()] * 3,
        [shape_of((nodes, padded), BF16), shape_of((3, nodes, padded), BF16),
         shape_of((2, nodes, padded), BF16)],
        1, 1,
        scratch=[
            pltpu.VMEM((6 * slots, half, padded), F32),
            pltpu.VMEM(interp_tiles.shape, BF16),
            pltpu.VMEM(cot_t.shape, BF16),
            pltpu.SemaphoreType.DMA((STEPS,)),
            pltpu.SemaphoreType.DMA((STEPS,)),
        ],
    )(*routes, tiles_in, cot_in_t)
    back_moved = to_east(back_east)

    def encode(after, weight):
        return call(
            encode_kernel, "encode",
            [smem(), smem(), anywhere()] + [vmem()] * 3,
            [vmem()] * 4,
            [shape_of(pair_shape, BF16)] * 3 + [shape_of((my_rows, width), BF16)],
            1, 1,
            scratch=[
                pltpu.VMEM((6 * slots, half, width), F32), pltpu.VMEM((grid_rows, width), BF16),
            ],
        )(*routes, after, grid_t, interp_tiles, weight)

    own_a, even_a, odd_a, hidden_a = encode(back_own, in_hbm(w_embed))
    even_in_a, odd_in_a = to_even(even_a), to_odd(odd_a)
    own_b, even_b, odd_b, hidden_b = encode(own_a, embed_other)
    even_in_b, odd_in_b = to_even(even_b), to_odd(odd_b)

    out_other, up_other, down_other = swap_rep(out_t), swap_rep(w_up), swap_rep(w_down)
    embed_shape = (slots, 2, half, width)
    mesh_other = swap_rep(mesh_embed)

    second = pl.BlockSpec((1, nodes, width), lambda i: (1, 0, 0))

    def add_east(after, *terms):
        return call(
            add_kernel, "add_east", [anywhere()] * len(after) + [second] * 3, whole((nodes, width)),
            shape_of((nodes, width), BF16), 3 * nodes * width, 6e5, grid=(1,),
        )(*after, *terms)

    send_a = add_east((back_moved,), own_a, even_in_a, odd_in_a)
    moved_a = to_east(send_a)

    base, local, local_other = call(
        local_kernel, "local_terms", [vmem()] * 5, [vmem()] * 3,
        [shape_of((channels, my_rows), F32)] + [shape_of((channels, width), F32)] * 2,
        4 * my_rows * latent * channels, 4e6,
    )(hidden_a, hidden_b, cot_t, out_t, out_other)

    send_b = add_east((moved_a,), own_b, even_in_b, odd_in_b)
    moved_b = to_east(send_b)

    back_even, back_odd = call(
        sides_kernel, "add_sides", [anywhere(), vmem(), vmem()], [vmem()] * 2,
        [shape_of((nodes, padded), BF16)] * 2, 3 * nodes * width, 1e6,
    )(send_b, back_side, back_moved)
    back_even_in, back_odd_in = to_even(back_even), to_odd(back_odd)

    first = pl.BlockSpec((1, nodes, width), lambda i: (0, 0, 0))
    sums_specs = [first] * 3 + [whole((nodes, width))]
    weights = (w_up, up_other, w_down, down_other, out_t, out_other)
    back_spec = whole((nodes, padded))
    mesh_scratch = [pltpu.VMEM((slots, half, width), F32), pltpu.SemaphoreType.DMA]
    proj, keep, give, mesh_give, mesh_filled = call(
        node_kernel, "node_update_and_gradients",
        sums_specs * 2 + [whole(embed_shape)] * 2
        + [back_spec, pl.BlockSpec((1, nodes, padded), lambda i: (0, 0, 0)), back_spec, back_spec]
        + [whole((channels, width))] * 2 + [whole(w.shape) for w in weights],
        [whole((nodes, padded))] + [whole((2 * latent, width))] * 2
        + [whole((nodes, width)), anywhere()],
        [shape_of((nodes, padded), BF16), shape_of((2 * latent, width), F32),
         shape_of((2 * latent, width), BF16), shape_of((nodes, width), BF16),
         shape_of(embed_shape, F32)],
        15 * nodes * latent * latent, 9e6, grid=(1,), exps=nodes * latent, scratch=mesh_scratch,
    )(
        own_a, even_in_a, odd_in_a, moved_a, own_b, even_in_b, odd_in_b, moved_b,
        mesh_embed.reshape(embed_shape), mesh_other.reshape(embed_shape),
        back_own, back_moved, back_even_in, back_odd_in, local, local_other, *weights,
    )

    proj_even, proj_odd = to_even(proj), to_odd(proj)
    hold = lambda rows: [pltpu.VMEM((rows, width), F32)]
    up_keep, up_give, outer_keep, outer_give = call(
        terms_kernel, "sum_terms", [vmem()] * 2, [vmem()] * 4,
        [shape_of((width, width), BF16)] * 4, 1, 1, scratch=hold(latent), weight=5e9,
    )(keep, swap_rep(give))

    count = len(sum_orders()[0])
    chains = [[outer_keep, outer_give], [up_keep, up_give]]
    latest = None

    def step_call(kernel, name, chain, step, out_rows, scratch=()):
        kept, given = chain[0], chain[-1]
        after = [latest] if latest is not None else [proj_even, proj_odd]
        made = call(
            kernel, name, [vmem()] * 2 + [anywhere()] * len(after), [vmem()] * len(out_rows),
            [shape_of((rows, width), BF16) for rows in out_rows], 1, 1, scratch=scratch,
        )(kept, sum_swap(given, step), *after)
        return list(made)

    for step in range(count):
        for c in range(2):
            rows = chains[c][0].shape[0]
            if step == 1 and c == 0:
                trio = call(
                    pack_kernel, "pack_nodes", [anywhere()] + [vmem()] * 3, vmem(),
                    shape_of((3, nodes, padded), BF16), 1, 1,
                )(latest, proj, proj_even, proj_odd)
                east_trio = lax.ppermute(trio, "lon", west_pairs)
            if step == 0:
                chains[c] = step_call(
                    functools.partial(halving_kernel, 1), "halve", chains[c], step,
                    [rows // 2] * 2, hold(rows),
                )
            else:
                chains[c] = step_call(whole_kernel, "add_whole", chains[c], step, [rows])
            latest = chains[c][-1]
    after_pick = chains[1][-1]
    for c in range(2):
        rows = chains[c][0].shape[0]
        chains[c] = step_call(
            functools.partial(join_kernel, 1), "join", chains[c], 1, [2 * rows]
        )
        latest = chains[c][-1]
    (outer_mine,), (up_mine,) = chains
    outer_theirs, up_theirs = sum_swap(outer_mine, 0), sum_swap(up_mine, 0)

    grad_mesh = pl.pallas_call(
        place_kernel,
        in_specs=[vmem(), anywhere()],
        out_specs=anywhere(),
        out_shape=shape_of(embed_shape, F32),
        scratch_shapes=mesh_scratch,
        input_output_aliases={1: 0},
        compiler_params=pltpu.CompilerParams(vmem_limit_bytes=VMEM_BYTES),
        cost_estimate=pl.CostEstimate(flops=1, bytes_accessed=1, transcendentals=0),
        name="place_mesh",
    )(swap_rep(mesh_give), mesh_filled).reshape(mesh_embed.shape)

    table_shape = (3 * slots, half, padded)
    mine_picked, theirs_picked = call(
        pick_kernel, "pick_nodes", [smem()] * 2 + [anywhere()] + [vmem()] * 2, [vmem()] * 2,
        [shape_of((blocks // 2, half, padded), BF16)] * 2, 1, 1,
    )(*routes, after_pick, trio.reshape(table_shape), east_trio.reshape(table_shape))
    grid_out_t = call(
        decode_kernel, "decode", [vmem()] * 4, vmem(),
        shape_of((channels, my_rows), BF16), 2 * my_rows * tile_rows * padded, 4e6,
        scratch=[pltpu.VMEM((blocks // 2, tile_rows, padded), BF16)],
    )(interp_tiles, base, mine_picked, swap_rep(theirs_picked))

    grad_down, grad_out = call(
        finish_outer_kernel, "finish_outer", [anywhere()] + [vmem()] * 4, [vmem()] * 2,
        [shape_of((width, latent), F32), shape_of((channels, width), F32)], 1, 1,
    )(in_hbm(grid_out_t), outer_mine, outer_theirs, out_t, out_other)
    grad_up = call(
        functools.partial(join_kernel, 0), "finish_up", [vmem()] * 2 + [anywhere()], vmem(),
        shape_of((latent, width), F32), 1, 1,
    )(up_mine, up_theirs, in_hbm(grid_out_t))
    return (grid_out_t.T, grad_out.T, grad_up, grad_down, grad_mesh)


def solution(mesh):
    patch = ("groups", "lat", "lon")
    placed = (
        P(patch, None),
        P(None, "rep"),
        P(patch, None, None),
        P(patch, None),
        P(patch),
        P(patch, "rep"),
        P(None, "rep"),
        P("rep", None),
        P("rep", None),
        P(patch, None),
    )
    return jax.shard_map(
        per_device,
        mesh=mesh,
        in_specs=placed,
        out_specs=(
            P(("groups", "lat", "lon", "rep"), None),
            P(("groups", "rep"), None),
            P("groups", "rep"),
            P(("groups", "rep"), None),
            P(patch, "rep"),
        ),
        check_vma=False,
    )
```

```python
import functools

import jax
import jax.numpy as jnp
from jax import lax
from jax.experimental import pallas as pl
from jax.experimental.pallas import tpu as pltpu
from jax.sharding import PartitionSpec as P

F32 = jnp.float32
BF16 = jnp.bfloat16
VMEM_BYTES = 20 * 1024 * 1024
STEPS = 4


def dot(left, right):
    return jnp.dot(left, right, preferred_element_type=F32)


def dot_rows(left, right):
    return lax.dot_general(left, right, (((0,), (0,)), ((), ())), preferred_element_type=F32)


def dot_last(left, right):
    return lax.dot_general(left, right, (((1,), (1,)), ((), ())), preferred_element_type=F32)


def sigmoid(values):
    return 0.5 * jnp.tanh(0.5 * values) + 0.5


def vmem():
    return pl.BlockSpec(memory_space=pltpu.VMEM)


def smem():
    return pl.BlockSpec(memory_space=pltpu.SMEM)


def anywhere():
    return pl.BlockSpec(memory_space=pl.ANY)


def whole(shape):
    return pl.BlockSpec(shape, lambda i: (0,) * len(shape))


def shape_of(shape, dtype):
    return jax.ShapeDtypeStruct(shape, dtype)


def call(kernel, name, in_specs, out_specs, out_shape, flops, nbytes, grid=(), scratch=(), exps=0,
         limit=VMEM_BYTES, weight=1):
    return pl.pallas_call(
        kernel,
        grid=grid,
        in_specs=in_specs,
        out_specs=out_specs,
        out_shape=out_shape,
        scratch_shapes=list(scratch),
        compiler_params=pltpu.CompilerParams(vmem_limit_bytes=limit),
        cost_estimate=pl.CostEstimate(flops=int(weight), bytes_accessed=1, transcendentals=0),
        name=name,
    )


def node_half(tile, r):
    half = tile.shape[1] // 2
    return jnp.where(r == 0, tile[:, :half], tile[:, half:]).T


def entry_of(device_ref, slot_ref, b, slots):
    lon_count = lax.axis_size("lon")
    lat, lon = lax.axis_index("lat"), lax.axis_index("lon")
    target = device_ref[b]
    band = lax.div(target, lon_count)
    sector = target - band * lon_count - lon
    sector = jnp.where(sector < 0, sector + lon_count, sector)
    step = band - lat
    even_step = 1 - 2 * lax.rem(lat, 2)
    side = jnp.where(step == 0, 0, jnp.where(step == even_step, 1, 2))
    return (side * 2 + sector) * slots + slot_ref[b]


def write_packed(total, outs):
    per = total.shape[0] // 3
    for k, out in enumerate(outs):
        block = total[k * per : (k + 1) * per]
        out[...] = block.reshape(out.shape).astype(out.dtype)


def back_kernel(
    device_ref, slot_ref, tiles_ref, cot_ref, own_ref, east_ref, side_ref,
    total, tiles, cots, tile_sems, cot_sems,
):
    blocks, rows = tiles.shape[0], tiles.shape[1]
    count = blocks // STEPS
    slots = total.shape[0] // 6
    channels = cots.shape[0]
    r = lax.axis_index("rep")
    copies = []
    for k in range(STEPS):
        part = pl.ds(k * count, count)
        cols = pl.ds(k * count * rows, count * rows)
        copies.append((
            pltpu.make_async_copy(tiles_ref.at[part], tiles.at[part], tile_sems.at[k]),
            pltpu.make_async_copy(cot_ref.at[:, cols], cots.at[:, cols], cot_sems.at[k]),
        ))
        for copy in copies[-1]:
            copy.start()
    total[...] = jnp.zeros_like(total)
    for b in range(blocks):
        if b % count == 0:
            for copy in copies[b // count]:
                copy.wait()
        at = entry_of(device_ref, slot_ref, b, slots)
        cot = cots[:, b * rows : (b + 1) * rows]
        total[at, :, :channels] += dot_last(node_half(tiles[b], r), cot)
    for k, out in ((0, own_ref), (2, side_ref.at[0]), (4, side_ref.at[1])):
        out[...] = total[k * slots : (k + 1) * slots].reshape(out.shape).astype(out.dtype)
    for k in range(3):
        block = total[(2 * k + 1) * slots : (2 * k + 2) * slots]
        east_ref[k] = block.reshape(east_ref.shape[1:]).astype(east_ref.dtype)


def encode_kernel(
    device_ref, slot_ref, after_ref, grid_ref, tiles_ref, weight_ref,
    own_ref, even_ref, odd_ref, hidden_ref, total, hold,
):
    blocks, rows = tiles_ref.shape[:2]
    slots = total.shape[0] // 6
    step_rows = blocks * rows // STEPS
    r = lax.axis_index("rep")
    total[...] = jnp.zeros_like(total)
    for k in range(STEPS):
        preact = dot_rows(grid_ref[:, k * step_rows : (k + 1) * step_rows], weight_ref[...])
        hold[k * step_rows : (k + 1) * step_rows, :] = (preact * sigmoid(preact)).astype(BF16)
        for b in range(k * blocks // STEPS, (k + 1) * blocks // STEPS):
            at = entry_of(device_ref, slot_ref, b, slots)
            total[at] += dot(node_half(tiles_ref[b], r), hold[b * rows : (b + 1) * rows, :])
    mine = hidden_ref.shape[0]
    hidden_ref[...] = hold[pl.ds(pl.multiple_of(r * mine, mine), mine), :]
    write_packed(total, (own_ref, even_ref, odd_ref))


def local_kernel(
    own_ref, oth_ref, cot_ref, out_ref, out_other_ref,
    base_ref, grad_ref, grad_other_ref,
):
    rows = own_ref.shape[0]
    r = lax.axis_index("rep")
    cot = cot_ref[:, pl.ds(pl.multiple_of(r * rows, rows), rows)]
    base_ref[...] = dot_last(out_ref[...], own_ref[...]) + dot_last(out_other_ref[...], oth_ref[...])
    grad_ref[...] = dot(cot, own_ref[...])
    grad_other_ref[...] = dot(cot, oth_ref[...])


def added(*values):
    total = values[0].astype(F32)
    for value in values[1:]:
        total = total + value.astype(F32)
    return total


def add_kernel(*refs):
    a, b, c, out = refs[-4:]
    out[...] = added(a[0], b[0], c[0]).astype(out.dtype)


def sides_kernel(after_ref, side_ref, moved_ref, even_ref, odd_ref):
    even_ref[...] = added(side_ref[0], moved_ref[1]).astype(even_ref.dtype)
    odd_ref[...] = added(side_ref[1], moved_ref[2]).astype(odd_ref.dtype)


def node_kernel(
    own_a, even_a, odd_a, moved_a, own_b, even_b, odd_b, moved_b, embed_ref, embed_other_ref,
    back_ref, back_moved_ref, back_even_ref, back_odd_ref, local_ref, local_other_ref,
    up_ref, up_other_ref, down_ref, down_other_ref, out_ref, out_other_ref,
    proj_ref, keep_ref, give_ref, mesh_give_ref, mesh_ref, mesh_half, mesh_sem,
):
    r = lax.axis_index("rep")
    nodes, width = moved_a.shape
    latent = 2 * width
    channels = out_ref.shape[0]
    first = pl.multiple_of(r * width, width)
    second = pl.multiple_of((1 - r) * width, width)
    states = []
    for embed, parts in (
        (embed_ref, (own_a[0], even_a[0], odd_a[0], moved_a[...])),
        (embed_other_ref, (own_b[0], even_b[0], odd_b[0], moved_b[...])),
    ):
        start = embed[:, r].reshape(nodes, width)
        states.append((start.astype(F32) + added(*parts)).astype(BF16).astype(F32))
    state = jnp.concatenate(states, axis=1)
    centered = state - jnp.mean(state, axis=-1, keepdims=True)
    inverse = lax.rsqrt(jnp.mean(centered * centered, axis=-1, keepdims=True) + 1e-05)
    norm = centered * inverse
    normed = norm.astype(BF16)

    cot = added(back_ref[...], back_moved_ref[0], back_even_ref[...], back_odd_ref[...]).astype(BF16)
    terms = cot[:, :channels]
    grad_own = dot(terms, out_ref[...]).astype(BF16)
    grad_oth = dot(terms, out_other_ref[...]).astype(BF16)

    update_own = jnp.zeros((nodes, width), F32)
    update_oth = jnp.zeros((nodes, width), F32)
    back_own = jnp.zeros((nodes, width), F32)
    back_oth = jnp.zeros((nodes, width), F32)
    sides = ((up_ref, down_ref, keep_ref), (up_other_ref, down_other_ref, give_ref))
    for u_ref, d_ref, o_ref in sides:
        up_own, up_oth = u_ref[pl.ds(first, width), :], u_ref[pl.ds(second, width), :]
        down_own, down_oth = d_ref[:, pl.ds(first, width)], d_ref[:, pl.ds(second, width)]
        hidden = dot(normed[:, :width], up_own) + dot(normed[:, width:], up_oth)
        squash = sigmoid(hidden)
        act = (hidden * squash).astype(BF16)
        update_own += dot(act, down_own)
        update_oth += dot(act, down_oth)
        o_ref[latent : latent + width, :] = dot_rows(act, cot).astype(o_ref.dtype)
        act_grad = dot_last(grad_own, down_own) + dot_last(grad_oth, down_oth)
        pre_grad = (act_grad * squash * (1.0 + hidden * (1.0 - squash))).astype(BF16)
        o_ref[pl.ds(first, width), :] = dot_rows(normed[:, :width], pre_grad).astype(o_ref.dtype)
        o_ref[pl.ds(second, width), :] = dot_rows(normed[:, width:], pre_grad).astype(o_ref.dtype)
        back_own += dot_last(pre_grad, up_own)
        back_oth += dot_last(pre_grad, up_oth)

    mesh_own = (states[0] + update_own).astype(BF16)
    mesh_oth = (states[1] + update_oth).astype(BF16)
    proj = dot_last(mesh_own, out_ref[...]) + dot_last(mesh_oth, out_other_ref[...])
    proj_ref[...] = jnp.zeros_like(proj_ref)
    proj_ref[:, :channels] = proj.astype(BF16)
    ends = ((keep_ref, mesh_own, local_ref), (give_ref, mesh_oth, local_other_ref))
    start = latent + width
    for o_ref, mesh, local in ends:
        grad = dot_rows(cot, mesh)
        o_ref[start : 2 * latent, :] = grad.astype(o_ref.dtype)
        o_ref[start : start + channels, :] = (grad[:channels] + local[...]).astype(o_ref.dtype)

    back = jnp.concatenate([back_own, back_oth], axis=1)
    slope = (
        back - jnp.mean(back, axis=-1, keepdims=True)
        - norm * jnp.mean(back * norm, axis=-1, keepdims=True)
    ) * inverse
    mesh_half[...] = (grad_own.astype(F32) + slope[:, :width]).reshape(mesh_half.shape)
    mesh_give_ref[...] = (grad_oth.astype(F32) + slope[:, width:]).astype(mesh_give_ref.dtype)
    copy = pltpu.make_async_copy(mesh_half, mesh_ref.at[:, r], mesh_sem)
    copy.start()
    copy.wait()


def place_kernel(got_ref, filled_ref, mesh_ref, mesh_half, mesh_sem):
    r = lax.axis_index("rep")
    mesh_half[...] = got_ref[...].astype(F32).reshape(mesh_half.shape)
    copy = pltpu.make_async_copy(mesh_half, mesh_ref.at[:, 1 - r], mesh_sem)
    copy.start()
    copy.wait()


def put_halves(value, step, keep_ref, give_ref, hold):
    rows = keep_ref.shape[0]
    bit = sum_bit(step)
    hold[...] = value
    keep_ref[...] = hold[pl.ds(pl.multiple_of(bit * rows, rows), rows), :].astype(keep_ref.dtype)
    give_ref[...] = hold[pl.ds(pl.multiple_of((1 - bit) * rows, rows), rows), :].astype(
        give_ref.dtype
    )


def terms_kernel(keep_ref, got_ref, *refs):
    outs, hold = refs[:4], refs[4]
    rows = hold.shape[0]
    for chain in range(2):
        part = slice(chain * rows, (chain + 1) * rows)
        put_halves(added(keep_ref[part, :], got_ref[part, :]), 0, *outs[2 * chain :][:2], hold)


def whole_kernel(kept_ref, got_ref, *refs):
    refs[-1][...] = added(kept_ref[...], got_ref[...]).astype(refs[-1].dtype)


def join_kernel(step, mine_ref, got_ref, *refs):
    out_ref = refs[-1]
    rows = mine_ref.shape[0]
    bit = sum_bit(step)
    out_ref[pl.ds(pl.multiple_of(bit * rows, rows), rows), :] = mine_ref[...].astype(out_ref.dtype)
    out_ref[pl.ds(pl.multiple_of((1 - bit) * rows, rows), rows), :] = got_ref[...].astype(
        out_ref.dtype
    )


def finish_outer_kernel(after_ref, mine_ref, other_ref, out_ref, out_other_ref, down_ref, grad_ref):
    r = lax.axis_index("rep")
    low = sum_bit(0) == 0
    width = mine_ref.shape[1]
    channels = out_ref.shape[0]
    mine, other = mine_ref[...], other_ref[...]
    terms = jnp.where(low, mine, other)[:, :channels]
    down_ref[:, pl.ds(pl.multiple_of(r * width, width), width)] = dot(terms, out_ref[...])
    down_ref[:, pl.ds(pl.multiple_of((1 - r) * width, width), width)] = dot(
        terms, out_other_ref[...]
    )
    grad_ref[...] = jnp.where(low, other, mine)[:channels].astype(F32)


def pack_kernel(after_ref, proj_ref, even_ref, odd_ref, out_ref):
    for k, part in enumerate((proj_ref, even_ref, odd_ref)):
        out_ref[k] = part[...]


def pick_kernel(device_ref, slot_ref, after_ref, own_ref, east_ref, mine_ref, theirs_ref):
    r = lax.axis_index("rep")
    blocks = mine_ref.shape[0]
    slots = own_ref.shape[0] // 3
    for out_ref, first in ((mine_ref, r * blocks), (theirs_ref, (1 - r) * blocks)):
        for i in range(blocks):
            at = entry_of(device_ref, slot_ref, first + i, slots)
            side = lax.div(at, 2 * slots)
            rest = at - side * 2 * slots

            @pl.when(rest < slots)
            def _(i=i, at=side * slots + rest, out_ref=out_ref):
                out_ref[i] = own_ref[at]

            @pl.when(rest >= slots)
            def _(i=i, at=side * slots + rest - slots, out_ref=out_ref):
                out_ref[i] = east_ref[at]


def decode_kernel(tiles_ref, base_ref, mine_ref, got_ref, out_ref, picked):
    r = lax.axis_index("rep")
    blocks, half = mine_ref.shape[:2]
    rows = tiles_ref.shape[1]
    channels = out_ref.shape[0]
    own = pl.ds(pl.multiple_of(r * half, half), half)
    other = pl.ds(pl.multiple_of((1 - r) * half, half), half)
    for i in range(blocks):
        picked[i, own, :] = mine_ref[i]
        picked[i, other, :] = got_ref[i]
    for i in range(blocks):
        cols = slice(i * rows, (i + 1) * rows)
        decoded = dot_last(picked[i].T, tiles_ref[r * blocks + i])
        out_ref[:, cols] = (base_ref[:, cols] + decoded[:channels]).astype(out_ref.dtype)


def along(axis, count, partner):
    pairs = []
    for source in range(count):
        to = partner(source)
        pairs.append((source, to if 0 <= to < count else source))
    return lambda value: lax.ppermute(value, axis, pairs)


def distances(axis):
    found, distance = [], 1
    while distance < lax.axis_size(axis):
        found.append((axis, distance))
        distance *= 2
    return found


def sum_orders():
    lat, lon = distances("lat"), distances("lon")
    return (lon + lat, lat + lon)


def sum_bit(step):
    bits = [
        lax.rem(lax.div(lax.axis_index(axis), distance), 2)
        for axis, distance in (order[step] for order in sum_orders())
    ]
    return jnp.where(lax.axis_index("rep") == 0, bits[0], bits[1])


def sum_swap(value, step):
    lat_count, lon_count = lax.axis_size("lat"), lax.axis_size("lon")
    orders = sum_orders()
    pairs = []
    for lat in range(lat_count):
        for lon in range(lon_count):
            for rep in range(2):
                axis, distance = orders[rep][step]
                to = (lat ^ distance, lon) if axis == "lat" else (lat, lon ^ distance)
                number = lambda a, b: (a * lon_count + b) * 2 + rep
                pairs.append((number(lat, lon), number(*to)))
    return lax.ppermute(value, ("lat", "lon", "rep"), pairs)


def per_device(
    grid_in, w_embed, interp_tiles, route_device, route_slot,
    mesh_embed, w_up, w_down, w_out, cotangent,
):
    lat_count, lon_count = lax.axis_size("lat"), lax.axis_size("lon")
    blocks, tile_rows = interp_tiles.shape[:2]
    grid_rows, channels = grid_in.shape
    my_rows = grid_rows // 2
    width = w_embed.shape[1]
    latent = 2 * width
    padded = -(-channels // 128) * 128
    slots = mesh_embed.shape[0] // tile_rows
    half = tile_rows // 2
    nodes = slots * half

    swap_rep = along("rep", 2, lambda i: 1 - i)
    to_even = along("lat", lat_count, lambda i: i ^ 1)
    to_odd = along("lat", lat_count, lambda i: ((i + 1) ^ 1) - 1)
    east_pairs = [(i, (i + 1) % lon_count) for i in range(lon_count)]
    west_pairs = [(j, i) for i, j in east_pairs]
    to_east = lambda value: lax.ppermute(value, "lon", east_pairs)

    in_hbm = lambda value: pltpu.with_memory_space_constraint(value, pltpu.HBM)
    device, slot = route_device.reshape(blocks), route_slot
    grid_t, cot_t, out_t = grid_in.T, cotangent.T, w_out.T
    routes = (in_hbm(device), in_hbm(slot))
    tiles_in, grid_in_t, cot_in_t = in_hbm(interp_tiles), in_hbm(grid_t), in_hbm(cot_t)
    pair_shape = (2, nodes, width)
    embed_other = swap_rep(w_embed)

    back_own, back_east, back_side = call(
        back_kernel, "back_messages",
        [smem(), smem(), anywhere(), anywhere()],
        [vmem()] * 3,
        [shape_of((nodes, padded), BF16), shape_of((3, nodes, padded), BF16),
         shape_of((2, nodes, padded), BF16)],
        1, 1,
        scratch=[
            pltpu.VMEM((6 * slots, half, padded), F32),
            pltpu.VMEM(interp_tiles.shape, BF16),
            pltpu.VMEM(cot_t.shape, BF16),
            pltpu.SemaphoreType.DMA((STEPS,)),
            pltpu.SemaphoreType.DMA((STEPS,)),
        ],
    )(*routes, tiles_in, cot_in_t)
    back_moved = to_east(back_east)

    def encode(after, weight):
        return call(
            encode_kernel, "encode",
            [smem(), smem(), anywhere()] + [vmem()] * 3,
            [vmem()] * 4,
            [shape_of(pair_shape, BF16)] * 3 + [shape_of((my_rows, width), BF16)],
            1, 1,
            scratch=[
                pltpu.VMEM((6 * slots, half, width), F32), pltpu.VMEM((grid_rows, width), BF16),
            ],
        )(*routes, after, grid_t, interp_tiles, weight)

    own_a, even_a, odd_a, hidden_a = encode(back_own, in_hbm(w_embed))
    even_in_a, odd_in_a = to_even(even_a), to_odd(odd_a)
    own_b, even_b, odd_b, hidden_b = encode(own_a, embed_other)
    even_in_b, odd_in_b = to_even(even_b), to_odd(odd_b)

    out_other, up_other, down_other = swap_rep(out_t), swap_rep(w_up), swap_rep(w_down)
    embed_shape = (slots, 2, half, width)
    mesh_other = swap_rep(mesh_embed)

    second = pl.BlockSpec((1, nodes, width), lambda i: (1, 0, 0))

    def add_east(after, *terms):
        return call(
            add_kernel, "add_east", [anywhere()] * len(after) + [second] * 3, whole((nodes, width)),
            shape_of((nodes, width), BF16), 3 * nodes * width, 6e5, grid=(1,),
        )(*after, *terms)

    send_a = add_east((back_moved,), own_a, even_in_a, odd_in_a)
    moved_a = to_east(send_a)

    base, local, local_other = call(
        local_kernel, "local_terms", [vmem()] * 5, [vmem()] * 3,
        [shape_of((channels, my_rows), F32)] + [shape_of((channels, width), F32)] * 2,
        4 * my_rows * latent * channels, 4e6,
    )(hidden_a, hidden_b, cot_t, out_t, out_other)

    send_b = add_east((moved_a,), own_b, even_in_b, odd_in_b)
    moved_b = to_east(send_b)

    back_even, back_odd = call(
        sides_kernel, "add_sides", [anywhere(), vmem(), vmem()], [vmem()] * 2,
        [shape_of((nodes, padded), BF16)] * 2, 3 * nodes * width, 1e6,
    )(send_b, back_side, back_moved)
    back_even_in, back_odd_in = to_even(back_even), to_odd(back_odd)

    first = pl.BlockSpec((1, nodes, width), lambda i: (0, 0, 0))
    sums_specs = [first] * 3 + [whole((nodes, width))]
    weights = (w_up, up_other, w_down, down_other, out_t, out_other)
    back_spec = whole((nodes, padded))
    mesh_scratch = [pltpu.VMEM((slots, half, width), F32), pltpu.SemaphoreType.DMA]
    proj, keep, give, mesh_give, mesh_filled = call(
        node_kernel, "node_update_and_gradients",
        sums_specs * 2 + [whole(embed_shape)] * 2
        + [back_spec, pl.BlockSpec((1, nodes, padded), lambda i: (0, 0, 0)), back_spec, back_spec]
        + [whole((channels, width))] * 2 + [whole(w.shape) for w in weights],
        [whole((nodes, padded))] + [whole((2 * latent, width))] * 2
        + [whole((nodes, width)), anywhere()],
        [shape_of((nodes, padded), BF16), shape_of((2 * latent, width), F32),
         shape_of((2 * latent, width), BF16), shape_of((nodes, width), BF16),
         shape_of(embed_shape, F32)],
        15 * nodes * latent * latent, 9e6, grid=(1,), exps=nodes * latent, scratch=mesh_scratch,
    )(
        own_a, even_in_a, odd_in_a, moved_a, own_b, even_in_b, odd_in_b, moved_b,
        mesh_embed.reshape(embed_shape), mesh_other.reshape(embed_shape),
        back_own, back_moved, back_even_in, back_odd_in, local, local_other, *weights,
    )

    proj_even, proj_odd = to_even(proj), to_odd(proj)
    hold = lambda rows: [pltpu.VMEM((rows, width), F32)]
    up_keep, up_give, outer_keep, outer_give = call(
        terms_kernel, "sum_terms", [vmem()] * 2, [vmem()] * 4,
        [shape_of((width, width), BF16)] * 4, 1, 1, scratch=hold(latent), weight=5e9,
    )(keep, swap_rep(give))

    count = len(sum_orders()[0])
    chains = [[outer_keep, outer_give], [up_keep, up_give]]
    latest = None

    def step_call(chain, step, rows):
        kept, given = chain[0], chain[-1]
        after = [latest] if latest is not None else [proj_even, proj_odd]
        made = call(
            whole_kernel, "add_whole", [vmem()] * 2 + [anywhere()] * len(after), vmem(),
            shape_of((rows, width), BF16), 1, 1,
        )(kept, sum_swap(given, step), *after)
        return [made]

    for step in range(count):
        for c in range(2):
            rows = chains[c][0].shape[0]
            if step == 1 and c == 0:
                trio = call(
                    pack_kernel, "pack_nodes", [anywhere()] + [vmem()] * 3, vmem(),
                    shape_of((3, nodes, padded), BF16), 1, 1,
                )(latest, proj, proj_even, proj_odd)
                east_trio = lax.ppermute(trio, "lon", west_pairs)
            chains[c] = step_call(chains[c], step, rows)
            latest = chains[c][-1]
    after_pick = chains[1][-1]
    (outer_mine,), (up_mine,) = chains
    outer_theirs, up_theirs = sum_swap(outer_mine, 0), sum_swap(up_mine, 0)

    grad_mesh = pl.pallas_call(
        place_kernel,
        in_specs=[vmem(), anywhere()],
        out_specs=anywhere(),
        out_shape=shape_of(embed_shape, F32),
        scratch_shapes=mesh_scratch,
        input_output_aliases={1: 0},
        compiler_params=pltpu.CompilerParams(vmem_limit_bytes=VMEM_BYTES),
        cost_estimate=pl.CostEstimate(flops=1, bytes_accessed=1, transcendentals=0),
        name="place_mesh",
    )(swap_rep(mesh_give), mesh_filled).reshape(mesh_embed.shape)

    table_shape = (3 * slots, half, padded)
    mine_picked, theirs_picked = call(
        pick_kernel, "pick_nodes", [smem()] * 2 + [anywhere()] + [vmem()] * 2, [vmem()] * 2,
        [shape_of((blocks // 2, half, padded), BF16)] * 2, 1, 1,
    )(*routes, after_pick, trio.reshape(table_shape), east_trio.reshape(table_shape))
    grid_out_t = call(
        decode_kernel, "decode", [vmem()] * 4, vmem(),
        shape_of((channels, my_rows), BF16), 2 * my_rows * tile_rows * padded, 4e6,
        scratch=[pltpu.VMEM((blocks // 2, tile_rows, padded), BF16)],
    )(interp_tiles, base, mine_picked, swap_rep(theirs_picked))

    grad_down, grad_out = call(
        finish_outer_kernel, "finish_outer", [anywhere()] + [vmem()] * 4, [vmem()] * 2,
        [shape_of((width, latent), F32), shape_of((channels, width), F32)], 1, 1,
    )(in_hbm(grid_out_t), outer_mine, outer_theirs, out_t, out_other)
    grad_up = call(
        functools.partial(join_kernel, 0), "finish_up", [vmem()] * 2 + [anywhere()], vmem(),
        shape_of((latent, width), F32), 1, 1,
    )(up_mine, up_theirs, in_hbm(grid_out_t))
    return (grid_out_t.T, grad_out.T, grad_up, grad_down, grad_mesh)


def solution(mesh):
    patch = ("groups", "lat", "lon")
    placed = (
        P(patch, None),
        P(None, "rep"),
        P(patch, None, None),
        P(patch, None),
        P(patch),
        P(patch, "rep"),
        P(None, "rep"),
        P("rep", None),
        P("rep", None),
        P(patch, None),
    )
    return jax.shard_map(
        per_device,
        mesh=mesh,
        in_specs=placed,
        out_specs=(
            P(("groups", "lat", "lon", "rep"), None),
            P(("groups", "rep"), None),
            P("groups", "rep"),
            P(("groups", "rep"), None),
            P(patch, "rep"),
        ),
        check_vma=False,
    )
```

```python
import functools

import jax
import jax.numpy as jnp
from jax import lax
from jax.experimental import pallas as pl
from jax.experimental.pallas import tpu as pltpu
from jax.sharding import PartitionSpec as P

F32 = jnp.float32
BF16 = jnp.bfloat16
VMEM_BYTES = 20 * 1024 * 1024
STEPS = 4


def dot(left, right):
    return jnp.dot(left, right, preferred_element_type=F32)


def dot_rows(left, right):
    return lax.dot_general(left, right, (((0,), (0,)), ((), ())), preferred_element_type=F32)


def dot_last(left, right):
    return lax.dot_general(left, right, (((1,), (1,)), ((), ())), preferred_element_type=F32)


def sigmoid(values):
    return 0.5 * jnp.tanh(0.5 * values) + 0.5


def vmem():
    return pl.BlockSpec(memory_space=pltpu.VMEM)


def smem():
    return pl.BlockSpec(memory_space=pltpu.SMEM)


def anywhere():
    return pl.BlockSpec(memory_space=pl.ANY)


def whole(shape):
    return pl.BlockSpec(shape, lambda i: (0,) * len(shape))


def shape_of(shape, dtype):
    return jax.ShapeDtypeStruct(shape, dtype)


def call(kernel, name, in_specs, out_specs, out_shape, flops, nbytes, grid=(), scratch=(), exps=0,
         limit=VMEM_BYTES, weight=1):
    return pl.pallas_call(
        kernel,
        grid=grid,
        in_specs=in_specs,
        out_specs=out_specs,
        out_shape=out_shape,
        scratch_shapes=list(scratch),
        compiler_params=pltpu.CompilerParams(vmem_limit_bytes=limit),
        cost_estimate=pl.CostEstimate(flops=int(weight), bytes_accessed=1, transcendentals=0),
        name=name,
    )


def node_half(tile, r):
    half = tile.shape[1] // 2
    return jnp.where(r == 0, tile[:, :half], tile[:, half:]).T


def entry_of(device_ref, slot_ref, b, slots):
    lon_count = lax.axis_size("lon")
    lat, lon = lax.axis_index("lat"), lax.axis_index("lon")
    target = device_ref[b]
    band = lax.div(target, lon_count)
    sector = target - band * lon_count - lon
    sector = jnp.where(sector < 0, sector + lon_count, sector)
    step = band - lat
    even_step = 1 - 2 * lax.rem(lat, 2)
    side = jnp.where(step == 0, 0, jnp.where(step == even_step, 1, 2))
    return (side * 2 + sector) * slots + slot_ref[b]


def write_packed(total, outs):
    per = total.shape[0] // 3
    for k, out in enumerate(outs):
        block = total[k * per : (k + 1) * per]
        out[...] = block.reshape(out.shape).astype(out.dtype)


def back_kernel(
    device_ref, slot_ref, tiles_ref, cot_ref, own_ref, east_ref, side_ref,
    total, tiles, cots, tile_sems, cot_sems,
):
    blocks, rows = tiles.shape[0], tiles.shape[1]
    count = blocks // STEPS
    slots = total.shape[0] // 6
    channels = cots.shape[0]
    r = lax.axis_index("rep")
    copies = []
    for k in range(STEPS):
        part = pl.ds(k * count, count)
        cols = pl.ds(k * count * rows, count * rows)
        copies.append((
            pltpu.make_async_copy(tiles_ref.at[part], tiles.at[part], tile_sems.at[k]),
            pltpu.make_async_copy(cot_ref.at[:, cols], cots.at[:, cols], cot_sems.at[k]),
        ))
        for copy in copies[-1]:
            copy.start()
    total[...] = jnp.zeros_like(total)
    for b in range(blocks):
        if b % count == 0:
            for copy in copies[b // count]:
                copy.wait()
        at = entry_of(device_ref, slot_ref, b, slots)
        cot = cots[:, b * rows : (b + 1) * rows]
        total[at, :, :channels] += dot_last(node_half(tiles[b], r), cot)
    for k, out in ((0, own_ref), (2, side_ref.at[0]), (4, side_ref.at[1])):
        out[...] = total[k * slots : (k + 1) * slots].reshape(out.shape).astype(out.dtype)
    for k in range(3):
        block = total[(2 * k + 1) * slots : (2 * k + 2) * slots]
        east_ref[k] = block.reshape(east_ref.shape[1:]).astype(east_ref.dtype)


def encode_kernel(device_ref, slot_ref, after_ref, grid_ref, tiles_ref, weight_ref, *refs):
    extra, (own_ref, even_ref, odd_ref, hidden_ref, total, hold) = refs[:-6], refs[-6:]
    blocks, rows = tiles_ref.shape[:2]
    slots = total.shape[0] // 6
    step_rows = blocks * rows // STEPS
    r = lax.axis_index("rep")
    total[...] = jnp.zeros_like(total)
    for k in range(STEPS):
        preact = dot_rows(grid_ref[:, k * step_rows : (k + 1) * step_rows], weight_ref[...])
        hold[k * step_rows : (k + 1) * step_rows, :] = (preact * sigmoid(preact)).astype(BF16)
        for b in range(k * blocks // STEPS, (k + 1) * blocks // STEPS):
            at = entry_of(device_ref, slot_ref, b, slots)
            total[at] += dot(node_half(tiles_ref[b], r), hold[b * rows : (b + 1) * rows, :])
    mine = hidden_ref.shape[0]
    hidden_ref[...] = hold[pl.ds(pl.multiple_of(r * mine, mine), mine), :]
    write_packed(total, (own_ref, even_ref.at[:2], odd_ref.at[:2]))
    if extra:
        side_ref, moved_ref = extra
        even_ref[2] = added(side_ref[0], moved_ref[1]).astype(even_ref.dtype)
        odd_ref[2] = added(side_ref[1], moved_ref[2]).astype(odd_ref.dtype)


def local_kernel(
    own_ref, oth_ref, cot_ref, out_ref, out_other_ref,
    base_ref, grad_ref, grad_other_ref,
):
    rows = own_ref.shape[0]
    r = lax.axis_index("rep")
    cot = cot_ref[:, pl.ds(pl.multiple_of(r * rows, rows), rows)]
    base_ref[...] = dot_last(out_ref[...], own_ref[...]) + dot_last(out_other_ref[...], oth_ref[...])
    grad_ref[...] = dot(cot, own_ref[...])
    grad_other_ref[...] = dot(cot, oth_ref[...])


def added(*values):
    total = values[0].astype(F32)
    for value in values[1:]:
        total = total + value.astype(F32)
    return total


def add_kernel(*refs):
    a, b, c, out = refs[-4:]
    out[...] = added(a[0], b[0], c[0]).astype(out.dtype)


def node_kernel(
    own_a, even_a, odd_a, moved_a, own_b, even_b, odd_b, moved_b, embed_ref, embed_other_ref,
    back_ref, back_moved_ref, back_even_ref, back_odd_ref, local_ref, local_other_ref,
    up_ref, up_other_ref, down_ref, down_other_ref, out_ref, out_other_ref,
    proj_ref, keep_ref, give_ref, mesh_give_ref, mesh_ref, mesh_half, mesh_sem,
):
    r = lax.axis_index("rep")
    nodes, width = moved_a.shape
    latent = 2 * width
    channels = out_ref.shape[0]
    first = pl.multiple_of(r * width, width)
    second = pl.multiple_of((1 - r) * width, width)
    states = []
    for embed, parts in (
        (embed_ref, (own_a[0], even_a[0], odd_a[0], moved_a[...])),
        (embed_other_ref, (own_b[0], even_b[0], odd_b[0], moved_b[...])),
    ):
        start = embed[:, r].reshape(nodes, width)
        states.append((start.astype(F32) + added(*parts)).astype(BF16).astype(F32))
    state = jnp.concatenate(states, axis=1)
    centered = state - jnp.mean(state, axis=-1, keepdims=True)
    inverse = lax.rsqrt(jnp.mean(centered * centered, axis=-1, keepdims=True) + 1e-05)
    norm = centered * inverse
    normed = norm.astype(BF16)

    cot = added(back_ref[...], back_moved_ref[0], back_even_ref[0], back_odd_ref[0]).astype(BF16)
    terms = cot[:, :channels]
    grad_own = dot(terms, out_ref[...]).astype(BF16)
    grad_oth = dot(terms, out_other_ref[...]).astype(BF16)

    update_own = jnp.zeros((nodes, width), F32)
    update_oth = jnp.zeros((nodes, width), F32)
    back_own = jnp.zeros((nodes, width), F32)
    back_oth = jnp.zeros((nodes, width), F32)
    sides = ((up_ref, down_ref, keep_ref), (up_other_ref, down_other_ref, give_ref))
    for u_ref, d_ref, o_ref in sides:
        up_own, up_oth = u_ref[pl.ds(first, width), :], u_ref[pl.ds(second, width), :]
        down_own, down_oth = d_ref[:, pl.ds(first, width)], d_ref[:, pl.ds(second, width)]
        hidden = dot(normed[:, :width], up_own) + dot(normed[:, width:], up_oth)
        squash = sigmoid(hidden)
        act = (hidden * squash).astype(BF16)
        update_own += dot(act, down_own)
        update_oth += dot(act, down_oth)
        o_ref[latent : latent + width, :] = dot_rows(act, cot).astype(o_ref.dtype)
        act_grad = dot_last(grad_own, down_own) + dot_last(grad_oth, down_oth)
        pre_grad = (act_grad * squash * (1.0 + hidden * (1.0 - squash))).astype(BF16)
        o_ref[pl.ds(first, width), :] = dot_rows(normed[:, :width], pre_grad).astype(o_ref.dtype)
        o_ref[pl.ds(second, width), :] = dot_rows(normed[:, width:], pre_grad).astype(o_ref.dtype)
        back_own += dot_last(pre_grad, up_own)
        back_oth += dot_last(pre_grad, up_oth)

    mesh_own = (states[0] + update_own).astype(BF16)
    mesh_oth = (states[1] + update_oth).astype(BF16)
    proj = dot_last(mesh_own, out_ref[...]) + dot_last(mesh_oth, out_other_ref[...])
    proj_ref[...] = jnp.zeros_like(proj_ref)
    proj_ref[:, :channels] = proj.astype(BF16)
    ends = ((keep_ref, mesh_own, local_ref), (give_ref, mesh_oth, local_other_ref))
    start = latent + width
    for o_ref, mesh, local in ends:
        grad = dot_rows(cot, mesh)
        o_ref[start : 2 * latent, :] = grad.astype(o_ref.dtype)
        o_ref[start : start + channels, :] = (grad[:channels] + local[...]).astype(o_ref.dtype)

    back = jnp.concatenate([back_own, back_oth], axis=1)
    slope = (
        back - jnp.mean(back, axis=-1, keepdims=True)
        - norm * jnp.mean(back * norm, axis=-1, keepdims=True)
    ) * inverse
    mesh_half[...] = (grad_own.astype(F32) + slope[:, :width]).reshape(mesh_half.shape)
    mesh_give_ref[...] = (grad_oth.astype(F32) + slope[:, width:]).astype(mesh_give_ref.dtype)
    copy = pltpu.make_async_copy(mesh_half, mesh_ref.at[:, r], mesh_sem)
    copy.start()
    copy.wait()


def place_kernel(got_ref, filled_ref, mesh_ref, mesh_half, mesh_sem):
    r = lax.axis_index("rep")
    mesh_half[...] = got_ref[...].astype(F32).reshape(mesh_half.shape)
    copy = pltpu.make_async_copy(mesh_half, mesh_ref.at[:, 1 - r], mesh_sem)
    copy.start()
    copy.wait()


def put_halves(value, step, keep_ref, give_ref, hold):
    rows = keep_ref.shape[0]
    bit = sum_bit(step)
    hold[...] = value
    keep_ref[...] = hold[pl.ds(pl.multiple_of(bit * rows, rows), rows), :].astype(keep_ref.dtype)
    give_ref[...] = hold[pl.ds(pl.multiple_of((1 - bit) * rows, rows), rows), :].astype(
        give_ref.dtype
    )


def terms_kernel(keep_ref, got_ref, *refs):
    outs, hold = refs[:4], refs[4]
    rows = hold.shape[0]
    for chain in range(2):
        part = slice(chain * rows, (chain + 1) * rows)
        put_halves(added(keep_ref[part, :], got_ref[part, :]), 0, *outs[2 * chain :][:2], hold)


def whole_kernel(kept_ref, got_ref, *refs):
    refs[-1][...] = added(kept_ref[...], got_ref[...]).astype(refs[-1].dtype)


def join_kernel(step, mine_ref, got_ref, *refs):
    out_ref = refs[-1]
    rows = mine_ref.shape[0]
    bit = sum_bit(step)
    out_ref[pl.ds(pl.multiple_of(bit * rows, rows), rows), :] = mine_ref[...].astype(out_ref.dtype)
    out_ref[pl.ds(pl.multiple_of((1 - bit) * rows, rows), rows), :] = got_ref[...].astype(
        out_ref.dtype
    )


def finish_outer_kernel(after_ref, mine_ref, other_ref, out_ref, out_other_ref, down_ref, grad_ref):
    r = lax.axis_index("rep")
    low = sum_bit(0) == 0
    width = mine_ref.shape[1]
    channels = out_ref.shape[0]
    mine, other = mine_ref[...], other_ref[...]
    terms = jnp.where(low, mine, other)[:, :channels]
    down_ref[:, pl.ds(pl.multiple_of(r * width, width), width)] = dot(terms, out_ref[...])
    down_ref[:, pl.ds(pl.multiple_of((1 - r) * width, width), width)] = dot(
        terms, out_other_ref[...]
    )
    grad_ref[...] = jnp.where(low, other, mine)[:channels].astype(F32)


def pack_kernel(after_ref, proj_ref, even_ref, odd_ref, out_ref):
    for k, part in enumerate((proj_ref, even_ref, odd_ref)):
        out_ref[k] = part[...]


def pick_kernel(device_ref, slot_ref, after_ref, own_ref, east_ref, mine_ref, theirs_ref):
    r = lax.axis_index("rep")
    blocks = mine_ref.shape[0]
    slots = own_ref.shape[0] // 3
    for out_ref, first in ((mine_ref, r * blocks), (theirs_ref, (1 - r) * blocks)):
        for i in range(blocks):
            at = entry_of(device_ref, slot_ref, first + i, slots)
            side = lax.div(at, 2 * slots)
            rest = at - side * 2 * slots

            @pl.when(rest < slots)
            def _(i=i, at=side * slots + rest, out_ref=out_ref):
                out_ref[i] = own_ref[at]

            @pl.when(rest >= slots)
            def _(i=i, at=side * slots + rest - slots, out_ref=out_ref):
                out_ref[i] = east_ref[at]


def decode_kernel(tiles_ref, base_ref, mine_ref, got_ref, out_ref, picked):
    r = lax.axis_index("rep")
    blocks, half = mine_ref.shape[:2]
    rows = tiles_ref.shape[1]
    channels = out_ref.shape[0]
    own = pl.ds(pl.multiple_of(r * half, half), half)
    other = pl.ds(pl.multiple_of((1 - r) * half, half), half)
    for i in range(blocks):
        picked[i, own, :] = mine_ref[i]
        picked[i, other, :] = got_ref[i]
    for i in range(blocks):
        cols = slice(i * rows, (i + 1) * rows)
        decoded = dot_last(picked[i].T, tiles_ref[r * blocks + i])
        out_ref[:, cols] = (base_ref[:, cols] + decoded[:channels]).astype(out_ref.dtype)


def along(axis, count, partner):
    pairs = []
    for source in range(count):
        to = partner(source)
        pairs.append((source, to if 0 <= to < count else source))
    return lambda value: lax.ppermute(value, axis, pairs)


def distances(axis):
    found, distance = [], 1
    while distance < lax.axis_size(axis):
        found.append((axis, distance))
        distance *= 2
    return found


def sum_orders():
    lat, lon = distances("lat"), distances("lon")
    return (lon + lat, lat + lon)


def sum_bit(step):
    bits = [
        lax.rem(lax.div(lax.axis_index(axis), distance), 2)
        for axis, distance in (order[step] for order in sum_orders())
    ]
    return jnp.where(lax.axis_index("rep") == 0, bits[0], bits[1])


def sum_swap(value, step):
    lat_count, lon_count = lax.axis_size("lat"), lax.axis_size("lon")
    orders = sum_orders()
    pairs = []
    for lat in range(lat_count):
        for lon in range(lon_count):
            for rep in range(2):
                axis, distance = orders[rep][step]
                to = (lat ^ distance, lon) if axis == "lat" else (lat, lon ^ distance)
                number = lambda a, b: (a * lon_count + b) * 2 + rep
                pairs.append((number(lat, lon), number(*to)))
    return lax.ppermute(value, ("lat", "lon", "rep"), pairs)


def per_device(
    grid_in, w_embed, interp_tiles, route_device, route_slot,
    mesh_embed, w_up, w_down, w_out, cotangent,
):
    lat_count, lon_count = lax.axis_size("lat"), lax.axis_size("lon")
    blocks, tile_rows = interp_tiles.shape[:2]
    grid_rows, channels = grid_in.shape
    my_rows = grid_rows // 2
    width = w_embed.shape[1]
    latent = 2 * width
    padded = -(-channels // 128) * 128
    slots = mesh_embed.shape[0] // tile_rows
    half = tile_rows // 2
    nodes = slots * half

    swap_rep = along("rep", 2, lambda i: 1 - i)
    to_even = along("lat", lat_count, lambda i: i ^ 1)
    to_odd = along("lat", lat_count, lambda i: ((i + 1) ^ 1) - 1)
    east_pairs = [(i, (i + 1) % lon_count) for i in range(lon_count)]
    west_pairs = [(j, i) for i, j in east_pairs]
    to_east = lambda value: lax.ppermute(value, "lon", east_pairs)

    in_hbm = lambda value: pltpu.with_memory_space_constraint(value, pltpu.HBM)
    device, slot = route_device.reshape(blocks), route_slot
    grid_t, cot_t, out_t = grid_in.T, cotangent.T, w_out.T
    routes = (in_hbm(device), in_hbm(slot))
    tiles_in, grid_in_t, cot_in_t = in_hbm(interp_tiles), in_hbm(grid_t), in_hbm(cot_t)
    pair_shape = (2, nodes, width)
    embed_other = swap_rep(w_embed)

    back_own, back_east, back_side = call(
        back_kernel, "back_messages",
        [smem(), smem(), anywhere(), anywhere()],
        [vmem()] * 3,
        [shape_of((nodes, padded), BF16), shape_of((3, nodes, padded), BF16),
         shape_of((2, nodes, padded), BF16)],
        1, 1,
        scratch=[
            pltpu.VMEM((6 * slots, half, padded), F32),
            pltpu.VMEM(interp_tiles.shape, BF16),
            pltpu.VMEM(cot_t.shape, BF16),
            pltpu.SemaphoreType.DMA((STEPS,)),
            pltpu.SemaphoreType.DMA((STEPS,)),
        ],
    )(*routes, tiles_in, cot_in_t)
    back_moved = to_east(back_east)

    def encode(after, weight, *extra):
        sent = (3,) + pair_shape[1:] if extra else pair_shape
        return call(
            encode_kernel, "encode",
            [smem(), smem(), anywhere()] + [vmem()] * (3 + len(extra)),
            [vmem()] * 4,
            [shape_of(pair_shape, BF16)] + [shape_of(sent, BF16)] * 2
            + [shape_of((my_rows, width), BF16)],
            1, 1,
            scratch=[
                pltpu.VMEM((6 * slots, half, width), F32), pltpu.VMEM((grid_rows, width), BF16),
            ],
        )(*routes, after, grid_t, interp_tiles, weight, *extra)

    own_a, even_a, odd_a, hidden_a = encode(back_own, in_hbm(w_embed))
    even_in_a, odd_in_a = to_even(even_a), to_odd(odd_a)
    own_b, even_b, odd_b, hidden_b = encode(own_a, embed_other, back_side, back_moved)
    even_in_b, odd_in_b = to_even(even_b), to_odd(odd_b)

    out_other, up_other, down_other = swap_rep(out_t), swap_rep(w_up), swap_rep(w_down)
    embed_shape = (slots, 2, half, width)
    mesh_other = swap_rep(mesh_embed)

    second = pl.BlockSpec((1, nodes, width), lambda i: (1, 0, 0))

    def add_east(after, *terms):
        return call(
            add_kernel, "add_east", [anywhere()] * len(after) + [second] * 3, whole((nodes, width)),
            shape_of((nodes, width), BF16), 3 * nodes * width, 6e5, grid=(1,),
        )(*after, *terms)

    send_a = add_east((own_b,), own_a, even_in_a, odd_in_a)
    moved_a = to_east(send_a)

    base, local, local_other = call(
        local_kernel, "local_terms", [vmem()] * 5, [vmem()] * 3,
        [shape_of((channels, my_rows), F32)] + [shape_of((channels, width), F32)] * 2,
        4 * my_rows * latent * channels, 4e6,
    )(hidden_a, hidden_b, cot_t, out_t, out_other)

    send_b = add_east((moved_a,), own_b, even_in_b, odd_in_b)
    moved_b = to_east(send_b)

    first = pl.BlockSpec((1, nodes, width), lambda i: (0, 0, 0))
    sums_specs = [first] * 3 + [whole((nodes, width))]
    weights = (w_up, up_other, w_down, down_other, out_t, out_other)
    back_spec = whole((nodes, padded))
    mesh_scratch = [pltpu.VMEM((slots, half, width), F32), pltpu.SemaphoreType.DMA]
    proj, keep, give, mesh_give, mesh_filled = call(
        node_kernel, "node_update_and_gradients",
        sums_specs * 2 + [whole(embed_shape)] * 2
        + [back_spec, pl.BlockSpec((1, nodes, padded), lambda i: (0, 0, 0))]
        + [pl.BlockSpec((1, nodes, padded), lambda i: (2, 0, 0))] * 2
        + [whole((channels, width))] * 2 + [whole(w.shape) for w in weights],
        [whole((nodes, padded))] + [whole((2 * latent, width))] * 2
        + [whole((nodes, width)), anywhere()],
        [shape_of((nodes, padded), BF16), shape_of((2 * latent, width), F32),
         shape_of((2 * latent, width), BF16), shape_of((nodes, width), BF16),
         shape_of(embed_shape, F32)],
        15 * nodes * latent * latent, 9e6, grid=(1,), exps=nodes * latent, scratch=mesh_scratch,
    )(
        own_a, even_in_a, odd_in_a, moved_a, own_b, even_in_b, odd_in_b, moved_b,
        mesh_embed.reshape(embed_shape), mesh_other.reshape(embed_shape),
        back_own, back_moved, even_in_b, odd_in_b, local, local_other, *weights,
    )

    proj_even, proj_odd = to_even(proj), to_odd(proj)
    hold = lambda rows: [pltpu.VMEM((rows, width), F32)]
    up_keep, up_give, outer_keep, outer_give = call(
        terms_kernel, "sum_terms", [vmem()] * 2, [vmem()] * 4,
        [shape_of((width, width), BF16)] * 4, 1, 1, scratch=hold(latent), weight=5e9,
    )(keep, swap_rep(give))

    count = len(sum_orders()[0])
    chains = [[outer_keep, outer_give], [up_keep, up_give]]
    latest = None

    def step_call(chain, step, rows):
        kept, given = chain[0], chain[-1]
        after = [latest] if latest is not None else [proj_even, proj_odd]
        made = call(
            whole_kernel, "add_whole", [vmem()] * 2 + [anywhere()] * len(after), vmem(),
            shape_of((rows, width), BF16), 1, 1,
        )(kept, sum_swap(given, step), *after)
        return [made]

    for step in range(count):
        for c in range(2):
            rows = chains[c][0].shape[0]
            if step == 1 and c == 0:
                trio = call(
                    pack_kernel, "pack_nodes", [anywhere()] + [vmem()] * 3, vmem(),
                    shape_of((3, nodes, padded), BF16), 1, 1,
                )(latest, proj, proj_even, proj_odd)
                east_trio = lax.ppermute(trio, "lon", west_pairs)
            chains[c] = step_call(chains[c], step, rows)
            latest = chains[c][-1]
    after_pick = chains[1][-1]
    (outer_mine,), (up_mine,) = chains
    outer_theirs, up_theirs = sum_swap(outer_mine, 0), sum_swap(up_mine, 0)

    grad_mesh = pl.pallas_call(
        place_kernel,
        in_specs=[vmem(), anywhere()],
        out_specs=anywhere(),
        out_shape=shape_of(embed_shape, F32),
        scratch_shapes=mesh_scratch,
        input_output_aliases={1: 0},
        compiler_params=pltpu.CompilerParams(vmem_limit_bytes=VMEM_BYTES),
        cost_estimate=pl.CostEstimate(flops=1, bytes_accessed=1, transcendentals=0),
        name="place_mesh",
    )(swap_rep(mesh_give), mesh_filled).reshape(mesh_embed.shape)

    table_shape = (3 * slots, half, padded)
    mine_picked, theirs_picked = call(
        pick_kernel, "pick_nodes", [smem()] * 2 + [anywhere()] + [vmem()] * 2, [vmem()] * 2,
        [shape_of((blocks // 2, half, padded), BF16)] * 2, 1, 1,
    )(*routes, after_pick, trio.reshape(table_shape), east_trio.reshape(table_shape))
    grid_out_t = call(
        decode_kernel, "decode", [vmem()] * 4, vmem(),
        shape_of((channels, my_rows), BF16), 2 * my_rows * tile_rows * padded, 4e6,
        scratch=[pltpu.VMEM((blocks // 2, tile_rows, padded), BF16)],
    )(interp_tiles, base, mine_picked, swap_rep(theirs_picked))

    grad_down, grad_out = call(
        finish_outer_kernel, "finish_outer", [anywhere()] + [vmem()] * 4, [vmem()] * 2,
        [shape_of((width, latent), F32), shape_of((channels, width), F32)], 1, 1,
    )(in_hbm(grid_out_t), outer_mine, outer_theirs, out_t, out_other)
    grad_up = call(
        functools.partial(join_kernel, 0), "finish_up", [vmem()] * 2 + [anywhere()], vmem(),
        shape_of((latent, width), F32), 1, 1,
    )(up_mine, up_theirs, in_hbm(grid_out_t))
    return (grid_out_t.T, grad_out.T, grad_up, grad_down, grad_mesh)


def solution(mesh):
    patch = ("groups", "lat", "lon")
    placed = (
        P(patch, None),
        P(None, "rep"),
        P(patch, None, None),
        P(patch, None),
        P(patch),
        P(patch, "rep"),
        P(None, "rep"),
        P("rep", None),
        P("rep", None),
        P(patch, None),
    )
    return jax.shard_map(
        per_device,
        mesh=mesh,
        in_specs=placed,
        out_specs=(
            P(("groups", "lat", "lon", "rep"), None),
            P(("groups", "rep"), None),
            P("groups", "rep"),
            P(("groups", "rep"), None),
            P(patch, "rep"),
        ),
        check_vma=False,
    )
```

```python
import functools

import jax
import jax.numpy as jnp
from jax import lax
from jax.experimental import pallas as pl
from jax.experimental.pallas import tpu as pltpu
from jax.sharding import PartitionSpec as P

F32 = jnp.float32
BF16 = jnp.bfloat16
VMEM_BYTES = 20 * 1024 * 1024
STEPS = 4


def dot(left, right):
    return jnp.dot(left, right, preferred_element_type=F32)


def dot_rows(left, right):
    return lax.dot_general(left, right, (((0,), (0,)), ((), ())), preferred_element_type=F32)


def dot_last(left, right):
    return lax.dot_general(left, right, (((1,), (1,)), ((), ())), preferred_element_type=F32)


def sigmoid(values):
    return 0.5 * jnp.tanh(0.5 * values) + 0.5


def vmem():
    return pl.BlockSpec(memory_space=pltpu.VMEM)


def smem():
    return pl.BlockSpec(memory_space=pltpu.SMEM)


def anywhere():
    return pl.BlockSpec(memory_space=pl.ANY)


def whole(shape):
    return pl.BlockSpec(shape, lambda i: (0,) * len(shape))


def shape_of(shape, dtype):
    return jax.ShapeDtypeStruct(shape, dtype)


def call(kernel, name, in_specs, out_specs, out_shape, flops, nbytes, grid=(), scratch=(), exps=0,
         limit=VMEM_BYTES, weight=1):
    return pl.pallas_call(
        kernel,
        grid=grid,
        in_specs=in_specs,
        out_specs=out_specs,
        out_shape=out_shape,
        scratch_shapes=list(scratch),
        compiler_params=pltpu.CompilerParams(vmem_limit_bytes=limit),
        cost_estimate=pl.CostEstimate(flops=int(weight), bytes_accessed=1, transcendentals=0),
        name=name,
    )


def node_half(tile, r):
    half = tile.shape[1] // 2
    return jnp.where(r == 0, tile[:, :half], tile[:, half:]).T


def entry_of(device_ref, slot_ref, b, slots):
    lon_count = lax.axis_size("lon")
    lat, lon = lax.axis_index("lat"), lax.axis_index("lon")
    target = device_ref[b]
    band = lax.div(target, lon_count)
    sector = target - band * lon_count - lon
    sector = jnp.where(sector < 0, sector + lon_count, sector)
    step = band - lat
    even_step = 1 - 2 * lax.rem(lat, 2)
    side = jnp.where(step == 0, 0, jnp.where(step == even_step, 1, 2))
    return (side * 2 + sector) * slots + slot_ref[b]


def write_packed(total, outs):
    per = total.shape[0] // 3
    for k, out in enumerate(outs):
        block = total[k * per : (k + 1) * per]
        out[...] = block.reshape(out.shape).astype(out.dtype)


def back_kernel(
    device_ref, slot_ref, tiles_ref, cot_ref, weight_ref, own_ref, east_ref, side_ref, held_ref,
    total, tiles, cots, tile_sems, cot_sems, weight_sem,
):
    blocks, rows = tiles.shape[0], tiles.shape[1]
    count = blocks // STEPS
    slots = total.shape[0] // 6
    channels = cots.shape[0]
    r = lax.axis_index("rep")
    copies = []
    for k in range(STEPS):
        part = pl.ds(k * count, count)
        cols = pl.ds(k * count * rows, count * rows)
        copies.append((
            pltpu.make_async_copy(tiles_ref.at[part], tiles.at[part], tile_sems.at[k]),
            pltpu.make_async_copy(cot_ref.at[:, cols], cots.at[:, cols], cot_sems.at[k]),
        ))
        for copy in copies[-1]:
            copy.start()
    weight_copy = pltpu.make_async_copy(weight_ref, held_ref, weight_sem)
    weight_copy.start()
    total[...] = jnp.zeros_like(total)
    for b in range(blocks):
        if b % count == 0:
            for copy in copies[b // count]:
                copy.wait()
        at = entry_of(device_ref, slot_ref, b, slots)
        cot = cots[:, b * rows : (b + 1) * rows]
        total[at, :, :channels] += dot_last(node_half(tiles[b], r), cot)
    for k, out in ((0, own_ref), (2, side_ref.at[0]), (4, side_ref.at[1])):
        out[...] = total[k * slots : (k + 1) * slots].reshape(out.shape).astype(out.dtype)
    for k in range(3):
        block = total[(2 * k + 1) * slots : (2 * k + 2) * slots]
        east_ref[k] = block.reshape(east_ref.shape[1:]).astype(east_ref.dtype)
    weight_copy.wait()


def encode_kernel(
    device_ref, slot_ref, after_ref, grid_ref, tiles_ref, weight_ref,
    own_ref, even_ref, odd_ref, hidden_ref, total, hold,
):
    blocks, rows = tiles_ref.shape[:2]
    slots = total.shape[0] // 6
    step_rows = blocks * rows // STEPS
    r = lax.axis_index("rep")
    total[...] = jnp.zeros_like(total)
    for k in range(STEPS):
        preact = dot_rows(grid_ref[:, k * step_rows : (k + 1) * step_rows], weight_ref[...])
        hold[k * step_rows : (k + 1) * step_rows, :] = (preact * sigmoid(preact)).astype(BF16)
        for b in range(k * blocks // STEPS, (k + 1) * blocks // STEPS):
            at = entry_of(device_ref, slot_ref, b, slots)
            total[at] += dot(node_half(tiles_ref[b], r), hold[b * rows : (b + 1) * rows, :])
    mine = hidden_ref.shape[0]
    hidden_ref[...] = hold[pl.ds(pl.multiple_of(r * mine, mine), mine), :]
    write_packed(total, (own_ref, even_ref, odd_ref))


def local_kernel(
    own_ref, oth_ref, cot_ref, out_ref, out_other_ref,
    base_ref, grad_ref, grad_other_ref,
):
    rows = own_ref.shape[0]
    r = lax.axis_index("rep")
    cot = cot_ref[:, pl.ds(pl.multiple_of(r * rows, rows), rows)]
    base_ref[...] = dot_last(out_ref[...], own_ref[...]) + dot_last(out_other_ref[...], oth_ref[...])
    grad_ref[...] = dot(cot, own_ref[...])
    grad_other_ref[...] = dot(cot, oth_ref[...])


def added(*values):
    total = values[0].astype(F32)
    for value in values[1:]:
        total = total + value.astype(F32)
    return total


def add_kernel(*refs):
    a, b, c, out = refs[-4:]
    out[...] = added(a[0], b[0], c[0]).astype(out.dtype)


def sides_kernel(after_ref, side_ref, moved_ref, even_ref, odd_ref):
    even_ref[...] = added(side_ref[0], moved_ref[1]).astype(even_ref.dtype)
    odd_ref[...] = added(side_ref[1], moved_ref[2]).astype(odd_ref.dtype)


def node_kernel(
    own_a, even_a, odd_a, moved_a, own_b, even_b, odd_b, moved_b, embed_ref, embed_other_ref,
    back_ref, back_moved_ref, back_even_ref, back_odd_ref, local_ref, local_other_ref,
    up_ref, up_other_ref, down_ref, down_other_ref, out_ref, out_other_ref,
    proj_ref, keep_ref, give_ref, mesh_give_ref, mesh_ref, mesh_half, mesh_sem,
):
    r = lax.axis_index("rep")
    nodes, width = moved_a.shape
    latent = 2 * width
    channels = out_ref.shape[0]
    first = pl.multiple_of(r * width, width)
    second = pl.multiple_of((1 - r) * width, width)
    states = []
    for embed, parts in (
        (embed_ref, (own_a[0], even_a[0], odd_a[0], moved_a[...])),
        (embed_other_ref, (own_b[0], even_b[0], odd_b[0], moved_b[...])),
    ):
        start = embed[:, r].reshape(nodes, width)
        states.append((start.astype(F32) + added(*parts)).astype(BF16).astype(F32))
    state = jnp.concatenate(states, axis=1)
    centered = state - jnp.mean(state, axis=-1, keepdims=True)
    inverse = lax.rsqrt(jnp.mean(centered * centered, axis=-1, keepdims=True) + 1e-05)
    norm = centered * inverse
    normed = norm.astype(BF16)

    cot = added(back_ref[...], back_moved_ref[0], back_even_ref[...], back_odd_ref[...]).astype(BF16)
    terms = cot[:, :channels]
    grad_own = dot(terms, out_ref[...]).astype(BF16)
    grad_oth = dot(terms, out_other_ref[...]).astype(BF16)

    update_own = jnp.zeros((nodes, width), F32)
    update_oth = jnp.zeros((nodes, width), F32)
    back_own = jnp.zeros((nodes, width), F32)
    back_oth = jnp.zeros((nodes, width), F32)
    sides = ((up_ref, down_ref, keep_ref), (up_other_ref, down_other_ref, give_ref))
    for u_ref, d_ref, o_ref in sides:
        up_own, up_oth = u_ref[pl.ds(first, width), :], u_ref[pl.ds(second, width), :]
        down_own, down_oth = d_ref[:, pl.ds(first, width)], d_ref[:, pl.ds(second, width)]
        hidden = dot(normed[:, :width], up_own) + dot(normed[:, width:], up_oth)
        squash = sigmoid(hidden)
        act = (hidden * squash).astype(BF16)
        update_own += dot(act, down_own)
        update_oth += dot(act, down_oth)
        o_ref[latent : latent + width, :] = dot_rows(act, cot).astype(o_ref.dtype)
        act_grad = dot_last(grad_own, down_own) + dot_last(grad_oth, down_oth)
        pre_grad = (act_grad * squash * (1.0 + hidden * (1.0 - squash))).astype(BF16)
        o_ref[pl.ds(first, width), :] = dot_rows(normed[:, :width], pre_grad).astype(o_ref.dtype)
        o_ref[pl.ds(second, width), :] = dot_rows(normed[:, width:], pre_grad).astype(o_ref.dtype)
        back_own += dot_last(pre_grad, up_own)
        back_oth += dot_last(pre_grad, up_oth)

    mesh_own = (states[0] + update_own).astype(BF16)
    mesh_oth = (states[1] + update_oth).astype(BF16)
    proj = dot_last(mesh_own, out_ref[...]) + dot_last(mesh_oth, out_other_ref[...])
    proj_ref[...] = jnp.zeros_like(proj_ref)
    proj_ref[:, :channels] = proj.astype(BF16)
    ends = ((keep_ref, mesh_own, local_ref), (give_ref, mesh_oth, local_other_ref))
    start = latent + width
    for o_ref, mesh, local in ends:
        grad = dot_rows(cot, mesh)
        o_ref[start : 2 * latent, :] = grad.astype(o_ref.dtype)
        o_ref[start : start + channels, :] = (grad[:channels] + local[...]).astype(o_ref.dtype)

    back = jnp.concatenate([back_own, back_oth], axis=1)
    slope = (
        back - jnp.mean(back, axis=-1, keepdims=True)
        - norm * jnp.mean(back * norm, axis=-1, keepdims=True)
    ) * inverse
    mesh_half[...] = (grad_own.astype(F32) + slope[:, :width]).reshape(mesh_half.shape)
    mesh_give_ref[...] = (grad_oth.astype(F32) + slope[:, width:]).astype(mesh_give_ref.dtype)
    copy = pltpu.make_async_copy(mesh_half, mesh_ref.at[:, r], mesh_sem)
    copy.start()
    copy.wait()


def place_kernel(got_ref, filled_ref, mesh_ref, mesh_half, mesh_sem):
    r = lax.axis_index("rep")
    mesh_half[...] = got_ref[...].astype(F32).reshape(mesh_half.shape)
    copy = pltpu.make_async_copy(mesh_half, mesh_ref.at[:, 1 - r], mesh_sem)
    copy.start()
    copy.wait()


def put_halves(value, step, keep_ref, give_ref, hold):
    rows = keep_ref.shape[0]
    bit = sum_bit(step)
    hold[...] = value
    keep_ref[...] = hold[pl.ds(pl.multiple_of(bit * rows, rows), rows), :].astype(keep_ref.dtype)
    give_ref[...] = hold[pl.ds(pl.multiple_of((1 - bit) * rows, rows), rows), :].astype(
        give_ref.dtype
    )


def terms_kernel(keep_ref, got_ref, *refs):
    outs, hold = refs[:4], refs[4]
    rows = hold.shape[0]
    for chain in range(2):
        part = slice(chain * rows, (chain + 1) * rows)
        put_halves(added(keep_ref[part, :], got_ref[part, :]), 0, *outs[2 * chain :][:2], hold)


def whole_kernel(kept_ref, got_ref, *refs):
    refs[-1][...] = added(kept_ref[...], got_ref[...]).astype(refs[-1].dtype)


def join_kernel(step, mine_ref, got_ref, *refs):
    out_ref = refs[-1]
    rows = mine_ref.shape[0]
    bit = sum_bit(step)
    out_ref[pl.ds(pl.multiple_of(bit * rows, rows), rows), :] = mine_ref[...].astype(out_ref.dtype)
    out_ref[pl.ds(pl.multiple_of((1 - bit) * rows, rows), rows), :] = got_ref[...].astype(
        out_ref.dtype
    )


def finish_outer_kernel(after_ref, mine_ref, other_ref, out_ref, out_other_ref, down_ref, grad_ref):
    r = lax.axis_index("rep")
    low = sum_bit(0) == 0
    width = mine_ref.shape[1]
    channels = out_ref.shape[0]
    mine, other = mine_ref[...], other_ref[...]
    terms = jnp.where(low, mine, other)[:, :channels]
    down_ref[:, pl.ds(pl.multiple_of(r * width, width), width)] = dot(terms, out_ref[...])
    down_ref[:, pl.ds(pl.multiple_of((1 - r) * width, width), width)] = dot(
        terms, out_other_ref[...]
    )
    grad_ref[...] = jnp.where(low, other, mine)[:channels].astype(F32)


def pack_kernel(after_ref, proj_ref, even_ref, odd_ref, out_ref):
    for k, part in enumerate((proj_ref, even_ref, odd_ref)):
        out_ref[k] = part[...]


def pick_kernel(device_ref, slot_ref, after_ref, own_ref, east_ref, mine_ref, theirs_ref):
    r = lax.axis_index("rep")
    blocks = mine_ref.shape[0]
    slots = own_ref.shape[0] // 3
    for out_ref, first in ((mine_ref, r * blocks), (theirs_ref, (1 - r) * blocks)):
        for i in range(blocks):
            at = entry_of(device_ref, slot_ref, first + i, slots)
            side = lax.div(at, 2 * slots)
            rest = at - side * 2 * slots

            @pl.when(rest < slots)
            def _(i=i, at=side * slots + rest, out_ref=out_ref):
                out_ref[i] = own_ref[at]

            @pl.when(rest >= slots)
            def _(i=i, at=side * slots + rest - slots, out_ref=out_ref):
                out_ref[i] = east_ref[at]


def decode_kernel(tiles_ref, base_ref, mine_ref, got_ref, out_ref, picked):
    r = lax.axis_index("rep")
    blocks, half = mine_ref.shape[:2]
    rows = tiles_ref.shape[1]
    channels = out_ref.shape[0]
    own = pl.ds(pl.multiple_of(r * half, half), half)
    other = pl.ds(pl.multiple_of((1 - r) * half, half), half)
    for i in range(blocks):
        picked[i, own, :] = mine_ref[i]
        picked[i, other, :] = got_ref[i]
    for i in range(blocks):
        cols = slice(i * rows, (i + 1) * rows)
        decoded = dot_last(picked[i].T, tiles_ref[r * blocks + i])
        out_ref[:, cols] = (base_ref[:, cols] + decoded[:channels]).astype(out_ref.dtype)


def along(axis, count, partner):
    pairs = []
    for source in range(count):
        to = partner(source)
        pairs.append((source, to if 0 <= to < count else source))
    return lambda value: lax.ppermute(value, axis, pairs)


def distances(axis):
    found, distance = [], 1
    while distance < lax.axis_size(axis):
        found.append((axis, distance))
        distance *= 2
    return found


def sum_orders():
    lat, lon = distances("lat"), distances("lon")
    return (lon + lat, lat + lon)


def sum_bit(step):
    bits = [
        lax.rem(lax.div(lax.axis_index(axis), distance), 2)
        for axis, distance in (order[step] for order in sum_orders())
    ]
    return jnp.where(lax.axis_index("rep") == 0, bits[0], bits[1])


def sum_swap(value, step):
    lat_count, lon_count = lax.axis_size("lat"), lax.axis_size("lon")
    orders = sum_orders()
    pairs = []
    for lat in range(lat_count):
        for lon in range(lon_count):
            for rep in range(2):
                axis, distance = orders[rep][step]
                to = (lat ^ distance, lon) if axis == "lat" else (lat, lon ^ distance)
                number = lambda a, b: (a * lon_count + b) * 2 + rep
                pairs.append((number(lat, lon), number(*to)))
    return lax.ppermute(value, ("lat", "lon", "rep"), pairs)


def per_device(
    grid_in, w_embed, interp_tiles, route_device, route_slot,
    mesh_embed, w_up, w_down, w_out, cotangent,
):
    lat_count, lon_count = lax.axis_size("lat"), lax.axis_size("lon")
    blocks, tile_rows = interp_tiles.shape[:2]
    grid_rows, channels = grid_in.shape
    my_rows = grid_rows // 2
    width = w_embed.shape[1]
    latent = 2 * width
    padded = -(-channels // 128) * 128
    slots = mesh_embed.shape[0] // tile_rows
    half = tile_rows // 2
    nodes = slots * half

    swap_rep = along("rep", 2, lambda i: 1 - i)
    to_even = along("lat", lat_count, lambda i: i ^ 1)
    to_odd = along("lat", lat_count, lambda i: ((i + 1) ^ 1) - 1)
    east_pairs = [(i, (i + 1) % lon_count) for i in range(lon_count)]
    west_pairs = [(j, i) for i, j in east_pairs]
    to_east = lambda value: lax.ppermute(value, "lon", east_pairs)

    in_hbm = lambda value: pltpu.with_memory_space_constraint(value, pltpu.HBM)
    device, slot = route_device.reshape(blocks), route_slot
    grid_t, cot_t, out_t = grid_in.T, cotangent.T, w_out.T
    routes = (in_hbm(device), in_hbm(slot))
    tiles_in, grid_in_t, cot_in_t = in_hbm(interp_tiles), in_hbm(grid_t), in_hbm(cot_t)
    pair_shape = (2, nodes, width)
    back_own, back_east, back_side, embed_own = call(
        back_kernel, "back_messages",
        [smem(), smem(), anywhere(), anywhere(), anywhere()],
        [vmem()] * 4,
        [shape_of((nodes, padded), BF16), shape_of((3, nodes, padded), BF16),
         shape_of((2, nodes, padded), BF16), shape_of((channels, width), BF16)],
        1, 1,
        scratch=[
            pltpu.VMEM((6 * slots, half, padded), F32),
            pltpu.VMEM(interp_tiles.shape, BF16),
            pltpu.VMEM(cot_t.shape, BF16),
            pltpu.SemaphoreType.DMA((STEPS,)),
            pltpu.SemaphoreType.DMA((STEPS,)),
            pltpu.SemaphoreType.DMA,
        ],
    )(*routes, tiles_in, cot_in_t, in_hbm(w_embed))
    back_moved = to_east(back_east)
    embed_other = swap_rep(embed_own)

    def encode(after, weight):
        return call(
            encode_kernel, "encode",
            [smem(), smem(), anywhere()] + [vmem()] * 3,
            [vmem()] * 4,
            [shape_of(pair_shape, BF16)] * 3 + [shape_of((my_rows, width), BF16)],
            1, 1,
            scratch=[
                pltpu.VMEM((6 * slots, half, width), F32), pltpu.VMEM((grid_rows, width), BF16),
            ],
        )(*routes, after, grid_t, interp_tiles, weight)

    own_a, even_a, odd_a, hidden_a = encode(back_own, embed_own)
    even_in_a, odd_in_a = to_even(even_a), to_odd(odd_a)
    own_b, even_b, odd_b, hidden_b = encode(own_a, embed_other)
    even_in_b, odd_in_b = to_even(even_b), to_odd(odd_b)

    out_other, up_other, down_other = swap_rep(out_t), swap_rep(w_up), swap_rep(w_down)
    embed_shape = (slots, 2, half, width)
    mesh_other = swap_rep(mesh_embed)

    second = pl.BlockSpec((1, nodes, width), lambda i: (1, 0, 0))

    def add_east(after, *terms):
        return call(
            add_kernel, "add_east", [anywhere()] * len(after) + [second] * 3, whole((nodes, width)),
            shape_of((nodes, width), BF16), 3 * nodes * width, 6e5, grid=(1,),
        )(*after, *terms)

    send_a = add_east((back_moved,), own_a, even_in_a, odd_in_a)
    moved_a = to_east(send_a)

    base, local, local_other = call(
        local_kernel, "local_terms", [vmem()] * 5, [vmem()] * 3,
        [shape_of((channels, my_rows), F32)] + [shape_of((channels, width), F32)] * 2,
        4 * my_rows * latent * channels, 4e6,
    )(hidden_a, hidden_b, cot_t, out_t, out_other)

    send_b = add_east((moved_a,), own_b, even_in_b, odd_in_b)
    moved_b = to_east(send_b)

    back_even, back_odd = call(
        sides_kernel, "add_sides", [anywhere(), vmem(), vmem()], [vmem()] * 2,
        [shape_of((nodes, padded), BF16)] * 2, 3 * nodes * width, 1e6,
    )(send_b, back_side, back_moved)
    back_even_in, back_odd_in = to_even(back_even), to_odd(back_odd)

    first = pl.BlockSpec((1, nodes, width), lambda i: (0, 0, 0))
    sums_specs = [first] * 3 + [whole((nodes, width))]
    weights = (w_up, up_other, w_down, down_other, out_t, out_other)
    back_spec = whole((nodes, padded))
    mesh_scratch = [pltpu.VMEM((slots, half, width), F32), pltpu.SemaphoreType.DMA]
    proj, keep, give, mesh_give, mesh_filled = call(
        node_kernel, "node_update_and_gradients",
        sums_specs * 2 + [whole(embed_shape)] * 2
        + [back_spec, pl.BlockSpec((1, nodes, padded), lambda i: (0, 0, 0)), back_spec, back_spec]
        + [whole((channels, width))] * 2 + [whole(w.shape) for w in weights],
        [whole((nodes, padded))] + [whole((2 * latent, width))] * 2
        + [whole((nodes, width)), anywhere()],
        [shape_of((nodes, padded), BF16), shape_of((2 * latent, width), F32),
         shape_of((2 * latent, width), BF16), shape_of((nodes, width), BF16),
         shape_of(embed_shape, F32)],
        15 * nodes * latent * latent, 9e6, grid=(1,), exps=nodes * latent, scratch=mesh_scratch,
    )(
        own_a, even_in_a, odd_in_a, moved_a, own_b, even_in_b, odd_in_b, moved_b,
        mesh_embed.reshape(embed_shape), mesh_other.reshape(embed_shape),
        back_own, back_moved, back_even_in, back_odd_in, local, local_other, *weights,
    )

    proj_even, proj_odd = to_even(proj), to_odd(proj)
    hold = lambda rows: [pltpu.VMEM((rows, width), F32)]
    up_keep, up_give, outer_keep, outer_give = call(
        terms_kernel, "sum_terms", [vmem()] * 2, [vmem()] * 4,
        [shape_of((width, width), BF16)] * 4, 1, 1, scratch=hold(latent), weight=5e9,
    )(keep, swap_rep(give))

    count = len(sum_orders()[0])
    chains = [[outer_keep, outer_give], [up_keep, up_give]]
    latest = None

    def step_call(chain, step, rows):
        kept, given = chain[0], chain[-1]
        after = [latest] if latest is not None else [proj_even, proj_odd]
        made = call(
            whole_kernel, "add_whole", [vmem()] * 2 + [anywhere()] * len(after), vmem(),
            shape_of((rows, width), BF16), 1, 1,
        )(kept, sum_swap(given, step), *after)
        return [made]

    for step in range(count):
        for c in range(2):
            rows = chains[c][0].shape[0]
            if step == 1 and c == 0:
                trio = call(
                    pack_kernel, "pack_nodes", [anywhere()] + [vmem()] * 3, vmem(),
                    shape_of((3, nodes, padded), BF16), 1, 1,
                )(latest, proj, proj_even, proj_odd)
                east_trio = lax.ppermute(trio, "lon", west_pairs)
            chains[c] = step_call(chains[c], step, rows)
            latest = chains[c][-1]
    after_pick = chains[1][-1]
    (outer_mine,), (up_mine,) = chains
    outer_theirs, up_theirs = sum_swap(outer_mine, 0), sum_swap(up_mine, 0)

    grad_mesh = pl.pallas_call(
        place_kernel,
        in_specs=[vmem(), anywhere()],
        out_specs=anywhere(),
        out_shape=shape_of(embed_shape, F32),
        scratch_shapes=mesh_scratch,
        input_output_aliases={1: 0},
        compiler_params=pltpu.CompilerParams(vmem_limit_bytes=VMEM_BYTES),
        cost_estimate=pl.CostEstimate(flops=1, bytes_accessed=1, transcendentals=0),
        name="place_mesh",
    )(swap_rep(mesh_give), mesh_filled).reshape(mesh_embed.shape)

    table_shape = (3 * slots, half, padded)
    mine_picked, theirs_picked = call(
        pick_kernel, "pick_nodes", [smem()] * 2 + [anywhere()] + [vmem()] * 2, [vmem()] * 2,
        [shape_of((blocks // 2, half, padded), BF16)] * 2, 1, 1,
    )(*routes, after_pick, trio.reshape(table_shape), east_trio.reshape(table_shape))
    grid_out_t = call(
        decode_kernel, "decode", [vmem()] * 4, vmem(),
        shape_of((channels, my_rows), BF16), 2 * my_rows * tile_rows * padded, 4e6,
        scratch=[pltpu.VMEM((blocks // 2, tile_rows, padded), BF16)],
    )(interp_tiles, base, mine_picked, swap_rep(theirs_picked))

    grad_down, grad_out = call(
        finish_outer_kernel, "finish_outer", [anywhere()] + [vmem()] * 4, [vmem()] * 2,
        [shape_of((width, latent), F32), shape_of((channels, width), F32)], 1, 1,
    )(in_hbm(grid_out_t), outer_mine, outer_theirs, out_t, out_other)
    grad_up = call(
        functools.partial(join_kernel, 0), "finish_up", [vmem()] * 2 + [anywhere()], vmem(),
        shape_of((latent, width), F32), 1, 1,
    )(up_mine, up_theirs, in_hbm(grid_out_t))
    return (grid_out_t.T, grad_out.T, grad_up, grad_down, grad_mesh)


def solution(mesh):
    patch = ("groups", "lat", "lon")
    placed = (
        P(patch, None),
        P(None, "rep"),
        P(patch, None, None),
        P(patch, None),
        P(patch),
        P(patch, "rep"),
        P(None, "rep"),
        P("rep", None),
        P("rep", None),
        P(patch, None),
    )
    return jax.shard_map(
        per_device,
        mesh=mesh,
        in_specs=placed,
        out_specs=(
            P(("groups", "lat", "lon", "rep"), None),
            P(("groups", "rep"), None),
            P("groups", "rep"),
            P(("groups", "rep"), None),
            P(patch, "rep"),
        ),
        check_vma=False,
    )
```
